512 devices in a mesh: stream: 32 (over x, y, core), cross: 16 (over z).
Axes of the slice: x: 4, y: 4, z: 16, core: 2. Of those that a mesh axis runs over, the one named last changes fastest.
Arguments:
- rhs: float32 [64, 5, 16384], P('stream', None, 'cross'), may hold values from -6 to 6
- diagonal: float32 [64, 16384], P('stream', 'cross'), may hold values from 1 to 10
- lower_transfer: float32 [64, 5, 5, 16384], P('stream', None, None, 'cross')
- upper_transfer: float32 [64, 5, 5, 16384], P('stream', None, None, 'cross')
- face_owner: int32 [16, 4], replicated, may hold values from 0 to 15, as said below
- face_start: int32 [16, 4], replicated, may hold values from 0 to 896, as said below
- face_count: int32 [16, 4], replicated, may hold values from 1 to 128, as said below
- face_flip: int32 [16, 4], replicated, may hold values from 0 to 1, as said below
- block_cells: int32 [16], replicated, may hold values from 512 to 1024
Outputs:
- solution: float32 [64, 5, 16384], P('stream', None, 'cross')
- residual: float32 [64, 5, 16384], P('stream', None, 'cross')
The draws below stay inside these ranges and needn't reach their ends.
Inputs may be any that keep to these rules, and one draw needn't show every extreme that they name: Links pair up: if face_owner[j, l] = n then face_owner[n, l] = j and n != j. `face_start`: link l's face lies within cells l * 256 to (l + 1) * 256 - 1 of its block. `face_count`: both sides of a link have the same count. `face_flip`: both sides of a link have the same flag.
All inputs are finite; a program needn't handle non-finite values.
Results may differ from the reference program's by a relative error of at most 0.00018.
Values sent between devices are 32-bit elements; how exact they have to be, the bound alone decides.
No kernel may reach another device: no remote copies, remote signals or barrier semaphores. Data moves between devices by JAX's collectives and lax.ppermute only.
A program may use at most 64 MiB of HBM per device.

```python
import math
import jax
import jax.numpy as jnp
from jax import lax

VARS = 5
CELLS = 1024
LINKS = 4
FACE = 128
ITERS = 2
STREAM_PLANES = 64
PLANE_CELL_TOTAL = 16384
N_CROSS = 16


def linking(key):
    region = CELLS // LINKS
    half = N_CROSS // 2
    owners = []
    starts = []
    counts = []
    flips = []
    for link in range(LINKS):
        sub = jax.random.fold_in(key, 100 + link)
        key_order, key_count, key_flip, key_start = jax.random.split(sub, 4)
        order = jax.random.permutation(key_order, N_CROSS).astype(jnp.int32).reshape(half, 2)
        first = order[:, 0]
        second = order[:, 1]
        blank = jnp.zeros((N_CROSS,), jnp.int32)
        owner = blank.at[first].set(second).at[second].set(first)
        pair_count = jax.random.randint(key_count, (half,), 1, FACE + 1).astype(jnp.int32).at[0].set(FACE)
        count = blank.at[first].set(pair_count).at[second].set(pair_count)
        pair_flip = jax.random.randint(key_flip, (half,), 0, 2).astype(jnp.int32)
        flip = blank.at[first].set(pair_flip).at[second].set(pair_flip)
        start = link * region + jax.random.randint(key_start, (N_CROSS,), 0, region - FACE + 1).astype(jnp.int32)
        if link == 0:
            start = start.at[0].set(0)
        if link == LINKS - 1:
            start = start.at[0].set(link * region + region - FACE)
        owners.append(owner)
        starts.append(start.astype(jnp.int32))
        counts.append(count)
        flips.append(flip)
    return (jnp.stack(owners, axis=1), jnp.stack(starts, axis=1), jnp.stack(counts, axis=1), jnp.stack(flips, axis=1))


def draw_face_owner(key, part):
    shared = linking(key)
    return shared[0]


def draw_face_start(key, part):
    shared = linking(key)
    return shared[1]


def draw_face_count(key, part):
    shared = linking(key)
    return shared[2]


def draw_face_flip(key, part):
    shared = linking(key)
    return shared[3]


def draw_block_cells(key, part):
    key = jax.random.fold_in(key, 5)
    key_live, key_where = jax.random.split(key)
    live = jax.random.randint(key_live, (N_CROSS,), CELLS // 2, CELLS + 1).astype(jnp.int32)
    widest = jax.random.randint(key_where, (), 0, N_CROSS).astype(jnp.int32)
    narrow = (widest + 1) % N_CROSS
    return live.at[widest].set(CELLS).at[narrow].set(CELLS // 2)


def transfer_draw(key, slow_share):
    random_keys = jax.random.split(key, 7)
    slow = jax.random.uniform(random_keys[0], (1, VARS, 1, PLANE_CELL_TOTAL)) < slow_share
    reach = jax.random.uniform(random_keys[1], (1, VARS, 1, PLANE_CELL_TOTAL), minval=0.1, maxval=2.0)
    memory = jax.random.uniform(random_keys[2], (1, VARS, 1, PLANE_CELL_TOTAL), minval=30.0, maxval=50.0)
    decay_rate = jnp.where(slow, jnp.exp(-reach / STREAM_PLANES), jnp.exp(-1.0 / memory))
    random_wobble = jax.random.uniform(random_keys[3], (STREAM_PLANES, VARS, 1, PLANE_CELL_TOTAL), minval=0.9, maxval=1.0)
    sudden_spike = jax.random.uniform(random_keys[4], (STREAM_PLANES, 1, 1, PLANE_CELL_TOTAL)) < 2.0 / STREAM_PLANES
    coupling_strength = jax.random.uniform(random_keys[5], (STREAM_PLANES, 1, 1, PLANE_CELL_TOTAL), minval=0.5, maxval=0.8)
    retained_faces = decay_rate * jnp.where(random_wobble > 0.0, jnp.sqrt(jnp.sqrt(random_wobble)) ** (1.0 / 4.0) * random_wobble ** 0.25, 1.0) * jnp.where(sudden_spike, coupling_strength, 1.0)
    coupling = jax.random.uniform(random_keys[6], (STREAM_PLANES, VARS, VARS, PLANE_CELL_TOTAL), minval=-0.25, maxval=0.25) * (1.0 - retained_faces)
    identity = jnp.eye(VARS, dtype=jnp.float32)[None, :, :, None]
    return jnp.where(identity > 0.0, retained_faces, coupling).astype(jnp.float32)


def draw_lower_transfer(key, part):
    key = jax.random.fold_in(key, 21)
    return transfer_draw(key, 0.5)


def draw_upper_transfer(key, part):
    key = jax.random.fold_in(key, 37)
    return transfer_draw(key, 0.5)


def steps_of(stream_key, dims, pieces, smallest, high):
    factor_of = 1.0
    for axis_at, parts in pieces:
        steps = jax.random.uniform(jax.random.fold_in(jax.random.fold_in(stream_key, 6), axis_at), (parts,), jnp.float32, smallest / len(pieces), high / len(pieces))
        factor_of = factor_of * jnp.repeat(jnp.exp(steps), dims[axis_at] // parts).reshape((-1,) + (1,) * (len(dims) - 1 - axis_at))
    return factor_of


def gaussian(stream_key, extent, width, most, cuts=(), kind=jnp.bfloat16):
    values = jax.random.normal(stream_key, extent, jnp.float32) * width
    if len(cuts) > 0:
        values = steps_of(stream_key, extent, cuts, -0.22, 0.18) * values
    return jnp.clip(values, min=-most, max=most).astype(kind)


def setup_inputs(seed: int = 0) -> dict:
    splits = jax.random.split(jax.random.key(seed), 10)
    rhs = gaussian(splits[0], (STREAM_PLANES, VARS, PLANE_CELL_TOTAL), 1.0, 6.0, ((0, 32), (2, 16)), jnp.float32)
    diagonal = jnp.clip(jnp.exp(math.log(10.0) - 2.3025851 * jax.random.uniform(splits[1], (STREAM_PLANES, PLANE_CELL_TOTAL), jnp.float32) ** steps_of(splits[1], (STREAM_PLANES, PLANE_CELL_TOTAL), ((0, 32), (1, 16)), -0.2, 0.2)), 1.0, 10.0)
    lower_transfer = draw_lower_transfer(jax.random.fold_in(splits[9], 71), 0)
    upper_transfer = draw_upper_transfer(jax.random.fold_in(splits[9], 71), 0)
    face_owner = draw_face_owner(jax.random.fold_in(splits[9], 71), 0)
    face_start = draw_face_start(jax.random.fold_in(splits[9], 71), 0)
    face_count = draw_face_count(jax.random.fold_in(splits[9], 71), 0)
    face_flip = draw_face_flip(jax.random.fold_in(splits[9], 71), 0)
    block_cells = draw_block_cells(jax.random.fold_in(splits[9], 71), 0)
    return dict(rhs=rhs, diagonal=diagonal, lower_transfer=lower_transfer, upper_transfer=upper_transfer, face_owner=face_owner, face_start=face_start, face_count=face_count, face_flip=face_flip, block_cells=block_cells)


FACE_WEIGHT = 0.25


def sweep(source, transfer, reverse):
    def advance(state, inputs):
        values, matrix = inputs
        state = values + jnp.sum(matrix * state[None, :, :], axis=1)
        return state, state
    start_state = jnp.zeros(source.shape[1:], jnp.float32)
    _, result = lax.scan(advance, start_state, (source, transfer), reverse=reverse)
    return result


def operate(field, diagonal, lower_transfer, upper_transfer, face_owner, face_start, face_count, face_flip):
    blank = jnp.zeros((1,) + field.shape[1:], jnp.float32)
    before = jnp.concatenate([blank, field[:-1]], axis=0)
    after = jnp.concatenate([field[1:], blank], axis=0)
    along = jnp.sum(lower_transfer * before[:, None], axis=2) + jnp.sum(upper_transfer * after[:, None], axis=2)
    positions = jnp.arange(FACE, dtype=jnp.int32)
    zero_index = jnp.zeros((), jnp.int32)
    faces = jnp.zeros_like(field)
    for block in range(N_CROSS):
        for link in range(LINKS):
            other = face_owner[block, link]
            count = face_count[block, link]
            source_cell = (other * CELLS + face_start[other, link]).astype(jnp.int32)
            tile_set = lax.dynamic_slice(field, (zero_index, zero_index, source_cell), (field.shape[0], VARS, FACE))
            picked = jnp.where(face_flip[block, link] == 1, count - 1 - positions, positions)
            picked = jnp.clip(picked, 0, FACE - 1).astype(jnp.int32)
            tile_set = jnp.take(tile_set, picked, axis=2)
            tile_set = tile_set * (positions < count).astype(jnp.float32)[None, None, :]
            target_cell = (block * CELLS + face_start[block, link]).astype(jnp.int32)
            current = lax.dynamic_slice(faces, (zero_index, zero_index, target_cell), (field.shape[0], VARS, FACE))
            faces = lax.dynamic_update_slice(faces, current + tile_set, (zero_index, zero_index, target_cell))
    return diagonal[:, None, :] * (field - along - FACE_WEIGHT * faces)


def reference(rhs, diagonal, lower_transfer, upper_transfer, face_owner, face_start, face_count, face_flip, block_cells):
    cell_index = jnp.arange(PLANE_CELL_TOTAL, dtype=jnp.int32)
    live_count = block_cells[cell_index // CELLS]
    live_mask = ((cell_index % CELLS) < live_count).astype(jnp.float32)
    live_source = rhs * live_mask[None, None, :]
    solution = jnp.zeros_like(rhs)
    residual = live_source
    for iteration in range(ITERS):
        lowered = sweep(residual / diagonal[:, None, :], lower_transfer, False)
        delta = sweep(lowered, upper_transfer, True)
        solution = solution + delta
        residual = live_source - operate(solution, diagonal, lower_transfer, upper_transfer, face_owner, face_start, face_count, face_flip)
    return solution, residual
```

```python
import functools

import jax
import jax.numpy as jnp
from jax import lax
from jax.experimental import pallas as pl
from jax.experimental.pallas import tpu as pltpu
from jax.sharding import PartitionSpec as P

VARS = 5
CELLS = 1024
LINKS = 4
WINDOW = CELLS // LINKS
STREAM = 32
CROSS = 16
PLANES = 2
CHUNKS = 8
GROUPS = 4
LANES = 128
FACE_WEIGHT = 0.25

LOWER = 0
UPPER = 25
SOURCE = 50
ROWS = 110

F32 = jnp.float32
BF16 = jnp.bfloat16
SMEM = pl.BlockSpec(memory_space=pltpu.SMEM)
VMEM = pl.BlockSpec(memory_space=pltpu.VMEM)
PARAMS = pltpu.CompilerParams(vmem_limit_bytes=24 * 1024 * 1024)


def cost(flops, moved):
    return pl.CostEstimate(flops=flops, bytes_accessed=moved, transcendentals=0)


def thirds(x):
    high = x.astype(BF16)
    rest = x - high.astype(F32)
    middle = rest.astype(BF16)
    low = (rest - middle.astype(F32)).astype(BF16)
    return high, middle, low


def slot_map(own, link, owner_ref, start_ref, count_ref, flip_ref):
    owner = owner_ref[link, own]
    count = count_ref[link, own]
    turned = jnp.logical_and(flip_ref[link, own] == 1, own > owner)
    bound = jnp.where(turned, count, 0)
    offset = start_ref[link, own] - link * WINDOW
    cell = lax.broadcasted_iota(jnp.int32, (1, WINDOW), 1)
    place = (cell - offset) & (WINDOW - 1)
    place = jnp.where(place < bound, count - 1 - place, place)
    rest = place & 127
    slot = ((rest >> 4) << 5) + (rest & 15) + ((place >> 7) << 4)
    rows = lax.broadcasted_iota(jnp.int32, (WINDOW, WINDOW), 0)
    return jnp.where(rows == slot, 1.0, 0.0).astype(BF16)


def pack_kernel(
    owner_ref, start_ref, count_ref, flip_ref, live_ref,
    rhs_ref, diagonal_ref, lower_ref, upper_ref, out_ref, rows_ref,
):
    own = lax.axis_index("cross")
    cell = lax.broadcasted_iota(jnp.int32, (PLANES, CELLS), 1)
    live = cell < live_ref[own]
    for a in range(VARS):
        for b in range(VARS):
            at = VARS * a + b
            rows_ref[pl.ds(2 * (LOWER + at), 2), :] = lower_ref[a, b]
            rows_ref[pl.ds(2 * (UPPER + at), 2), :] = upper_ref[a, b]
        source = jnp.where(live, rhs_ref[a], 0.0) / diagonal_ref[...]
        rows_ref[pl.ds(2 * (SOURCE + a), 2), :] = source
    rows_ref[pl.ds(ROWS, LANES - ROWS), :] = jnp.zeros((LANES - ROWS, CELLS), F32)
    for link in range(LINKS):
        onehot = slot_map(own, link, owner_ref, start_ref, count_ref, flip_ref)
        parts = thirds(rows_ref[:, link * WINDOW:(link + 1) * WINDOW])
        high, middle, low = [
            lax.dot_general(onehot, part, (((1,), (1,)), ((), ())), preferred_element_type=F32)
            for part in parts
        ]
        out_ref[link * WINDOW:(link + 1) * WINDOW, :] = (low + middle) + high


def entry(system_ref, k, p, at):
    row = 2 * at + p
    return system_ref[k, row:row + 1, :]


def product(system_ref, k, p, at, state):
    out = []
    for a in range(VARS):
        terms = [
            entry(system_ref, k, p, at + VARS * a + b) * state[b] for b in range(VARS)
        ]
        out.append((terms[0] + terms[1]) + (terms[2] + terms[3]) + terms[4])
    return out


def get_rows(ref, k, p):
    return [ref[k, 8 * p + a:8 * p + a + 1, :] for a in range(VARS)]


def put_rows(ref, k, p, rows):
    for a in range(VARS):
        ref[k, 8 * p + a:8 * p + a + 1, :] = rows[a]


def turn(state, by):
    return tuple(pltpu.roll(x, by, 1) for x in state)


def lower_sweep(step):
    state = tuple(jnp.zeros((1, LANES), F32) for _ in range(VARS))
    for group in range(GROUPS):
        if group:
            state = turn(state, 32)
        state = lax.fori_loop(0, CHUNKS, functools.partial(step, group), state, unroll=True)


def upper_sweep(step):
    state = tuple(jnp.zeros((1, LANES), F32) for _ in range(VARS))
    for group in reversed(range(GROUPS)):
        if group < GROUPS - 1:
            state = turn(state, 96)
        state = lax.fori_loop(
            0, CHUNKS, lambda i, x: step(group, CHUNKS - 1 - i, x), state, unroll=True
        )


def merged(ref):
    shape = (CHUNKS * 16, LANES)
    lane = lax.broadcasted_iota(jnp.int32, shape, 1) >> 5
    row = lax.broadcasted_iota(jnp.int32, shape, 0) & 7
    parts = [ref[group].reshape(shape) for group in range(GROUPS)]
    out = jnp.where(lane == 0, parts[0], jnp.where(lane == 1, parts[1], jnp.where(lane == 2, parts[2], parts[3])))
    return jnp.where(row < VARS, out, 0.0)


def publish(field, send_ref):
    turned = field.T
    for group in range(GROUPS):
        send_ref[pl.ds(group, 16, stride=GROUPS), :] = turned[32 * group:32 * group + 16]


def receive(face_ref):
    parts = []
    for group in range(GROUPS):
        parts.append(face_ref[pl.ds(group, 16, stride=GROUPS), :])
        parts.append(jnp.zeros((16, LANES), F32))
    return FACE_WEIGHT * jnp.concatenate(parts, axis=0).T


def upper_pass(system_ref, lowered_ref, coupled_ref, delta_ref):
    def upper(group, k, state):
        for p in reversed(range(PLANES)):
            coupled = product(system_ref, k, p, UPPER, state)
            put_rows(coupled_ref.at[group], k, p, coupled)
            lowered = get_rows(lowered_ref.at[group], k, p)
            state = tuple(w + e for w, e in zip(lowered, coupled))
            put_rows(delta_ref.at[group], k, p, state)
        return state

    upper_sweep(upper)


def first_kernel(in_ref, system_ref, coupled_out, delta_out, send_ref, lowered_ref, coupled_ref, delta_ref):
    for k in range(CHUNKS):
        block = jnp.concatenate([in_ref[CHUNKS * g + k] for g in range(GROUPS)], axis=0)
        system_ref[k] = block.T

    def lower(group, k, state):
        for p in range(PLANES):
            along = product(system_ref, k, p, LOWER, state)
            state = tuple(entry(system_ref, k, p, SOURCE + a) + along[a] for a in range(VARS))
            put_rows(lowered_ref.at[group], k, p, state)
        return state

    lower_sweep(lower)
    upper_pass(system_ref, lowered_ref, coupled_ref, delta_ref)
    coupled_out[...] = merged(coupled_ref).reshape(coupled_out.shape)
    delta = merged(delta_ref)
    delta_out[...] = delta
    publish(delta, send_ref)


def swap_kernel(owner_ref, count_ref, in_ref, out_ref):
    position = lax.axis_index("stream")
    link = position >> 3
    slot = ((position & 7) << 4) + lax.axis_index("cross")
    for block in range(CROSS):
        tile = in_ref[owner_ref[link, block]]
        keep = jnp.full(tile.shape, count_ref[link, block], jnp.int32) > slot
        out_ref[block] = jnp.where(keep, tile, 0.0)


def second_kernel(
    system_ref, coupled_in, delta_in, face_ref,
    solution_ref, along_ref, send_ref,
    faces_ref, lowered_ref, coupled_ref, delta_ref, last_ref,
):
    faces_ref[...] = receive(face_ref).reshape(faces_ref.shape)

    def lower(group, k, state):
        for p in range(PLANES):
            along = product(system_ref, k, p, LOWER, state)
            faces = get_rows(faces_ref, k, p)
            lowered = [f + x for f, x in zip(faces, along)]
            put_rows(lowered_ref.at[group], k, p, lowered)
            before = get_rows(coupled_in, k, p)
            state = tuple(w + e for w, e in zip(lowered, before))
        return state

    lower_sweep(lower)
    upper_pass(system_ref, lowered_ref, coupled_ref, delta_ref)
    delta = merged(delta_ref)
    publish(delta, send_ref)
    solution_ref[...] = delta_in[...] + delta
    last_ref[...] = merged(coupled_ref).reshape(last_ref.shape)
    lane = lax.broadcasted_iota(jnp.int32, (1, LANES), 1)
    for k in range(CHUNKS):
        if k:
            before = get_rows(last_ref, k - 1, 1)
        else:
            before = [
                jnp.where(lane < 32, 0.0, x) for x in turn(get_rows(last_ref, CHUNKS - 1, 1), 32)
            ]
        put_rows(along_ref, k, 0, product(system_ref, k, 0, LOWER, before))
        before = get_rows(last_ref, k, 0)
        put_rows(along_ref, k, 1, product(system_ref, k, 1, LOWER, before))


def regroup(parts):
    lane = lax.broadcasted_iota(jnp.int32, parts[0].shape, 1)
    first_half = lane < 64
    even = (lane & 32) == 0
    half = [None] * 4
    for i in range(2):
        x, y = parts[i], parts[i + 2]
        half[i] = jnp.where(first_half, x, pltpu.roll(y, 64, 1))
        half[i + 2] = jnp.where(first_half, pltpu.roll(x, 64, 1), y)
    out = [None] * 4
    for i in (0, 2):
        x, y = half[i], half[i + 1]
        out[i] = jnp.where(even, x, pltpu.roll(y, 32, 1))
        out[i + 1] = jnp.where(even, pltpu.roll(x, 96, 1), y)
    return out


def last_kernel(solution_ref, along_ref, face_ref, out_ref, residual_ref):
    residual_ref[...] = along_ref[...] + receive(face_ref).reshape(residual_ref.shape)
    for k in range(CHUNKS):
        tiles = [solution_ref[16 * k + 8 * p:16 * k + 8 * p + 8, :] for p in range(PLANES)]
        tiles += [residual_ref[k, 8 * p:8 * p + 8, :] for p in range(PLANES)]
        for group, tile in enumerate(regroup(tiles)):
            out_ref[CHUNKS * group + k] = tile


def unpack_kernel(
    owner_ref, start_ref, count_ref, flip_ref, diagonal_ref, in_ref, solution_ref, residual_ref, rows_ref
):
    own = lax.axis_index("cross")
    for column in range(8):
        tiles = regroup([in_ref[4 * column + e] for e in range(4)])
        for g, tile in enumerate(tiles):
            rows_ref[8 * g:8 * g + 8, LANES * column:LANES * (column + 1)] = tile
    for link in range(LINKS):
        window = slice(link * WINDOW, (link + 1) * WINDOW)
        onehot = slot_map(own, link, owner_ref, start_ref, count_ref, flip_ref)
        high, middle, low = [
            jnp.dot(part, onehot, preferred_element_type=F32) for part in thirds(rows_ref[:, window])
        ]
        cells = (low + middle) + high
        for p in range(PLANES):
            residual = cells[16 + 8 * p:16 + 8 * p + VARS] * diagonal_ref[p:p + 1, window]
            for a in range(VARS):
                solution_ref[a, p:p + 1, window] = cells[8 * p + a:8 * p + a + 1]
                residual_ref[a, p:p + 1, window] = residual[a:a + 1]


def shape(*dims):
    return jax.ShapeDtypeStruct(dims, F32)


def exchange(send, face_owner, face_count):
    arrived = lax.all_to_all(send.reshape(CROSS, GROUPS, LANES), "cross", 0, 0, tiled=True)
    swapped = pl.pallas_call(
        swap_kernel,
        out_shape=shape(CROSS, GROUPS, LANES),
        in_specs=[SMEM, SMEM, VMEM],
        out_specs=VMEM,
        name="swap_faces",
    )(face_owner, face_count, arrived)
    back = lax.all_to_all(swapped, "cross", 0, 0, tiled=True)
    return back.reshape(CROSS * GROUPS, LANES)


def local(
    rhs,
    diagonal,
    lower_transfer,
    upper_transfer,
    face_owner,
    face_start,
    face_count,
    face_flip,
    block_cells,
):
    face_owner, face_count = face_owner.T, face_count.T
    links = (face_owner, face_start.T, face_count, face_flip.T)
    packed = pl.pallas_call(
        pack_kernel,
        out_shape=shape(CELLS, LANES),
        in_specs=[SMEM] * 5 + [VMEM] * 4,
        out_specs=VMEM,
        scratch_shapes=[pltpu.VMEM((LANES, CELLS), F32)],
        compiler_params=PARAMS,
        name="pack_cells",
    )(
        *links,
        block_cells,
        rhs.transpose(1, 0, 2),
        diagonal,
        lower_transfer.transpose(1, 2, 0, 3),
        upper_transfer.transpose(1, 2, 0, 3),
    )
    arrived = lax.all_to_all(packed.reshape(STREAM, 32, LANES), "stream", 0, 0, tiled=True)

    passes = pltpu.VMEM((GROUPS, CHUNKS, 16, LANES), F32)
    system, coupled, delta, send = pl.pallas_call(
        first_kernel,
        out_shape=[
            shape(CHUNKS, LANES, LANES), shape(CHUNKS, 16, LANES), shape(LANES, LANES), shape(64, LANES)
        ],
        in_specs=[VMEM],
        out_specs=[VMEM] * 4,
        scratch_shapes=[passes] * 3,
        compiler_params=PARAMS,
        name="first_sweeps",
    )(arrived)
    faces = exchange(send, face_owner, face_count)
    total, along, send = pl.pallas_call(
        second_kernel,
        out_shape=[shape(LANES, LANES), shape(CHUNKS, 16, LANES), shape(64, LANES)],
        in_specs=[VMEM] * 4,
        out_specs=[VMEM] * 3,
        scratch_shapes=[pltpu.VMEM((CHUNKS, 16, LANES), F32)] + [passes] * 3
        + [pltpu.VMEM((CHUNKS, 16, LANES), F32)],
        compiler_params=PARAMS,
        name="second_sweeps",
    )(system, coupled, delta, faces)
    faces = exchange(send, face_owner, face_count)
    results = pl.pallas_call(
        last_kernel,
        out_shape=shape(STREAM, 8, LANES),
        in_specs=[VMEM] * 3,
        out_specs=VMEM,
        scratch_shapes=[pltpu.VMEM((CHUNKS, 16, LANES), F32)],
        compiler_params=PARAMS,
        name="pack_results",
    )(total, along, faces)
    returned = lax.all_to_all(results, "stream", 0, 0, tiled=True)
    results = pl.pallas_call(
        unpack_kernel,
        out_shape=[shape(VARS, PLANES, CELLS)] * 2,
        in_specs=[SMEM] * 4 + [VMEM] * 2,
        out_specs=[VMEM] * 2,
        scratch_shapes=[pltpu.VMEM((32, CELLS), F32)],
        compiler_params=PARAMS,
        name="unpack_cells",
    )(*links, diagonal, returned)
    return tuple(x.transpose(1, 0, 2) for x in results)


def solution(mesh):
    return jax.shard_map(
        local,
        mesh=mesh,
        in_specs=(
            P("stream", None, "cross"),
            P("stream", "cross"),
            P("stream", None, None, "cross"),
            P("stream", None, None, "cross"),
            P(),
            P(),
            P(),
            P(),
            P(),
        ),
        out_specs=(P("stream", None, "cross"), P("stream", None, "cross")),
        check_vma=False,
    )
```

```python
import functools

import jax
import jax.numpy as jnp
from jax import lax
from jax.experimental import pallas as pl
from jax.experimental.pallas import tpu as pltpu
from jax.sharding import PartitionSpec as P

VARS = 5
CELLS = 1024
LINKS = 4
WINDOW = CELLS // LINKS
STREAM = 32
CROSS = 16
PLANES = 2
CHUNKS = 8
GROUPS = 4
LANES = 128
FACE_WEIGHT = 0.25

LOWER = 0
UPPER = 25
SOURCE = 50
ROWS = 110

F32 = jnp.float32
BF16 = jnp.bfloat16
HBM = pl.BlockSpec(memory_space=pltpu.HBM)
SMEM = pl.BlockSpec(memory_space=pltpu.SMEM)
VMEM = pl.BlockSpec(memory_space=pltpu.VMEM)
PARAMS = pltpu.CompilerParams(vmem_limit_bytes=24 * 1024 * 1024)
WIDE = pltpu.CompilerParams(vmem_limit_bytes=62 * 1024 * 1024)
TABLE = pltpu.SMEM((LINKS, CROSS), jnp.int32)
BOTH = ("stream", "cross")


def thirds(x):
    high = x.astype(BF16)
    rest = x - high.astype(F32)
    middle = rest.astype(BF16)
    low = (rest - middle.astype(F32)).astype(BF16)
    return high, middle, low


def copy_in(pairs, sems):
    copies = [pltpu.make_async_copy(src, dst, sems.at[i]) for i, (src, dst) in enumerate(pairs)]
    for copy in copies:
        copy.start()
    return copies


def places(own, link, owner_ref, start_ref, count_ref, flip_ref):
    owner = owner_ref[link, own]
    count = count_ref[link, own]
    turned = jnp.logical_and(flip_ref[link, own] == 1, own > owner)
    bound = jnp.where(turned, count, 0)
    offset = start_ref[link, own] - link * WINDOW
    cell = lax.broadcasted_iota(jnp.int32, (1, WINDOW), 1)
    place = (cell - offset) & (WINDOW - 1)
    return jnp.where(place < bound, count - 1 - place, place)


def onehot(row):
    rows = lax.broadcasted_iota(jnp.int32, (WINDOW, WINDOW), 0)
    return jnp.where(rows == row, 1.0, 0.0).astype(BF16)


def pack_kernel(
    owner_in, start_in, count_in, flip_in, live_in, rhs_in, diagonal_in, lower_in, upper_in,
    out_ref,
    owner_ref, start_ref, count_ref, flip_ref, live_ref, rhs_ref, diagonal_ref, lower_ref, upper_ref,
    rows_ref, sems,
):
    copies = copy_in(
        [
            (lower_in, lower_ref), (upper_in, upper_ref), (rhs_in, rhs_ref),
            (diagonal_in, diagonal_ref), (live_in, live_ref), (owner_in, owner_ref),
            (start_in, start_ref), (count_in, count_ref), (flip_in, flip_ref),
        ],
        sems,
    )
    own = lax.axis_index("cross")
    rows_ref[pl.ds(ROWS, LANES - ROWS), :] = jnp.zeros((LANES - ROWS, CELLS), F32)
    for copy in copies:
        copy.wait()
    cell = lax.broadcasted_iota(jnp.int32, (PLANES, CELLS), 1)
    live = cell < live_ref[own]
    for a in range(VARS):
        for b in range(VARS):
            at = VARS * a + b
            rows_ref[pl.ds(2 * (LOWER + at), 2), :] = lower_ref[a, b]
            rows_ref[pl.ds(2 * (UPPER + at), 2), :] = upper_ref[a, b]
        source = jnp.where(live, rhs_ref[a], 0.0) / diagonal_ref[...]
        rows_ref[pl.ds(2 * (SOURCE + a), 2), :] = source
    for link in range(LINKS):
        place = places(own, link, owner_ref, start_ref, count_ref, flip_ref)
        rest = place & 127
        matrix = onehot(2 * rest + (place >> 7))
        high, middle, low = [
            lax.dot_general(matrix, part, (((1,), (1,)), ((), ())), preferred_element_type=F32)
            for part in thirds(rows_ref[:, link * WINDOW:(link + 1) * WINDOW])
        ]
        out_ref[link * WINDOW:(link + 1) * WINDOW, :] = (low + middle) + high


def entry(system_ref, k, p, at):
    row = 2 * at + p
    return system_ref[k, row:row + 1, :]


def product(system_ref, k, p, at, state):
    out = []
    for a in range(VARS):
        terms = [
            entry(system_ref, k, p, at + VARS * a + b) * state[b] for b in range(VARS)
        ]
        out.append((terms[0] + terms[1]) + (terms[2] + terms[3]) + terms[4])
    return out


def get_rows(ref, k, p):
    return [ref[k, 8 * p + a:8 * p + a + 1, :] for a in range(VARS)]


def put_rows(ref, k, p, rows):
    for a in range(VARS):
        ref[k, 8 * p + a:8 * p + a + 1, :] = rows[a]


def turn(state, by):
    return tuple(pltpu.roll(x, by, 1) for x in state)


def lower_sweep(step):
    state = tuple(jnp.zeros((1, LANES), F32) for _ in range(VARS))
    for group in range(GROUPS):
        if group:
            state = turn(state, 32)
        state = lax.fori_loop(0, CHUNKS, functools.partial(step, group), state, unroll=True)


def upper_sweep(step):
    state = tuple(jnp.zeros((1, LANES), F32) for _ in range(VARS))
    for group in reversed(range(GROUPS)):
        if group < GROUPS - 1:
            state = turn(state, 96)
        state = lax.fori_loop(
            0, CHUNKS, lambda i, x: step(group, CHUNKS - 1 - i, x), state, unroll=True
        )


def merged(ref):
    shape = (CHUNKS * 16, LANES)
    lane = lax.broadcasted_iota(jnp.int32, shape, 1) >> 5
    row = lax.broadcasted_iota(jnp.int32, shape, 0) & 7
    parts = [ref[group].reshape(shape) for group in range(GROUPS)]
    out = jnp.where(lane == 0, parts[0], jnp.where(lane == 1, parts[1], jnp.where(lane == 2, parts[2], parts[3])))
    return jnp.where(row < VARS, out, 0.0)


def upper_pass(system_ref, lowered_ref, coupled_ref, delta_ref):
    def upper(group, k, state):
        for p in reversed(range(PLANES)):
            coupled = product(system_ref, k, p, UPPER, state)
            put_rows(coupled_ref.at[group], k, p, coupled)
            lowered = get_rows(lowered_ref.at[group], k, p)
            state = tuple(w + e for w, e in zip(lowered, coupled))
            put_rows(delta_ref.at[group], k, p, state)
        return state

    upper_sweep(upper)


def face_matrix(owner_ref, count_ref):
    position = lax.axis_index("stream")
    link = position >> 3
    slot = ((position & 7) << 4) + lax.axis_index("cross")
    lane = lax.broadcasted_iota(jnp.int32, (1, LANES), 1)
    source = jnp.full((1, LANES), -1, jnp.int32)
    for block in range(CROSS):
        taken = jnp.where(slot < count_ref[link, block], owner_ref[link, block], -LANES)
        source = jnp.where((lane & 31) == block, (lane & 96) + taken, source)
    rows = lax.broadcasted_iota(jnp.int32, (LANES, LANES), 0)
    return jnp.where(rows == source, FACE_WEIGHT, 0.0).astype(BF16)


def faces_of(field, matrix):
    high, middle, low = [jnp.dot(part, matrix, preferred_element_type=F32) for part in thirds(field)]
    return (low + middle) + high


def solve_kernel(
    owner_in, count_in, in_ref, out_ref,
    owner_ref, count_ref, system_ref, faces_ref, last_ref, solution_ref, residual_ref,
    lowered_ref, coupled_ref, delta_ref, sems,
):
    copies = copy_in([(owner_in, owner_ref), (count_in, count_ref)], sems)
    for k in range(CHUNKS):
        parts = []
        for group in range(GROUPS):
            first = (CHUNKS * group + k) * 32
            parts += [in_ref[pl.ds(first + half, CROSS, stride=2), :] for half in range(2)]
        system_ref[k] = jnp.concatenate(parts, axis=0).T
    for copy in copies:
        copy.wait()
    matrix = face_matrix(owner_ref, count_ref)

    def lower_first(group, k, state):
        for p in range(PLANES):
            along = product(system_ref, k, p, LOWER, state)
            state = tuple(entry(system_ref, k, p, SOURCE + a) + along[a] for a in range(VARS))
            put_rows(lowered_ref.at[group], k, p, state)
        return state

    lower_sweep(lower_first)
    upper_pass(system_ref, lowered_ref, coupled_ref, delta_ref)
    last_ref[...] = merged(coupled_ref).reshape(last_ref.shape)
    first = merged(delta_ref)
    faces_ref[...] = faces_of(first, matrix).reshape(faces_ref.shape)

    def lower_second(group, k, state):
        for p in range(PLANES):
            along = product(system_ref, k, p, LOWER, state)
            lowered = [f + x for f, x in zip(get_rows(faces_ref, k, p), along)]
            put_rows(lowered_ref.at[group], k, p, lowered)
            state = tuple(w + e for w, e in zip(lowered, get_rows(last_ref, k, p)))
        return state

    lower_sweep(lower_second)
    upper_pass(system_ref, lowered_ref, coupled_ref, delta_ref)
    second = merged(delta_ref)
    solution_ref[...] = (first + second).reshape(solution_ref.shape)
    last_ref[...] = merged(coupled_ref).reshape(last_ref.shape)
    lane = lax.broadcasted_iota(jnp.int32, (1, LANES), 1)
    for k in range(CHUNKS):
        if k:
            before = get_rows(last_ref, k - 1, 1)
        else:
            before = [
                jnp.where(lane < 32, 0.0, x) for x in turn(get_rows(last_ref, CHUNKS - 1, 1), 32)
            ]
        put_rows(residual_ref, k, 0, product(system_ref, k, 0, LOWER, before))
        before = get_rows(last_ref, k, 0)
        put_rows(residual_ref, k, 1, product(system_ref, k, 1, LOWER, before))
    residual_ref[...] = residual_ref[...] + faces_of(second, matrix).reshape(residual_ref.shape)

    lane = lax.broadcasted_iota(jnp.int32, (CROSS, LANES), 1) >> 5
    for half in range(2):
        parts = []
        for k in range(4 * half, 4 * half + 4):
            parts += [solution_ref[k], residual_ref[k]]
        turned = jnp.concatenate(parts, axis=0).T
        for group in range(GROUPS):
            face = turned[32 * group:32 * group + 16]
            other = pltpu.roll(turned[32 * group + 16:32 * group + 32], 64, 1)
            for k in range(4):
                first = (CHUNKS * group + 4 * half + k) * CROSS
                out_ref[first:first + CROSS, :] = jnp.where(lane == k, face, other)


def unpack_kernel(
    owner_in, start_in, count_in, flip_in, diagonal_in, in_ref,
    solution_ref, residual_ref,
    owner_ref, start_ref, count_ref, flip_ref, diagonal_ref, rows_ref, sems,
):
    copies = copy_in(
        [
            (owner_in, owner_ref), (start_in, start_ref), (count_in, count_ref),
            (flip_in, flip_ref), (diagonal_in, diagonal_ref),
        ],
        sems,
    )
    own = lax.axis_index("cross")
    group = lax.axis_index("stream") & 3
    face = pl.multiple_of(group * 32, 32)
    other = pl.multiple_of(((group + 2) & 3) * 32, 32)
    for link in range(LINKS):
        rows_ref[link] = in_ref[link * LANES:(link + 1) * LANES, :].T
    for copy in copies:
        copy.wait()
    for link in range(LINKS):
        window = slice(link * WINDOW, (link + 1) * WINDOW)
        matrix = onehot(places(own, link, owner_ref, start_ref, count_ref, flip_ref))
        slots = jnp.concatenate(
            [rows_ref[link, pl.ds(face, 32), :], rows_ref[link, pl.ds(other, 32), :]], axis=1
        )
        high, middle, low = [
            jnp.dot(part, matrix, preferred_element_type=F32) for part in thirds(slots)
        ]
        cells = (low + middle) + high
        for p in range(PLANES):
            residual = cells[16 + 8 * p:16 + 8 * p + VARS] * diagonal_ref[p:p + 1, window]
            for a in range(VARS):
                solution_ref[a, p:p + 1, window] = cells[8 * p + a:8 * p + a + 1]
                residual_ref[a, p:p + 1, window] = residual[a:a + 1]


def shape(*dims):
    return jax.ShapeDtypeStruct(dims, F32)


def local(
    rhs,
    diagonal,
    lower_transfer,
    upper_transfer,
    face_owner,
    face_start,
    face_count,
    face_flip,
    block_cells,
):
    owner, start, count, flip = face_owner.T, face_start.T, face_count.T, face_flip.T
    transfer = pltpu.VMEM((VARS, VARS, PLANES, CELLS), F32)
    planes = pltpu.VMEM((PLANES, CELLS), F32)
    packed = pl.pallas_call(
        pack_kernel,
        out_shape=shape(CELLS, LANES),
        in_specs=[HBM] * 9,
        out_specs=VMEM,
        scratch_shapes=[TABLE] * 4
        + [
            pltpu.SMEM((CROSS,), jnp.int32), pltpu.VMEM((VARS, PLANES, CELLS), F32), planes,
            transfer, transfer, pltpu.VMEM((LANES, CELLS), F32), pltpu.SemaphoreType.DMA((9,)),
        ],
        compiler_params=WIDE,
        name="pack_cells",
    )(
        owner, start, count, flip,
        block_cells,
        rhs.transpose(1, 0, 2),
        diagonal,
        lower_transfer.transpose(1, 2, 0, 3),
        upper_transfer.transpose(1, 2, 0, 3),
    )
    arrived = lax.all_to_all(packed.reshape(STREAM * CROSS, 2, LANES), BOTH, 0, 0, tiled=True)

    passes = pltpu.VMEM((GROUPS, CHUNKS, 16, LANES), F32)
    chunks = pltpu.VMEM((CHUNKS, 16, LANES), F32)
    results = pl.pallas_call(
        solve_kernel,
        out_shape=shape(STREAM * CROSS, LANES),
        in_specs=[HBM, HBM, VMEM],
        out_specs=VMEM,
        scratch_shapes=[TABLE] * 2
        + [pltpu.VMEM((CHUNKS, LANES, LANES), F32)]
        + [chunks] * 4
        + [passes] * 3
        + [pltpu.SemaphoreType.DMA((2,))],
        compiler_params=PARAMS,
        name="solve_cells",
    )(owner, count, arrived.reshape(CELLS, LANES))
    returned = lax.all_to_all(results.reshape(STREAM * CROSS, 1, LANES), BOTH, 0, 0, tiled=True)
    outs = pl.pallas_call(
        unpack_kernel,
        out_shape=[shape(VARS, PLANES, CELLS)] * 2,
        in_specs=[HBM] * 5 + [VMEM],
        out_specs=[VMEM] * 2,
        scratch_shapes=[TABLE] * 4
        + [planes, pltpu.VMEM((LINKS, LANES, LANES), F32), pltpu.SemaphoreType.DMA((5,))],
        compiler_params=PARAMS,
        name="unpack_cells",
    )(owner, start, count, flip, diagonal, returned.reshape(STREAM * CROSS, LANES))
    return tuple(x.transpose(1, 0, 2) for x in outs)


def solution(mesh):
    return jax.shard_map(
        local,
        mesh=mesh,
        in_specs=(
            P("stream", None, "cross"),
            P("stream", "cross"),
            P("stream", None, None, "cross"),
            P("stream", None, None, "cross"),
            P(),
            P(),
            P(),
            P(),
            P(),
        ),
        out_specs=(P("stream", None, "cross"), P("stream", None, "cross")),
        check_vma=False,
    )
```

```python
import functools

import jax
import jax.numpy as jnp
from jax import lax
from jax.experimental import pallas as pl
from jax.experimental.pallas import tpu as pltpu
from jax.sharding import PartitionSpec as P

VARS = 5
CELLS = 1024
LINKS = 4
WINDOW = CELLS // LINKS
STREAM = 32
CROSS = 16
PLANES = 2
CHUNKS = 8
GROUPS = 4
LANES = 128
FACE_WEIGHT = 0.25

LOWER = 0
UPPER = 25
SOURCE = 50
ROWS = 110
KEPT = 28
PIECES = 7

F32 = jnp.float32
BF16 = jnp.bfloat16
HBM = pl.BlockSpec(memory_space=pltpu.HBM)
SMEM = pl.BlockSpec(memory_space=pltpu.SMEM)
VMEM = pl.BlockSpec(memory_space=pltpu.VMEM)
PARAMS = pltpu.CompilerParams(vmem_limit_bytes=24 * 1024 * 1024)
WIDE = pltpu.CompilerParams(vmem_limit_bytes=62 * 1024 * 1024)
TABLE = pltpu.SMEM((LINKS, CROSS), jnp.int32)


def thirds(x):
    high = x.astype(BF16)
    rest = x - high.astype(F32)
    middle = rest.astype(BF16)
    low = (rest - middle.astype(F32)).astype(BF16)
    return jnp.concatenate([high, middle, low], axis=0)


def times(x, matrix):
    n = x.shape[0]
    parts = jnp.dot(thirds(x), matrix, preferred_element_type=F32)
    return (parts[2 * n:] + parts[n:2 * n]) + parts[:n]


def copy_in(pairs, sems):
    copies = [pltpu.make_async_copy(src, dst, sems.at[i]) for i, (src, dst) in enumerate(pairs)]
    for copy in copies:
        copy.start()
    return copies


def slots_of(own, link, owner_ref, start_ref, count_ref, flip_ref):
    owner = owner_ref[link, own]
    count = count_ref[link, own]
    turned = jnp.logical_and(flip_ref[link, own] == 1, own > owner)
    bound = jnp.where(turned, count, 0)
    offset = start_ref[link, own] - link * WINDOW
    cell = lax.broadcasted_iota(jnp.int32, (1, WINDOW), 1)
    place = (cell - offset) & (WINDOW - 1)
    place = jnp.where(place < bound, count - 1 - place, place)
    rest = place & 127
    return ((rest >> 4) << 5) + ((place >> 7) << 4) + (rest & 15)


def onehot(row):
    rows = lax.broadcasted_iota(jnp.int32, (WINDOW, WINDOW), 0)
    return jnp.where(rows == row, 1.0, 0.0).astype(BF16)


def pack_kernel(
    owner_in, start_in, count_in, flip_in, live_in, rhs_in, diagonal_in, lower_in, upper_in,
    out_ref, slots_ref,
    owner_ref, start_ref, count_ref, flip_ref, live_ref, rhs_ref, diagonal_ref, lower_ref, upper_ref,
    rows_ref, matrix_ref, sems,
):
    copies = copy_in(
        [
            (owner_in, owner_ref), (start_in, start_ref), (count_in, count_ref),
            (flip_in, flip_ref), (live_in, live_ref), (rhs_in, rhs_ref),
            (diagonal_in, diagonal_ref), (lower_in, lower_ref), (upper_in, upper_ref),
        ],
        sems,
    )
    own = lax.axis_index("cross")
    rows_ref[pl.ds(ROWS, LANES - ROWS), :] = jnp.zeros((LANES - ROWS, CELLS), F32)
    for copy in copies[:5]:
        copy.wait()
    for link in range(LINKS):
        slots = slots_of(own, link, owner_ref, start_ref, count_ref, flip_ref)
        slots_ref[link:link + 1, :] = slots
        matrix_ref[link] = onehot(slots)
    for copy in copies[5:]:
        copy.wait()
    cell = lax.broadcasted_iota(jnp.int32, (PLANES, CELLS), 1)
    live = cell < live_ref[own]
    for a in range(VARS):
        for b in range(VARS):
            at = VARS * a + b
            rows_ref[pl.ds(2 * (LOWER + at), 2), :] = lower_ref[a, b]
            rows_ref[pl.ds(2 * (UPPER + at), 2), :] = upper_ref[a, b]
        source = jnp.where(live, rhs_ref[a], 0.0) / diagonal_ref[...]
        rows_ref[pl.ds(2 * (SOURCE + a), 2), :] = source
    for link in range(LINKS):
        parts = lax.dot_general(
            matrix_ref[link],
            thirds(rows_ref[:, link * WINDOW:(link + 1) * WINDOW]),
            (((1,), (1,)), ((), ())),
            preferred_element_type=F32,
        )
        out_ref[link * WINDOW:(link + 1) * WINDOW, :] = (
            parts[:, 2 * LANES:] + parts[:, LANES:2 * LANES]
        ) + parts[:, :LANES]


def entry(system_ref, k, p, at):
    row = 2 * at + p
    return system_ref[k, row:row + 1, :]


def terms(system_ref, k, p, at, state):
    return [
        [entry(system_ref, k, p, at + VARS * a + b) * state[b] for b in range(VARS)]
        for a in range(VARS)
    ]


def total(rows, first=None):
    if first is None:
        return tuple((t[0] + t[1]) + (t[2] + t[3]) + t[4] for t in rows)
    return tuple(((x + t[0]) + (t[1] + t[2])) + (t[3] + t[4]) for x, t in zip(first, rows))


def get_rows(ref, k, p):
    return [ref[k, 8 * p + a:8 * p + a + 1, :] for a in range(VARS)]


def put_rows(ref, k, p, rows):
    for a in range(VARS):
        ref[k, 8 * p + a:8 * p + a + 1, :] = rows[a]


def turn(state, by):
    return tuple(pltpu.roll(x, by, 1) for x in state)


def lower_sweep(step):
    state = tuple(jnp.zeros((1, LANES), F32) for _ in range(VARS))
    for group in range(GROUPS):
        if group:
            state = turn(state, 32)
        state = lax.fori_loop(0, CHUNKS, functools.partial(step, group), state, unroll=True)


def upper_sweep(step):
    state = tuple(jnp.zeros((1, LANES), F32) for _ in range(VARS))
    for group in reversed(range(GROUPS)):
        if group < GROUPS - 1:
            state = turn(state, 96)
        state = lax.fori_loop(
            0, CHUNKS, lambda i, x: step(group, CHUNKS - 1 - i, x), state, unroll=True
        )


def merged(ref):
    shape = (CHUNKS * 16, LANES)
    lane = lax.broadcasted_iota(jnp.int32, shape, 1) >> 5
    row = lax.broadcasted_iota(jnp.int32, shape, 0) & 7
    parts = [ref[group].reshape(shape) for group in range(GROUPS)]
    out = jnp.where(lane == 0, parts[0], jnp.where(lane == 1, parts[1], jnp.where(lane == 2, parts[2], parts[3])))
    return jnp.where(row < VARS, out, 0.0)


def upper_pass(system_ref, lowered_ref, coupled_ref, delta_ref):
    def upper(group, k, state):
        for p in reversed(range(PLANES)):
            coupled = terms(system_ref, k, p, UPPER, state)
            put_rows(coupled_ref.at[group], k, p, total(coupled))
            state = total(coupled, get_rows(lowered_ref.at[group], k, p))
            put_rows(delta_ref.at[group], k, p, state)
        return state

    upper_sweep(upper)


def face_matrix(owner_ref, count_ref):
    position = lax.axis_index("stream")
    link = position >> 3
    slot = ((position & 7) << 4) + lax.axis_index("cross")
    lane = lax.broadcasted_iota(jnp.int32, (1, LANES), 1)
    source = jnp.full((1, LANES), -1, jnp.int32)
    for block in range(CROSS):
        taken = jnp.where(slot < count_ref[link, block], owner_ref[link, block], -LANES)
        source = jnp.where((lane & 31) == block, (lane & 96) + taken, source)
    rows = lax.broadcasted_iota(jnp.int32, (LANES, LANES), 0)
    return jnp.where(rows == source, FACE_WEIGHT, 0.0).astype(BF16)


def faces_kernel(in_ref, out_ref):
    lane = lax.broadcasted_iota(jnp.int32, (CROSS, LANES), 1)
    for row in range(KEPT):
        piece = row % PIECES
        first = 32 * (KEPT + row // PIECES)
        spare = pltpu.roll(in_ref[first:first + CROSS, :], ROWS - 16 * piece, 1)
        own = in_ref[32 * row:32 * row + CROSS, :]
        out_ref[pl.ds(row, CROSS, stride=KEPT), :] = jnp.where(lane < ROWS, own, spare)


def face_rows(face_ref, chunk):
    if chunk < KEPT:
        return face_ref[pl.ds(chunk, CROSS, stride=KEPT), :]
    piece_of = lax.broadcasted_iota(jnp.int32, (CROSS, LANES), 1) >> 4
    out = jnp.zeros((CROSS, LANES), F32)
    for piece in range(PIECES):
        row = PIECES * (chunk - KEPT) + piece
        moved = pltpu.roll(
            face_ref[pl.ds(row, CROSS, stride=KEPT), :], LANES - ROWS + 16 * piece, 1
        )
        out = jnp.where(piece_of == piece, moved, out)
    return out


def solve_kernel(
    owner_in, count_in, in_ref, face_ref, out_ref, send_ref,
    owner_ref, count_ref, system_ref, faces_ref, last_ref, solution_ref, residual_ref,
    lowered_ref, coupled_ref, delta_ref, values_ref, sems,
):
    values_ref[160:, :] = jnp.zeros((96, LANES), F32)
    copies = copy_in([(owner_in, owner_ref), (count_in, count_ref)], sems)
    for k in range(CHUNKS):
        parts = []
        for group in range(GROUPS):
            chunk = CHUNKS * group + k
            parts += [
                face_rows(face_ref, chunk),
                in_ref[32 * chunk + 16:32 * chunk + 32, :],
            ]
        system_ref[k] = jnp.concatenate(parts, axis=0).T
    for copy in copies:
        copy.wait()
    matrix = face_matrix(owner_ref, count_ref)

    def lower_first(group, k, state):
        for p in range(PLANES):
            along = terms(system_ref, k, p, LOWER, state)
            state = total(along, [entry(system_ref, k, p, SOURCE + a) for a in range(VARS)])
            put_rows(lowered_ref.at[group], k, p, state)
        return state

    lower_sweep(lower_first)
    upper_pass(system_ref, lowered_ref, coupled_ref, delta_ref)
    last_ref[...] = merged(coupled_ref).reshape(last_ref.shape)
    first = merged(delta_ref)
    faces_ref[...] = times(first, matrix).reshape(faces_ref.shape)

    def lower_second(group, k, state):
        for p in range(PLANES):
            along = terms(system_ref, k, p, LOWER, state)
            faces = get_rows(faces_ref, k, p)
            put_rows(lowered_ref.at[group], k, p, total(along, faces))
            state = total(along, [f + e for f, e in zip(faces, get_rows(last_ref, k, p))])
        return state

    lower_sweep(lower_second)
    upper_pass(system_ref, lowered_ref, coupled_ref, delta_ref)
    second = merged(delta_ref)
    solution_ref[...] = (first + second).reshape(solution_ref.shape)
    last_ref[...] = merged(coupled_ref).reshape(last_ref.shape)
    lane = lax.broadcasted_iota(jnp.int32, (1, LANES), 1)
    for k in range(CHUNKS):
        if k:
            before = get_rows(last_ref, k - 1, 1)
        else:
            before = [
                jnp.where(lane < 32, 0.0, x) for x in turn(get_rows(last_ref, CHUNKS - 1, 1), 32)
            ]
        put_rows(residual_ref, k, 0, total(terms(system_ref, k, 0, LOWER, before)))
        before = get_rows(last_ref, k, 0)
        put_rows(residual_ref, k, 1, total(terms(system_ref, k, 1, LOWER, before)))
    residual_ref[...] = residual_ref[...] + times(second, matrix).reshape(residual_ref.shape)

    for k in range(CHUNKS):
        out_ref[k, 0:16, :] = solution_ref[k]
        out_ref[k, 16:32, :] = residual_ref[k]
    for k in range(CHUNKS):
        for g in range(4):
            at = 5 * (4 * k + g)
            values_ref[at:at + VARS, :] = out_ref[k, 8 * g:8 * g + VARS, :]
    turned = values_ref[0:LANES, :].T
    others = values_ref[LANES:2 * LANES, :].T
    lane_group = lax.broadcasted_iota(jnp.int32, (CROSS, LANES), 1) >> 5
    fifth = others[0:CROSS]
    for group in range(GROUPS):
        rows = slice(32 * group, 32 * group + CROSS)
        send_ref[pl.ds(group, CROSS, stride=5), :] = turned[rows]
        if group:
            fifth = jnp.where(lane_group == group, pltpu.roll(others[rows], 32 * group, 1), fifth)
    send_ref[pl.ds(4, CROSS, stride=5), :] = fifth


def regroup(parts):
    lane = lax.broadcasted_iota(jnp.int32, parts[0].shape, 1)
    first_half = lane < 64
    even = (lane & 32) == 0
    half = [None] * 4
    for i in range(2):
        x, y = parts[i], parts[i + 2]
        half[i] = jnp.where(first_half, x, pltpu.roll(y, 64, 1))
        half[i + 2] = jnp.where(first_half, pltpu.roll(x, 64, 1), y)
    out = [None] * 4
    for i in (0, 2):
        x, y = half[i], half[i + 1]
        out[i] = jnp.where(even, x, pltpu.roll(y, 32, 1))
        out[i + 1] = jnp.where(even, pltpu.roll(x, 96, 1), y)
    return out


def join_kernel(in_ref, face_ref, out_ref, values_ref):
    lane = lax.broadcasted_iota(jnp.int32, (8, LANES), 1)
    returned = (lane & 16) == 0
    blank = jnp.zeros((16, LANES), F32)
    fifth = face_ref[pl.ds(4, CROSS, stride=5), :]
    parts = []
    others = []
    for group in range(GROUPS):
        parts += [face_ref[pl.ds(group, CROSS, stride=5), :], blank]
        others += [pltpu.roll(fifth, (LANES - 32 * group) % LANES, 1) if group else fifth, blank]
    values_ref[0:LANES, :] = jnp.concatenate(parts, axis=0).T
    values_ref[LANES:2 * LANES, :] = jnp.concatenate(others, axis=0).T
    for k in range(CHUNKS):
        tiles = []
        for g in range(4):
            at = 5 * (4 * k + g)
            tiles.append(jnp.where(returned, values_ref[at:at + 8, :], in_ref[k, 8 * g:8 * g + 8, :]))
        for group, tile in enumerate(regroup(tiles)):
            out_ref[CHUNKS * group + k] = tile


def unpack_kernel(slots_ref, diagonal_ref, in_ref, solution_ref, residual_ref, rows_ref):
    for column in range(8):
        tiles = regroup([in_ref[4 * column + e] for e in range(4)])
        for g, tile in enumerate(tiles):
            rows_ref[8 * g:8 * g + 8, LANES * column:LANES * (column + 1)] = tile
    for link in range(LINKS):
        window = slice(link * WINDOW, (link + 1) * WINDOW)
        cells = times(rows_ref[:, window], onehot(slots_ref[link:link + 1, :]))
        for p in range(PLANES):
            residual = cells[16 + 8 * p:16 + 8 * p + VARS] * diagonal_ref[p:p + 1, window]
            for a in range(VARS):
                solution_ref[a, p:p + 1, window] = cells[8 * p + a:8 * p + a + 1]
                residual_ref[a, p:p + 1, window] = residual[a:a + 1]


def shape(*dims):
    return jax.ShapeDtypeStruct(dims, F32)


def local(
    rhs,
    diagonal,
    lower_transfer,
    upper_transfer,
    face_owner,
    face_start,
    face_count,
    face_flip,
    block_cells,
):
    owner, start, count, flip = face_owner.T, face_start.T, face_count.T, face_flip.T
    transfer = pltpu.VMEM((VARS, VARS, PLANES, CELLS), F32)
    planes = pltpu.VMEM((PLANES, CELLS), F32)
    packed, slots = pl.pallas_call(
        pack_kernel,
        out_shape=[shape(CELLS, LANES), jax.ShapeDtypeStruct((LINKS, WINDOW), jnp.int32)],
        in_specs=[HBM] * 9,
        out_specs=[VMEM] * 2,
        scratch_shapes=[TABLE] * 4
        + [
            pltpu.SMEM((CROSS,), jnp.int32), pltpu.VMEM((VARS, PLANES, CELLS), F32), planes,
            transfer, transfer, pltpu.VMEM((LANES, CELLS), F32),
            pltpu.VMEM((LINKS, WINDOW, WINDOW), BF16), pltpu.SemaphoreType.DMA((9,)),
        ],
        compiler_params=WIDE,
        name="pack_cells",
    )(
        owner, start, count, flip,
        block_cells,
        rhs.transpose(1, 0, 2),
        diagonal,
        lower_transfer.transpose(1, 2, 0, 3),
        upper_transfer.transpose(1, 2, 0, 3),
    )
    arrived = lax.all_to_all(packed.reshape(STREAM, 32, LANES), "stream", 0, 0, tiled=True)
    arrived = arrived.reshape(CELLS, LANES)
    faces = pl.pallas_call(
        faces_kernel,
        out_shape=shape(CROSS * KEPT, LANES),
        in_specs=[VMEM],
        out_specs=VMEM,
        compiler_params=PARAMS,
        name="take_faces",
    )(arrived)
    faces = lax.all_to_all(faces.reshape(CROSS * KEPT // 4, 4, LANES), "cross", 0, 0, tiled=True)

    passes = pltpu.VMEM((GROUPS, CHUNKS, 16, LANES), F32)
    chunks = pltpu.VMEM((CHUNKS, 16, LANES), F32)
    results, faces = pl.pallas_call(
        solve_kernel,
        out_shape=[shape(CHUNKS, 32, LANES), shape(5 * CROSS, LANES)],
        in_specs=[HBM, HBM, VMEM, VMEM],
        out_specs=[VMEM, VMEM],
        scratch_shapes=[TABLE] * 2
        + [pltpu.VMEM((CHUNKS, LANES, LANES), F32)]
        + [chunks] * 4
        + [passes] * 3
        + [pltpu.VMEM((2 * LANES, LANES), F32), pltpu.SemaphoreType.DMA((2,))],
        compiler_params=PARAMS,
        name="solve_cells",
    )(owner, count, arrived, faces.reshape(CROSS * KEPT, LANES))
    faces = lax.all_to_all(faces.reshape(5 * CROSS, 1, LANES), "cross", 0, 0, tiled=True)
    results = pl.pallas_call(
        join_kernel,
        out_shape=shape(STREAM, 8, LANES),
        in_specs=[VMEM, VMEM],
        out_specs=VMEM,
        scratch_shapes=[pltpu.VMEM((2 * LANES, LANES), F32)],
        compiler_params=PARAMS,
        name="join_faces",
    )(results, faces.reshape(5 * CROSS, LANES))
    returned = lax.all_to_all(results, "stream", 0, 0, tiled=True)
    outs = pl.pallas_call(
        unpack_kernel,
        out_shape=[shape(VARS, PLANES, CELLS)] * 2,
        in_specs=[VMEM] * 3,
        out_specs=[VMEM] * 2,
        scratch_shapes=[pltpu.VMEM((32, CELLS), F32)],
        compiler_params=PARAMS,
        name="unpack_cells",
    )(slots, diagonal, returned)
    return tuple(x.transpose(1, 0, 2) for x in outs)


def solution(mesh):
    return jax.shard_map(
        local,
        mesh=mesh,
        in_specs=(
            P("stream", None, "cross"),
            P("stream", "cross"),
            P("stream", None, None, "cross"),
            P("stream", None, None, "cross"),
            P(),
            P(),
            P(),
            P(),
            P(),
        ),
        out_specs=(P("stream", None, "cross"), P("stream", None, "cross")),
        check_vma=False,
    )
```

```python
import functools

import jax
import jax.numpy as jnp
from jax import lax
from jax.experimental import pallas as pl
from jax.experimental.pallas import tpu as pltpu
from jax.sharding import PartitionSpec as P

VARS = 5
CELLS = 1024
LINKS = 4
WINDOW = CELLS // LINKS
STREAM = 32
CROSS = 16
PLANES = 2
CHUNKS = 8
GROUPS = 4
LANES = 128
FACE_WEIGHT = 0.25

LOWER = 0
UPPER = 25
SOURCE = 50
ROWS = 110
KEPT = 28
PIECES = 7

F32 = jnp.float32
BF16 = jnp.bfloat16
HBM = pl.BlockSpec(memory_space=pltpu.HBM)
SMEM = pl.BlockSpec(memory_space=pltpu.SMEM)
VMEM = pl.BlockSpec(memory_space=pltpu.VMEM)
PARAMS = pltpu.CompilerParams(vmem_limit_bytes=24 * 1024 * 1024)
WIDE = pltpu.CompilerParams(vmem_limit_bytes=62 * 1024 * 1024)
TABLE = pltpu.SMEM((LINKS, CROSS), jnp.int32)


def thirds(x):
    high = x.astype(BF16)
    rest = x - high.astype(F32)
    middle = rest.astype(BF16)
    low = (rest - middle.astype(F32)).astype(BF16)
    return jnp.concatenate([high, middle, low], axis=0)


def times(x, matrix):
    n = x.shape[0]
    parts = jnp.dot(thirds(x), matrix, preferred_element_type=F32)
    return (parts[2 * n:] + parts[n:2 * n]) + parts[:n]


def copy_in(pairs, sems):
    copies = [pltpu.make_async_copy(src, dst, sems.at[i]) for i, (src, dst) in enumerate(pairs)]
    for copy in copies:
        copy.start()
    return copies


def slots_of(own, link, owner_ref, start_ref, count_ref, flip_ref):
    owner = owner_ref[link, own]
    count = count_ref[link, own]
    turned = jnp.logical_and(flip_ref[link, own] == 1, own > owner)
    bound = jnp.where(turned, count, 0)
    offset = start_ref[link, own] - link * WINDOW
    cell = lax.broadcasted_iota(jnp.int32, (1, WINDOW), 1)
    place = (cell - offset) & (WINDOW - 1)
    place = jnp.where(place < bound, count - 1 - place, place)
    rest = place & 127
    return ((rest >> 4) << 5) + ((place >> 7) << 4) + (rest & 15)


def onehot(row):
    rows = lax.broadcasted_iota(jnp.int32, (WINDOW, WINDOW), 0)
    return jnp.where(rows == row, 1.0, 0.0).astype(BF16)


def pack_kernel(
    owner_in, start_in, count_in, flip_in, live_in, rhs_in, diagonal_in, lower_in, upper_in,
    out_ref, slots_ref,
    owner_ref, start_ref, count_ref, flip_ref, live_ref, rhs_ref, diagonal_ref, lower_ref, upper_ref,
    rows_ref, matrix_ref, sems,
):
    copies = copy_in(
        [
            (owner_in, owner_ref), (start_in, start_ref), (count_in, count_ref),
            (flip_in, flip_ref), (live_in, live_ref), (rhs_in, rhs_ref),
            (diagonal_in, diagonal_ref), (lower_in, lower_ref), (upper_in, upper_ref),
        ],
        sems,
    )
    own = lax.axis_index("cross")
    rows_ref[pl.ds(ROWS, LANES - ROWS), :] = jnp.zeros((LANES - ROWS, CELLS), F32)
    for copy in copies[:5]:
        copy.wait()
    for link in range(LINKS):
        slots = slots_of(own, link, owner_ref, start_ref, count_ref, flip_ref)
        slots_ref[link:link + 1, :] = slots
        matrix_ref[link] = onehot(slots)
    for copy in copies[5:]:
        copy.wait()
    cell = lax.broadcasted_iota(jnp.int32, (PLANES, CELLS), 1)
    live = cell < live_ref[own]
    for a in range(VARS):
        for b in range(VARS):
            at = VARS * a + b
            rows_ref[pl.ds(2 * (LOWER + at), 2), :] = lower_ref[a, b]
            rows_ref[pl.ds(2 * (UPPER + at), 2), :] = upper_ref[a, b]
        source = jnp.where(live, rhs_ref[a], 0.0) / diagonal_ref[...]
        rows_ref[pl.ds(2 * (SOURCE + a), 2), :] = source
    for link in range(LINKS):
        parts = lax.dot_general(
            matrix_ref[link],
            thirds(rows_ref[:, link * WINDOW:(link + 1) * WINDOW]),
            (((1,), (1,)), ((), ())),
            preferred_element_type=F32,
        )
        out_ref[link * WINDOW:(link + 1) * WINDOW, :] = (
            parts[:, 2 * LANES:] + parts[:, LANES:2 * LANES]
        ) + parts[:, :LANES]


def total(rows, first=None):
    if first is None:
        return [(t[0] + t[1]) + (t[2] + t[3]) + t[4] for t in rows]
    return [((x + t[0]) + (t[1] + t[2])) + (t[3] + t[4]) for x, t in zip(first, rows)]


def entry(system_ref, at, p):
    row = 8 * (2 * at + p)
    return system_ref[row:row + 8, :]


def apply(system_ref, at, p, x, first=None):
    return total(
        [[entry(system_ref, at + VARS * a + b, p) * x[b] for b in range(VARS)] for a in range(VARS)],
        first,
    )


def compose(system_ref, at, later, earlier, out_ref):
    for c in range(VARS):
        column = [entry(system_ref, at + VARS * b + c, earlier) for b in range(VARS)]
        for a, x in enumerate(apply(system_ref, at, later, column)):
            out_ref[VARS * a + c] = x


def relay(matrix_ref, offset, offset_ref, state_ref, up):
    for a in range(VARS):
        offset_ref[a] = offset[a]
    state = [jnp.zeros((1, LANES), F32) for _ in range(VARS)]
    groups = range(GROUPS) if up else range(GROUPS - 1, -1, -1)
    chunks = range(CHUNKS) if up else range(CHUNKS - 1, -1, -1)
    for group in groups:
        if group != groups[0]:
            state = [pltpu.roll(x, 32 if up else 96, 1) for x in state]
        for k in chunks:
            row = slice(k, k + 1)
            for a in range(VARS):
                state_ref[group, a, row, :] = state[a]
            state = total(
                [
                    [matrix_ref[VARS * a + b, row, :] * state[b] for b in range(VARS)]
                    for a in range(VARS)
                ],
                [offset_ref[a, row, :] for a in range(VARS)],
            )
    lane = lax.broadcasted_iota(jnp.int32, (CHUNKS, LANES), 1) >> 5
    out = []
    for a in range(VARS):
        x = state_ref[GROUPS - 1, a]
        for group in range(GROUPS - 1):
            x = jnp.where(lane == group, state_ref[group, a], x)
        out.append(x)
    return out


def plus(x, y):
    return [a + b for a, b in zip(x, y)]


def face_matrix(owner_ref, count_ref):
    position = lax.axis_index("stream")
    link = position >> 3
    slot = ((position & 7) << 4) + lax.axis_index("cross")
    lane = lax.broadcasted_iota(jnp.int32, (1, LANES), 1)
    source = jnp.full((1, LANES), -1, jnp.int32)
    for block in range(CROSS):
        taken = jnp.where(slot < count_ref[link, block], owner_ref[link, block], -LANES)
        source = jnp.where((lane & 31) == block, (lane & 96) + taken, source)
    rows = lax.broadcasted_iota(jnp.int32, (LANES, LANES), 0)
    return jnp.where(rows == source, FACE_WEIGHT, 0.0).astype(BF16)


def faces_kernel(in_ref, out_ref):
    lane = lax.broadcasted_iota(jnp.int32, (CROSS, LANES), 1)
    for row in range(KEPT):
        piece = row % PIECES
        first = 32 * (KEPT + row // PIECES)
        spare = pltpu.roll(in_ref[first:first + CROSS, :], ROWS - 16 * piece, 1)
        own = in_ref[32 * row:32 * row + CROSS, :]
        out_ref[pl.ds(row, CROSS, stride=KEPT), :] = jnp.where(lane < ROWS, own, spare)


def face_rows(face_ref, chunk):
    if chunk < KEPT:
        return face_ref[pl.ds(chunk, CROSS, stride=KEPT), :]
    piece_of = lax.broadcasted_iota(jnp.int32, (CROSS, LANES), 1) >> 4
    out = jnp.zeros((CROSS, LANES), F32)
    for piece in range(PIECES):
        row = PIECES * (chunk - KEPT) + piece
        moved = pltpu.roll(
            face_ref[pl.ds(row, CROSS, stride=KEPT), :], LANES - ROWS + 16 * piece, 1
        )
        out = jnp.where(piece_of == piece, moved, out)
    return out


def solve_kernel(
    owner_in, count_in, in_ref, face_ref, out_ref, send_ref,
    owner_ref, count_ref, system_ref, lower_ref, upper_ref, offset_ref, state_ref, values_ref, sems,
):
    copies = copy_in([(owner_in, owner_ref), (count_in, count_ref)], sems)
    values_ref[160:, :] = jnp.zeros((96, LANES), F32)
    for k in range(CHUNKS):
        parts = []
        for group in range(GROUPS):
            chunk = CHUNKS * group + k
            parts += [face_rows(face_ref, chunk), in_ref[32 * chunk + 16:32 * chunk + 32, :]]
        system_ref[pl.ds(k, LANES, stride=CHUNKS), :] = jnp.concatenate(parts, axis=0).T
    for copy in copies:
        copy.wait()
    matrix = face_matrix(owner_ref, count_ref)
    lower = functools.partial(apply, system_ref, LOWER)
    upper = functools.partial(apply, system_ref, UPPER)
    compose(system_ref, LOWER, 1, 0, lower_ref)
    compose(system_ref, UPPER, 0, 1, upper_ref)

    def upper_sweep(lowered):
        offset = upper(0, lowered[1], lowered[0])
        after = relay(upper_ref, offset, offset_ref, state_ref, False)
        coupled_1 = upper(1, after)
        delta_1 = plus(lowered[1], coupled_1)
        coupled_0 = upper(0, delta_1)
        return [coupled_0, coupled_1], [plus(lowered[0], coupled_0), delta_1]

    def faces_of(delta):
        parts = times(jnp.concatenate(delta[0] + delta[1], axis=0), matrix)
        rows = [parts[CHUNKS * i:CHUNKS * (i + 1)] for i in range(2 * VARS)]
        return [rows[:VARS], rows[VARS:]]

    source = [[entry(system_ref, SOURCE + a, p) for a in range(VARS)] for p in range(PLANES)]
    before = relay(lower_ref, lower(1, source[0], source[1]), offset_ref, state_ref, True)
    lowered_0 = lower(0, before, source[0])
    lowered_1 = lower(1, lowered_0, source[1])
    coupled, first = upper_sweep([lowered_0, lowered_1])

    faces = faces_of(first)
    joint_0 = plus(faces[0], coupled[0])
    joint_1 = plus(faces[1], coupled[1])
    before = relay(lower_ref, lower(1, joint_0, joint_1), offset_ref, state_ref, True)
    along = lower(0, before)
    lowered_1 = lower(1, plus(joint_0, along), faces[1])
    coupled, second = upper_sweep([plus(faces[0], along), lowered_1])

    faces = faces_of(second)
    row = lax.broadcasted_iota(jnp.int32, (CHUNKS, LANES), 0)
    lane = lax.broadcasted_iota(jnp.int32, (CHUNKS, LANES), 1)
    previous = []
    for x in coupled[1]:
        x = pltpu.roll(x, 1, 0)
        x = jnp.where(row == 0, jnp.where(lane < 32, 0.0, pltpu.roll(x, 32, 1)), x)
        previous.append(x)
    results = [
        plus(first[0], second[0]),
        plus(first[1], second[1]),
        lower(0, previous, faces[0]),
        lower(1, coupled[0], faces[1]),
    ]
    for g in range(4):
        for a in range(VARS):
            out_ref[pl.ds(8 * g + a, CHUNKS, stride=32), :] = results[g][a]
            values_ref[pl.ds(5 * g + a, CHUNKS, stride=20), :] = results[g][a]
    turned = values_ref[0:LANES, :].T
    others = values_ref[LANES:2 * LANES, :].T
    lane_group = lax.broadcasted_iota(jnp.int32, (CROSS, LANES), 1) >> 5
    fifth = others[0:CROSS]
    for group in range(GROUPS):
        rows = slice(32 * group, 32 * group + CROSS)
        send_ref[pl.ds(group, CROSS, stride=5), :] = turned[rows]
        if group:
            fifth = jnp.where(lane_group == group, pltpu.roll(others[rows], 32 * group, 1), fifth)
    send_ref[pl.ds(4, CROSS, stride=5), :] = fifth


def regroup(parts):
    lane = lax.broadcasted_iota(jnp.int32, parts[0].shape, 1)
    first_half = lane < 64
    even = (lane & 32) == 0
    half = [None] * 4
    for i in range(2):
        x, y = parts[i], parts[i + 2]
        half[i] = jnp.where(first_half, x, pltpu.roll(y, 64, 1))
        half[i + 2] = jnp.where(first_half, pltpu.roll(x, 64, 1), y)
    out = [None] * 4
    for i in (0, 2):
        x, y = half[i], half[i + 1]
        out[i] = jnp.where(even, x, pltpu.roll(y, 32, 1))
        out[i + 1] = jnp.where(even, pltpu.roll(x, 96, 1), y)
    return out


def join_kernel(in_ref, face_ref, out_ref, values_ref):
    lane = lax.broadcasted_iota(jnp.int32, (8, LANES), 1)
    returned = (lane & 16) == 0
    blank = jnp.zeros((16, LANES), F32)
    fifth = face_ref[pl.ds(4, CROSS, stride=5), :]
    parts = []
    others = []
    for group in range(GROUPS):
        parts += [face_ref[pl.ds(group, CROSS, stride=5), :], blank]
        others += [pltpu.roll(fifth, (LANES - 32 * group) % LANES, 1) if group else fifth, blank]
    values_ref[0:LANES, :] = jnp.concatenate(parts, axis=0).T
    values_ref[LANES:2 * LANES, :] = jnp.concatenate(others, axis=0).T
    for k in range(CHUNKS):
        tiles = []
        for g in range(4):
            at = 5 * (4 * k + g)
            tiles.append(jnp.where(returned, values_ref[at:at + 8, :], in_ref[32 * k + 8 * g:32 * k + 8 * g + 8, :]))
        for group, tile in enumerate(regroup(tiles)):
            out_ref[CHUNKS * group + k] = tile


def unpack_kernel(slots_ref, diagonal_ref, in_ref, solution_ref, residual_ref, rows_ref):
    for column in range(8):
        tiles = regroup([in_ref[4 * column + e] for e in range(4)])
        for g, tile in enumerate(tiles):
            rows_ref[8 * g:8 * g + 8, LANES * column:LANES * (column + 1)] = tile
    for link in range(LINKS):
        window = slice(link * WINDOW, (link + 1) * WINDOW)
        cells = times(rows_ref[:, window], onehot(slots_ref[link:link + 1, :]))
        for p in range(PLANES):
            residual = cells[16 + 8 * p:16 + 8 * p + VARS] * diagonal_ref[p:p + 1, window]
            for a in range(VARS):
                solution_ref[a, p:p + 1, window] = cells[8 * p + a:8 * p + a + 1]
                residual_ref[a, p:p + 1, window] = residual[a:a + 1]


def shape(*dims):
    return jax.ShapeDtypeStruct(dims, F32)


def local(
    rhs,
    diagonal,
    lower_transfer,
    upper_transfer,
    face_owner,
    face_start,
    face_count,
    face_flip,
    block_cells,
):
    owner, start, count, flip = face_owner.T, face_start.T, face_count.T, face_flip.T
    transfer = pltpu.VMEM((VARS, VARS, PLANES, CELLS), F32)
    planes = pltpu.VMEM((PLANES, CELLS), F32)
    packed, slots = pl.pallas_call(
        pack_kernel,
        out_shape=[shape(CELLS, LANES), jax.ShapeDtypeStruct((LINKS, WINDOW), jnp.int32)],
        in_specs=[HBM] * 9,
        out_specs=[VMEM] * 2,
        scratch_shapes=[TABLE] * 4
        + [
            pltpu.SMEM((CROSS,), jnp.int32), pltpu.VMEM((VARS, PLANES, CELLS), F32), planes,
            transfer, transfer, pltpu.VMEM((LANES, CELLS), F32),
            pltpu.VMEM((LINKS, WINDOW, WINDOW), BF16), pltpu.SemaphoreType.DMA((9,)),
        ],
        compiler_params=WIDE,
        name="pack_cells",
    )(
        owner, start, count, flip,
        block_cells,
        rhs.transpose(1, 0, 2),
        diagonal,
        lower_transfer.transpose(1, 2, 0, 3),
        upper_transfer.transpose(1, 2, 0, 3),
    )
    arrived = lax.all_to_all(packed.reshape(STREAM, 32, LANES), "stream", 0, 0, tiled=True)
    arrived = arrived.reshape(CELLS, LANES)
    faces = pl.pallas_call(
        faces_kernel,
        out_shape=shape(CROSS * KEPT, LANES),
        in_specs=[VMEM],
        out_specs=VMEM,
        compiler_params=PARAMS,
        name="take_faces",
    )(arrived)
    faces = lax.all_to_all(faces.reshape(CROSS * KEPT // 4, 4, LANES), "cross", 0, 0, tiled=True)

    composed = pltpu.VMEM((VARS * VARS, CHUNKS, LANES), F32)
    results, faces = pl.pallas_call(
        solve_kernel,
        out_shape=[shape(CHUNKS * 32, LANES), shape(5 * CROSS, LANES)],
        in_specs=[HBM, HBM, VMEM, VMEM],
        out_specs=[VMEM, VMEM],
        scratch_shapes=[TABLE] * 2
        + [
            pltpu.VMEM((CHUNKS * LANES, LANES), F32), composed, composed,
            pltpu.VMEM((VARS, CHUNKS, LANES), F32),
            pltpu.VMEM((GROUPS, VARS, CHUNKS, LANES), F32),
            pltpu.VMEM((2 * LANES, LANES), F32),
            pltpu.SemaphoreType.DMA((2,)),
        ],
        compiler_params=PARAMS,
        name="solve_cells",
    )(owner, count, arrived, faces.reshape(CROSS * KEPT, LANES))
    faces = lax.all_to_all(faces.reshape(5 * CROSS, 1, LANES), "cross", 0, 0, tiled=True)
    results = pl.pallas_call(
        join_kernel,
        out_shape=shape(STREAM, 8, LANES),
        in_specs=[VMEM, VMEM],
        out_specs=VMEM,
        scratch_shapes=[pltpu.VMEM((2 * LANES, LANES), F32)],
        compiler_params=PARAMS,
        name="join_faces",
    )(results, faces.reshape(5 * CROSS, LANES))
    returned = lax.all_to_all(results, "stream", 0, 0, tiled=True)
    outs = pl.pallas_call(
        unpack_kernel,
        out_shape=[shape(VARS, PLANES, CELLS)] * 2,
        in_specs=[VMEM] * 3,
        out_specs=[VMEM] * 2,
        scratch_shapes=[pltpu.VMEM((32, CELLS), F32)],
        compiler_params=PARAMS,
        name="unpack_cells",
    )(slots, diagonal, returned)
    return tuple(x.transpose(1, 0, 2) for x in outs)


def solution(mesh):
    return jax.shard_map(
        local,
        mesh=mesh,
        in_specs=(
            P("stream", None, "cross"),
            P("stream", "cross"),
            P("stream", None, None, "cross"),
            P("stream", None, None, "cross"),
            P(),
            P(),
            P(),
            P(),
            P(),
        ),
        out_specs=(P("stream", None, "cross"), P("stream", None, "cross")),
        check_vma=False,
    )
```

```python
import functools

import jax
import jax.numpy as jnp
from jax import lax
from jax.experimental import pallas as pl
from jax.experimental.pallas import tpu as pltpu
from jax.sharding import PartitionSpec as P

VARS = 5
CELLS = 1024
LINKS = 4
WINDOW = CELLS // LINKS
STREAM = 32
CROSS = 16
PLANES = 2
CHUNKS = 8
GROUPS = 4
LANES = 128
FACE_WEIGHT = 0.25

LOWER = 0
UPPER = 25
SOURCE = 50
ROWS = 110
KEPT = 28
PIECES = 7

F32 = jnp.float32
BF16 = jnp.bfloat16
HBM = pl.BlockSpec(memory_space=pltpu.HBM)
SMEM = pl.BlockSpec(memory_space=pltpu.SMEM)
VMEM = pl.BlockSpec(memory_space=pltpu.VMEM)
PARAMS = pltpu.CompilerParams(vmem_limit_bytes=24 * 1024 * 1024)
TABLE = pltpu.SMEM((LINKS, CROSS), jnp.int32)


def thirds(x):
    high = x.astype(BF16)
    rest = x - high.astype(F32)
    middle = rest.astype(BF16)
    low = (rest - middle.astype(F32)).astype(BF16)
    return jnp.concatenate([high, middle, low], axis=0)


def times(x, matrix):
    n = x.shape[0]
    parts = jnp.dot(thirds(x), matrix, preferred_element_type=F32)
    return (parts[2 * n:] + parts[n:2 * n]) + parts[:n]


def copy_in(pairs, sems):
    copies = [pltpu.make_async_copy(src, dst, sems.at[i]) for i, (src, dst) in enumerate(pairs)]
    for copy in copies:
        copy.start()
    return copies


def slots_of(own, link, owner_ref, start_ref, count_ref, flip_ref):
    owner = owner_ref[link, own]
    count = count_ref[link, own]
    turned = jnp.logical_and(flip_ref[link, own] == 1, own > owner)
    bound = jnp.where(turned, count, 0)
    offset = start_ref[link, own] - link * WINDOW
    cell = lax.broadcasted_iota(jnp.int32, (1, WINDOW), 1)
    place = (cell - offset) & (WINDOW - 1)
    place = jnp.where(place < bound, count - 1 - place, place)
    rest = place & 127
    return ((rest >> 4) << 5) + ((place >> 7) << 4) + (rest & 15)


def onehot(row):
    rows = lax.broadcasted_iota(jnp.int32, (WINDOW, WINDOW), 0)
    return jnp.where(rows == row, 1.0, 0.0).astype(BF16)


def pack_kernel(
    owner_in, start_in, count_in, flip_in, live_in, rhs_in, diagonal_in, lower_in, upper_in,
    out_ref, matrix_ref,
    owner_ref, start_ref, count_ref, flip_ref, live_ref, rhs_ref, diagonal_ref, lower_ref, upper_ref,
    rows_ref, sems,
):
    copies = copy_in(
        [
            (owner_in, owner_ref), (start_in, start_ref), (count_in, count_ref),
            (flip_in, flip_ref), (live_in, live_ref), (rhs_in, rhs_ref),
            (diagonal_in, diagonal_ref), (lower_in, lower_ref), (upper_in, upper_ref),
        ],
        sems,
    )
    own = lax.axis_index("cross")
    rows_ref[pl.ds(ROWS, LANES - ROWS), :] = jnp.zeros((LANES - ROWS, CELLS), F32)
    for copy in copies[:5]:
        copy.wait()
    for link in range(LINKS):
        matrix_ref[link] = onehot(slots_of(own, link, owner_ref, start_ref, count_ref, flip_ref))
    for copy in copies[5:]:
        copy.wait()
    cell = lax.broadcasted_iota(jnp.int32, (PLANES, CELLS), 1)
    live = cell < live_ref[own]
    for a in range(VARS):
        for b in range(VARS):
            at = VARS * a + b
            rows_ref[pl.ds(2 * (LOWER + at), 2), :] = lower_ref[a, b]
            rows_ref[pl.ds(2 * (UPPER + at), 2), :] = upper_ref[a, b]
        source = jnp.where(live, rhs_ref[a], 0.0) / diagonal_ref[...]
        rows_ref[pl.ds(2 * (SOURCE + a), 2), :] = source
    for link in range(LINKS):
        parts = lax.dot_general(
            matrix_ref[link],
            thirds(rows_ref[:, link * WINDOW:(link + 1) * WINDOW]),
            (((1,), (1,)), ((), ())),
            preferred_element_type=F32,
        )
        out_ref[link * WINDOW:(link + 1) * WINDOW, :] = (
            parts[:, 2 * LANES:] + parts[:, LANES:2 * LANES]
        ) + parts[:, :LANES]


def total(rows, first=None):
    if first is None:
        return [(t[0] + t[1]) + (t[2] + t[3]) + t[4] for t in rows]
    return [((x + t[0]) + (t[1] + t[2])) + (t[3] + t[4]) for x, t in zip(first, rows)]


def entry(system_ref, at, p):
    row = 8 * (2 * at + p)
    return system_ref[row:row + 8, :]


def apply(system_ref, at, p, x, first=None):
    return total(
        [[entry(system_ref, at + VARS * a + b, p) * x[b] for b in range(VARS)] for a in range(VARS)],
        first,
    )


def compose(system_ref, at, later, earlier, out_ref):
    for c in range(VARS):
        column = [entry(system_ref, at + VARS * b + c, earlier) for b in range(VARS)]
        for a, x in enumerate(apply(system_ref, at, later, column)):
            out_ref[VARS * a + c] = x


def relay(matrix_ref, offset, offset_ref, state_ref, up):
    for a in range(VARS):
        offset_ref[a] = offset[a]
    state = [jnp.zeros((1, LANES), F32) for _ in range(VARS)]
    groups = range(GROUPS) if up else range(GROUPS - 1, -1, -1)
    chunks = range(CHUNKS) if up else range(CHUNKS - 1, -1, -1)
    for group in groups:
        if group != groups[0]:
            state = [pltpu.roll(x, 32 if up else 96, 1) for x in state]
        for k in chunks:
            row = slice(k, k + 1)
            for a in range(VARS):
                state_ref[group, a, row, :] = state[a]
            state = total(
                [
                    [matrix_ref[VARS * a + b, row, :] * state[b] for b in range(VARS)]
                    for a in range(VARS)
                ],
                [offset_ref[a, row, :] for a in range(VARS)],
            )
    lane = lax.broadcasted_iota(jnp.int32, (CHUNKS, LANES), 1) >> 5
    out = []
    for a in range(VARS):
        x = state_ref[GROUPS - 1, a]
        for group in range(GROUPS - 1):
            x = jnp.where(lane == group, state_ref[group, a], x)
        out.append(x)
    return out


def plus(x, y):
    return [a + b for a, b in zip(x, y)]


def face_matrix(owner_ref, count_ref):
    position = lax.axis_index("stream")
    link = position >> 3
    slot = ((position & 7) << 4) + lax.axis_index("cross")
    lane = lax.broadcasted_iota(jnp.int32, (1, LANES), 1)
    source = jnp.full((1, LANES), -1, jnp.int32)
    for block in range(CROSS):
        taken = jnp.where(slot < count_ref[link, block], owner_ref[link, block], -LANES)
        source = jnp.where((lane & 31) == block, (lane & 96) + taken, source)
    rows = lax.broadcasted_iota(jnp.int32, (LANES, LANES), 0)
    return jnp.where(rows == source, FACE_WEIGHT, 0.0).astype(BF16)


def faces_kernel(in_ref, out_ref):
    lane = lax.broadcasted_iota(jnp.int32, (CROSS, LANES), 1)
    for row in range(KEPT):
        piece = row % PIECES
        first = 32 * (KEPT + row // PIECES)
        spare = pltpu.roll(in_ref[first:first + CROSS, :], ROWS - 16 * piece, 1)
        own = in_ref[32 * row:32 * row + CROSS, :]
        out_ref[pl.ds(row, CROSS, stride=KEPT), :] = jnp.where(lane < ROWS, own, spare)


def face_rows(face_ref, chunk):
    if chunk < KEPT:
        return face_ref[pl.ds(chunk, CROSS, stride=KEPT), :]
    piece_of = lax.broadcasted_iota(jnp.int32, (CROSS, LANES), 1) >> 4
    out = jnp.zeros((CROSS, LANES), F32)
    for piece in range(PIECES):
        row = PIECES * (chunk - KEPT) + piece
        moved = pltpu.roll(
            face_ref[pl.ds(row, CROSS, stride=KEPT), :], LANES - ROWS + 16 * piece, 1
        )
        out = jnp.where(piece_of == piece, moved, out)
    return out


def solve_kernel(
    owner_in, count_in, in_ref, face_ref, out_ref, send_ref,
    owner_ref, count_ref, system_ref, lower_ref, upper_ref, offset_ref, state_ref, values_ref, sems,
):
    copies = copy_in([(owner_in, owner_ref), (count_in, count_ref)], sems)
    values_ref[160:, :] = jnp.zeros((96, LANES), F32)
    for k in range(CHUNKS):
        parts = []
        for group in range(GROUPS):
            chunk = CHUNKS * group + k
            parts += [face_rows(face_ref, chunk), in_ref[32 * chunk + 16:32 * chunk + 32, :]]
        system_ref[pl.ds(k, LANES, stride=CHUNKS), :] = jnp.concatenate(parts, axis=0).T
    for copy in copies:
        copy.wait()
    matrix = face_matrix(owner_ref, count_ref)
    lower = functools.partial(apply, system_ref, LOWER)
    upper = functools.partial(apply, system_ref, UPPER)
    compose(system_ref, LOWER, 1, 0, lower_ref)
    compose(system_ref, UPPER, 0, 1, upper_ref)

    def upper_sweep(lowered):
        offset = upper(0, lowered[1], lowered[0])
        after = relay(upper_ref, offset, offset_ref, state_ref, False)
        coupled_1 = upper(1, after)
        delta_1 = plus(lowered[1], coupled_1)
        coupled_0 = upper(0, delta_1)
        return [coupled_0, coupled_1], [plus(lowered[0], coupled_0), delta_1]

    def faces_of(delta):
        parts = times(jnp.concatenate(delta[0] + delta[1], axis=0), matrix)
        rows = [parts[CHUNKS * i:CHUNKS * (i + 1)] for i in range(2 * VARS)]
        return [rows[:VARS], rows[VARS:]]

    source = [[entry(system_ref, SOURCE + a, p) for a in range(VARS)] for p in range(PLANES)]
    before = relay(lower_ref, lower(1, source[0], source[1]), offset_ref, state_ref, True)
    lowered_0 = lower(0, before, source[0])
    lowered_1 = lower(1, lowered_0, source[1])
    coupled, first = upper_sweep([lowered_0, lowered_1])

    faces = faces_of(first)
    joint_0 = plus(faces[0], coupled[0])
    joint_1 = plus(faces[1], coupled[1])
    before = relay(lower_ref, lower(1, joint_0, joint_1), offset_ref, state_ref, True)
    along = lower(0, before)
    lowered_1 = lower(1, plus(joint_0, along), faces[1])
    coupled, second = upper_sweep([plus(faces[0], along), lowered_1])

    faces = faces_of(second)
    row = lax.broadcasted_iota(jnp.int32, (CHUNKS, LANES), 0)
    lane = lax.broadcasted_iota(jnp.int32, (CHUNKS, LANES), 1)
    previous = []
    for x in coupled[1]:
        x = pltpu.roll(x, 1, 0)
        x = jnp.where(row == 0, jnp.where(lane < 32, 0.0, pltpu.roll(x, 32, 1)), x)
        previous.append(x)
    results = [
        plus(first[0], second[0]),
        plus(first[1], second[1]),
        lower(0, previous, faces[0]),
        lower(1, coupled[0], faces[1]),
    ]
    for g in range(4):
        for a in range(VARS):
            out_ref[pl.ds(8 * g + a, CHUNKS, stride=32), :] = results[g][a]
            values_ref[pl.ds(5 * g + a, CHUNKS, stride=20), :] = results[g][a]
    turned = values_ref[0:LANES, :].T
    others = values_ref[LANES:2 * LANES, :].T
    lane_group = lax.broadcasted_iota(jnp.int32, (CROSS, LANES), 1) >> 5
    fifth = others[0:CROSS]
    for group in range(GROUPS):
        rows = slice(32 * group, 32 * group + CROSS)
        send_ref[pl.ds(group, CROSS, stride=5), :] = turned[rows]
        if group:
            fifth = jnp.where(lane_group == group, pltpu.roll(others[rows], 32 * group, 1), fifth)
    send_ref[pl.ds(4, CROSS, stride=5), :] = fifth


def regroup(parts):
    lane = lax.broadcasted_iota(jnp.int32, parts[0].shape, 1)
    first_half = lane < 64
    even = (lane & 32) == 0
    half = [None] * 4
    for i in range(2):
        x, y = parts[i], parts[i + 2]
        half[i] = jnp.where(first_half, x, pltpu.roll(y, 64, 1))
        half[i + 2] = jnp.where(first_half, pltpu.roll(x, 64, 1), y)
    out = [None] * 4
    for i in (0, 2):
        x, y = half[i], half[i + 1]
        out[i] = jnp.where(even, x, pltpu.roll(y, 32, 1))
        out[i + 1] = jnp.where(even, pltpu.roll(x, 96, 1), y)
    return out


def join_kernel(in_ref, face_ref, out_ref, values_ref):
    lane = lax.broadcasted_iota(jnp.int32, (8, LANES), 1)
    returned = (lane & 16) == 0
    blank = jnp.zeros((16, LANES), F32)
    fifth = face_ref[pl.ds(4, CROSS, stride=5), :]
    parts = []
    others = []
    for group in range(GROUPS):
        parts += [face_ref[pl.ds(group, CROSS, stride=5), :], blank]
        others += [pltpu.roll(fifth, (LANES - 32 * group) % LANES, 1) if group else fifth, blank]
    values_ref[0:LANES, :] = jnp.concatenate(parts, axis=0).T
    values_ref[LANES:2 * LANES, :] = jnp.concatenate(others, axis=0).T
    for k in range(CHUNKS):
        tiles = []
        for g in range(4):
            at = 5 * (4 * k + g)
            tiles.append(jnp.where(returned, values_ref[at:at + 8, :], in_ref[32 * k + 8 * g:32 * k + 8 * g + 8, :]))
        for group, tile in enumerate(regroup(tiles)):
            out_ref[CHUNKS * group + k] = tile


def unpack_kernel(matrix_ref, diagonal_ref, in_ref, solution_ref, residual_ref, rows_ref):
    for column in range(8):
        tiles = regroup([in_ref[4 * column + e] for e in range(4)])
        for g, tile in enumerate(tiles):
            rows_ref[8 * g:8 * g + 8, LANES * column:LANES * (column + 1)] = tile
    for link in range(LINKS):
        window = slice(link * WINDOW, (link + 1) * WINDOW)
        cells = times(rows_ref[:, window], matrix_ref[link])
        for p in range(PLANES):
            residual = cells[16 + 8 * p:16 + 8 * p + VARS] * diagonal_ref[p:p + 1, window]
            for a in range(VARS):
                solution_ref[a, p:p + 1, window] = cells[8 * p + a:8 * p + a + 1]
                residual_ref[a, p:p + 1, window] = residual[a:a + 1]


def shape(*dims):
    return jax.ShapeDtypeStruct(dims, F32)


def local(
    rhs,
    diagonal,
    lower_transfer,
    upper_transfer,
    face_owner,
    face_start,
    face_count,
    face_flip,
    block_cells,
):
    owner, start, count, flip = face_owner.T, face_start.T, face_count.T, face_flip.T
    transfer = pltpu.VMEM((VARS, VARS, PLANES, CELLS), F32)
    planes = pltpu.VMEM((PLANES, CELLS), F32)
    in_hbm = functools.partial(pltpu.with_memory_space_constraint, memory_space=pltpu.HBM)
    packed, matrix = pl.pallas_call(
        pack_kernel,
        out_shape=[shape(CELLS, LANES), jax.ShapeDtypeStruct((LINKS, WINDOW, WINDOW), BF16)],
        in_specs=[HBM] * 9,
        out_specs=[VMEM] * 2,
        scratch_shapes=[TABLE] * 4
        + [
            pltpu.SMEM((CROSS,), jnp.int32), pltpu.VMEM((VARS, PLANES, CELLS), F32), planes,
            transfer, transfer, pltpu.VMEM((LANES, CELLS), F32), pltpu.SemaphoreType.DMA((9,)),
        ],
        compiler_params=PARAMS,
        name="pack_cells",
    )(
        *[
            in_hbm(x)
            for x in (
                owner, start, count, flip,
                block_cells,
                rhs.transpose(1, 0, 2),
                diagonal,
                lower_transfer.transpose(1, 2, 0, 3),
                upper_transfer.transpose(1, 2, 0, 3),
            )
        ]
    )
    arrived = lax.all_to_all(packed.reshape(STREAM, 32, LANES), "stream", 0, 0, tiled=True)
    arrived = arrived.reshape(CELLS, LANES)
    faces = pl.pallas_call(
        faces_kernel,
        out_shape=shape(CROSS * KEPT, LANES),
        in_specs=[VMEM],
        out_specs=VMEM,
        compiler_params=PARAMS,
        name="take_faces",
    )(arrived)
    faces = lax.all_to_all(faces.reshape(CROSS * KEPT // 4, 4, LANES), "cross", 0, 0, tiled=True)

    composed = pltpu.VMEM((VARS * VARS, CHUNKS, LANES), F32)
    results, faces = pl.pallas_call(
        solve_kernel,
        out_shape=[shape(CHUNKS * 32, LANES), shape(5 * CROSS, LANES)],
        in_specs=[HBM, HBM, VMEM, VMEM],
        out_specs=[VMEM, VMEM],
        scratch_shapes=[TABLE] * 2
        + [
            pltpu.VMEM((CHUNKS * LANES, LANES), F32), composed, composed,
            pltpu.VMEM((VARS, CHUNKS, LANES), F32),
            pltpu.VMEM((GROUPS, VARS, CHUNKS, LANES), F32),
            pltpu.VMEM((2 * LANES, LANES), F32),
            pltpu.SemaphoreType.DMA((2,)),
        ],
        compiler_params=PARAMS,
        name="solve_cells",
    )(owner, count, arrived, faces.reshape(CROSS * KEPT, LANES))
    faces = lax.all_to_all(faces.reshape(5 * CROSS, 1, LANES), "cross", 0, 0, tiled=True)
    results = pl.pallas_call(
        join_kernel,
        out_shape=shape(STREAM, 8, LANES),
        in_specs=[VMEM, VMEM],
        out_specs=VMEM,
        scratch_shapes=[pltpu.VMEM((2 * LANES, LANES), F32)],
        compiler_params=PARAMS,
        name="join_faces",
    )(results, faces.reshape(5 * CROSS, LANES))
    returned = lax.all_to_all(results, "stream", 0, 0, tiled=True)
    outs = pl.pallas_call(
        unpack_kernel,
        out_shape=[shape(VARS, PLANES, CELLS)] * 2,
        in_specs=[VMEM] * 3,
        out_specs=[VMEM] * 2,
        scratch_shapes=[pltpu.VMEM((32, CELLS), F32)],
        compiler_params=PARAMS,
        name="unpack_cells",
    )(matrix, diagonal, returned)
    return tuple(x.transpose(1, 0, 2) for x in outs)


def solution(mesh):
    return jax.shard_map(
        local,
        mesh=mesh,
        in_specs=(
            P("stream", None, "cross"),
            P("stream", "cross"),
            P("stream", None, None, "cross"),
            P("stream", None, None, "cross"),
            P(),
            P(),
            P(),
            P(),
            P(),
        ),
        out_specs=(P("stream", None, "cross"), P("stream", None, "cross")),
        check_vma=False,
    )
```

```python
import functools

import jax
import jax.numpy as jnp
from jax import lax
from jax.experimental import pallas as pl
from jax.experimental.pallas import tpu as pltpu
from jax.sharding import PartitionSpec as P

VARS = 5
CELLS = 1024
LINKS = 4
WINDOW = CELLS // LINKS
STREAM = 32
CROSS = 16
PLANES = 2
CHUNKS = 8
GROUPS = 4
LANES = 128
FACE_WEIGHT = 0.25

LOWER = 0
UPPER = 25
SOURCE = 50
ROWS = 110
KEPT = 28
PIECES = 7

F32 = jnp.float32
BF16 = jnp.bfloat16
HBM = pl.BlockSpec(memory_space=pltpu.HBM)
SMEM = pl.BlockSpec(memory_space=pltpu.SMEM)
VMEM = pl.BlockSpec(memory_space=pltpu.VMEM)
PARAMS = pltpu.CompilerParams(vmem_limit_bytes=24 * 1024 * 1024)
TABLE = pltpu.SMEM((LINKS, CROSS), jnp.int32)


def thirds(x):
    high = x.astype(BF16)
    rest = x - high.astype(F32)
    middle = rest.astype(BF16)
    low = (rest - middle.astype(F32)).astype(BF16)
    return jnp.concatenate([high, middle, low], axis=0)


def times(x, matrix):
    n = x.shape[0]
    parts = jnp.dot(thirds(x), matrix, preferred_element_type=F32)
    return (parts[2 * n:] + parts[n:2 * n]) + parts[:n]


def copy_in(pairs, sems):
    copies = [pltpu.make_async_copy(src, dst, sems.at[i]) for i, (src, dst) in enumerate(pairs)]
    for copy in copies:
        copy.start()
    return copies


def slots_of(own, link, owner_ref, start_ref, count_ref, flip_ref):
    owner = owner_ref[link, own]
    count = count_ref[link, own]
    turned = jnp.logical_and(flip_ref[link, own] == 1, own > owner)
    bound = jnp.where(turned, count, 0)
    offset = start_ref[link, own] - link * WINDOW
    cell = lax.broadcasted_iota(jnp.int32, (1, WINDOW), 1)
    place = (cell - offset) & (WINDOW - 1)
    place = jnp.where(place < bound, count - 1 - place, place)
    rest = place & 127
    return ((rest >> 4) << 5) + ((place >> 7) << 4) + (rest & 15)


def onehot(row):
    rows = lax.broadcasted_iota(jnp.int32, (WINDOW, WINDOW), 0)
    return jnp.where(rows == row, 1.0, 0.0).astype(BF16)


def pack_kernel(
    owner_in, start_in, count_in, flip_in, live_in, rhs_in, diagonal_in, lower_in, upper_in,
    out_ref, matrix_ref,
    owner_ref, start_ref, count_ref, flip_ref, live_ref, rhs_ref, diagonal_ref, lower_ref, upper_ref,
    rows_ref, sems,
):
    copies = copy_in(
        [
            (owner_in, owner_ref), (start_in, start_ref), (count_in, count_ref),
            (flip_in, flip_ref), (live_in, live_ref), (rhs_in, rhs_ref),
            (diagonal_in, diagonal_ref), (lower_in, lower_ref), (upper_in, upper_ref),
        ],
        sems,
    )
    own = lax.axis_index("cross")
    rows_ref[pl.ds(ROWS, LANES - ROWS), :] = jnp.zeros((LANES - ROWS, CELLS), F32)
    for copy in copies[:5]:
        copy.wait()
    for link in range(LINKS):
        matrix_ref[link] = onehot(slots_of(own, link, owner_ref, start_ref, count_ref, flip_ref))
    for copy in copies[5:]:
        copy.wait()
    cell = lax.broadcasted_iota(jnp.int32, (PLANES, CELLS), 1)
    live = cell < live_ref[own]
    for a in range(VARS):
        for b in range(VARS):
            at = VARS * a + b
            rows_ref[pl.ds(2 * (LOWER + at), 2), :] = lower_ref[a, b]
            rows_ref[pl.ds(2 * (UPPER + at), 2), :] = upper_ref[a, b]
        source = jnp.where(live, rhs_ref[a], 0.0) / diagonal_ref[...]
        rows_ref[pl.ds(2 * (SOURCE + a), 2), :] = source
    for link in range(LINKS):
        parts = lax.dot_general(
            matrix_ref[link],
            thirds(rows_ref[:, link * WINDOW:(link + 1) * WINDOW]),
            (((1,), (1,)), ((), ())),
            preferred_element_type=F32,
        )
        out_ref[link * WINDOW:(link + 1) * WINDOW, :] = (
            parts[:, 2 * LANES:] + parts[:, LANES:2 * LANES]
        ) + parts[:, :LANES]


def total(rows, first=None):
    if first is None:
        return [(t[0] + t[1]) + (t[2] + t[3]) + t[4] for t in rows]
    return [((x + t[0]) + (t[1] + t[2])) + (t[3] + t[4]) for x, t in zip(first, rows)]


def entry(system_ref, at, p):
    row = 8 * (2 * at + p)
    return system_ref[row:row + 8, :]


def apply(system_ref, at, p, x, first=None):
    return total(
        [[entry(system_ref, at + VARS * a + b, p) * x[b] for b in range(VARS)] for a in range(VARS)],
        first,
    )


def compose(system_ref, at, later, earlier, out_ref):
    for c in range(VARS):
        column = [entry(system_ref, at + VARS * b + c, earlier) for b in range(VARS)]
        for a, x in enumerate(apply(system_ref, at, later, column)):
            out_ref[VARS * a + c] = x


def relay(matrix_ref, offset, offset_ref, state_ref, up):
    for a in range(VARS):
        offset_ref[a] = offset[a]
    state = [jnp.zeros((1, LANES), F32) for _ in range(VARS)]
    groups = range(GROUPS) if up else range(GROUPS - 1, -1, -1)
    chunks = range(CHUNKS) if up else range(CHUNKS - 1, -1, -1)
    for group in groups:
        if group != groups[0]:
            state = [pltpu.roll(x, 32 if up else 96, 1) for x in state]
        for k in chunks:
            row = slice(k, k + 1)
            for a in range(VARS):
                state_ref[group, a, row, :] = state[a]
            state = total(
                [
                    [matrix_ref[VARS * a + b, row, :] * state[b] for b in range(VARS)]
                    for a in range(VARS)
                ],
                [offset_ref[a, row, :] for a in range(VARS)],
            )
    lane = lax.broadcasted_iota(jnp.int32, (CHUNKS, LANES), 1) >> 5
    out = []
    for a in range(VARS):
        x = state_ref[GROUPS - 1, a]
        for group in range(GROUPS - 1):
            x = jnp.where(lane == group, state_ref[group, a], x)
        out.append(x)
    return out


def plus(x, y):
    return [a + b for a, b in zip(x, y)]


def face_matrix(owner_ref, count_ref):
    position = lax.axis_index("stream")
    link = position >> 3
    slot = ((position & 7) << 4) + lax.axis_index("cross")
    lane = lax.broadcasted_iota(jnp.int32, (1, LANES), 1)
    source = jnp.full((1, LANES), -1, jnp.int32)
    for block in range(CROSS):
        taken = jnp.where(slot < count_ref[link, block], owner_ref[link, block], -LANES)
        source = jnp.where((lane & 31) == block, (lane & 96) + taken, source)
    rows = lax.broadcasted_iota(jnp.int32, (LANES, LANES), 0)
    return jnp.where(rows == source, FACE_WEIGHT, 0.0).astype(BF16)


def faces_kernel(in_ref, out_ref):
    lane = lax.broadcasted_iota(jnp.int32, (CROSS, LANES), 1)
    for row in range(KEPT):
        piece = row % PIECES
        first = 32 * (KEPT + row // PIECES)
        spare = pltpu.roll(in_ref[first:first + CROSS, :], ROWS - 16 * piece, 1)
        own = in_ref[32 * row:32 * row + CROSS, :]
        out_ref[pl.ds(row, CROSS, stride=KEPT), :] = jnp.where(lane < ROWS, own, spare)


def gather_faces(face_ref, rows_ref):
    piece_of = lax.broadcasted_iota(jnp.int32, (CROSS, LANES), 1) >> 4
    for chunk in range(KEPT, STREAM):
        last = jnp.zeros((CROSS, LANES), F32)
        for piece in range(PIECES):
            row = PIECES * (chunk - KEPT) + piece
            found = face_ref[pl.ds(row, CROSS, stride=KEPT), :]
            rows_ref[CROSS * row:CROSS * (row + 1), :] = found
            moved = pltpu.roll(found, LANES - ROWS + 16 * piece, 1)
            last = jnp.where(piece_of == piece, moved, last)
        rows_ref[CROSS * chunk:CROSS * (chunk + 1), :] = last


def solve_kernel(
    owner_in, count_in, in_ref, face_ref, out_ref, send_ref,
    owner_ref, count_ref, rows_ref, system_ref, lower_ref, upper_ref, offset_ref, state_ref, values_ref, sems,
):
    copies = copy_in([(owner_in, owner_ref), (count_in, count_ref)], sems)
    values_ref[160:, :] = jnp.zeros((96, LANES), F32)
    gather_faces(face_ref, rows_ref)
    for k in range(CHUNKS):
        parts = []
        for group in range(GROUPS):
            chunk = CHUNKS * group + k
            parts += [
                rows_ref[CROSS * chunk:CROSS * (chunk + 1), :],
                in_ref[32 * chunk + 16:32 * chunk + 32, :],
            ]
        system_ref[pl.ds(k, LANES, stride=CHUNKS), :] = jnp.concatenate(parts, axis=0).T
    for copy in copies:
        copy.wait()
    matrix = face_matrix(owner_ref, count_ref)
    lower = functools.partial(apply, system_ref, LOWER)
    upper = functools.partial(apply, system_ref, UPPER)
    compose(system_ref, LOWER, 1, 0, lower_ref)
    compose(system_ref, UPPER, 0, 1, upper_ref)

    def upper_sweep(lowered):
        offset = upper(0, lowered[1], lowered[0])
        after = relay(upper_ref, offset, offset_ref, state_ref, False)
        coupled_1 = upper(1, after)
        delta_1 = plus(lowered[1], coupled_1)
        coupled_0 = upper(0, delta_1)
        return [coupled_0, coupled_1], [plus(lowered[0], coupled_0), delta_1]

    def faces_of(delta):
        parts = times(jnp.concatenate(delta[0] + delta[1], axis=0), matrix)
        rows = [parts[CHUNKS * i:CHUNKS * (i + 1)] for i in range(2 * VARS)]
        return [rows[:VARS], rows[VARS:]]

    source = [[entry(system_ref, SOURCE + a, p) for a in range(VARS)] for p in range(PLANES)]
    before = relay(lower_ref, lower(1, source[0], source[1]), offset_ref, state_ref, True)
    lowered_0 = lower(0, before, source[0])
    lowered_1 = lower(1, lowered_0, source[1])
    coupled, first = upper_sweep([lowered_0, lowered_1])

    faces = faces_of(first)
    joint_0 = plus(faces[0], coupled[0])
    joint_1 = plus(faces[1], coupled[1])
    before = relay(lower_ref, lower(1, joint_0, joint_1), offset_ref, state_ref, True)
    along = lower(0, before)
    lowered_1 = lower(1, plus(joint_0, along), faces[1])
    coupled, second = upper_sweep([plus(faces[0], along), lowered_1])

    faces = faces_of(second)
    row = lax.broadcasted_iota(jnp.int32, (CHUNKS, LANES), 0)
    lane = lax.broadcasted_iota(jnp.int32, (CHUNKS, LANES), 1)
    previous = []
    for x in coupled[1]:
        x = pltpu.roll(x, 1, 0)
        x = jnp.where(row == 0, jnp.where(lane < 32, 0.0, pltpu.roll(x, 32, 1)), x)
        previous.append(x)
    results = [
        plus(first[0], second[0]),
        plus(first[1], second[1]),
        lower(0, previous, faces[0]),
        lower(1, coupled[0], faces[1]),
    ]
    for g in range(4):
        for a in range(VARS):
            at = CHUNKS * (VARS * g + a)
            out_ref[at:at + CHUNKS, :] = results[g][a]
            values_ref[at:at + CHUNKS, :] = results[g][a]
    turned = values_ref[0:LANES, :].T
    others = values_ref[LANES:2 * LANES, :].T
    lane_group = lax.broadcasted_iota(jnp.int32, (CROSS, LANES), 1) >> 5
    fifth = others[0:CROSS]
    for group in range(GROUPS):
        rows = slice(32 * group, 32 * group + CROSS)
        send_ref[pl.ds(group, CROSS, stride=5), :] = turned[rows]
        if group:
            fifth = jnp.where(lane_group == group, pltpu.roll(others[rows], 32 * group, 1), fifth)
    send_ref[pl.ds(4, CROSS, stride=5), :] = fifth


def regroup(parts):
    lane = lax.broadcasted_iota(jnp.int32, parts[0].shape, 1)
    first_half = lane < 64
    even = (lane & 32) == 0
    half = [None] * 4
    for i in range(2):
        x, y = parts[i], parts[i + 2]
        half[i] = jnp.where(first_half, x, pltpu.roll(y, 64, 1))
        half[i + 2] = jnp.where(first_half, pltpu.roll(x, 64, 1), y)
    out = [None] * 4
    for i in (0, 2):
        x, y = half[i], half[i + 1]
        out[i] = jnp.where(even, x, pltpu.roll(y, 32, 1))
        out[i + 1] = jnp.where(even, pltpu.roll(x, 96, 1), y)
    return out


def join_kernel(in_ref, face_ref, out_ref, values_ref):
    lane = lax.broadcasted_iota(jnp.int32, (8, LANES), 1)
    returned = (lane & 16) == 0
    blank = jnp.zeros((16, LANES), F32)
    fifth = face_ref[pl.ds(4, CROSS, stride=5), :]
    parts = []
    others = []
    for group in range(GROUPS):
        parts += [face_ref[pl.ds(group, CROSS, stride=5), :], blank]
        others += [pltpu.roll(fifth, (LANES - 32 * group) % LANES, 1) if group else fifth, blank]
    values_ref[0:LANES, :] = jnp.concatenate(parts, axis=0).T
    values_ref[LANES:2 * LANES, :] = jnp.concatenate(others, axis=0).T
    for a in range(VARS):
        tiles = []
        for g in range(4):
            at = CHUNKS * (VARS * g + a)
            rows = slice(at, at + CHUNKS)
            tiles.append(jnp.where(returned, values_ref[rows, :], in_ref[rows, :]))
        for group, tile in enumerate(regroup(tiles)):
            out_ref[pl.ds(VARS * CHUNKS * group + a, CHUNKS, stride=VARS), :] = tile


def unpack_kernel(matrix_ref, diagonal_ref, in_ref, solution_ref, residual_ref, rows_ref):
    for column in range(8):
        tiles = regroup(
            [in_ref[VARS * (4 * column + e):VARS * (4 * column + e + 1), :] for e in range(4)]
        )
        for g, tile in enumerate(tiles):
            rows_ref[8 * g:8 * g + VARS, LANES * column:LANES * (column + 1)] = tile
    for link in range(LINKS):
        window = slice(link * WINDOW, (link + 1) * WINDOW)
        cells = times(rows_ref[:, window], matrix_ref[link])
        for p in range(PLANES):
            residual = cells[16 + 8 * p:16 + 8 * p + VARS] * diagonal_ref[p:p + 1, window]
            for a in range(VARS):
                solution_ref[a, p:p + 1, window] = cells[8 * p + a:8 * p + a + 1]
                residual_ref[a, p:p + 1, window] = residual[a:a + 1]


def shape(*dims):
    return jax.ShapeDtypeStruct(dims, F32)


def local(
    rhs,
    diagonal,
    lower_transfer,
    upper_transfer,
    face_owner,
    face_start,
    face_count,
    face_flip,
    block_cells,
):
    owner, start, count, flip = face_owner.T, face_start.T, face_count.T, face_flip.T
    transfer = pltpu.VMEM((VARS, VARS, PLANES, CELLS), F32)
    planes = pltpu.VMEM((PLANES, CELLS), F32)
    in_hbm = functools.partial(pltpu.with_memory_space_constraint, memory_space=pltpu.HBM)
    packed, matrix = pl.pallas_call(
        pack_kernel,
        out_shape=[shape(CELLS, LANES), jax.ShapeDtypeStruct((LINKS, WINDOW, WINDOW), BF16)],
        in_specs=[HBM] * 9,
        out_specs=[VMEM] * 2,
        scratch_shapes=[TABLE] * 4
        + [
            pltpu.SMEM((CROSS,), jnp.int32), pltpu.VMEM((VARS, PLANES, CELLS), F32), planes,
            transfer, transfer, pltpu.VMEM((LANES, CELLS), F32), pltpu.SemaphoreType.DMA((9,)),
        ],
        compiler_params=PARAMS,
        name="pack_cells",
    )(
        *[
            in_hbm(x)
            for x in (
                owner, start, count, flip,
                block_cells,
                rhs.transpose(1, 0, 2),
                diagonal,
                lower_transfer.transpose(1, 2, 0, 3),
                upper_transfer.transpose(1, 2, 0, 3),
            )
        ]
    )
    arrived = lax.all_to_all(packed.reshape(STREAM, 32, LANES), "stream", 0, 0, tiled=True)
    arrived = arrived.reshape(CELLS, LANES)
    faces = pl.pallas_call(
        faces_kernel,
        out_shape=shape(CROSS * KEPT, LANES),
        in_specs=[VMEM],
        out_specs=VMEM,
        compiler_params=PARAMS,
        name="take_faces",
    )(arrived)
    faces = lax.all_to_all(faces.reshape(CROSS * KEPT // 4, 4, LANES), "cross", 0, 0, tiled=True)

    composed = pltpu.VMEM((VARS * VARS, CHUNKS, LANES), F32)
    results, faces = pl.pallas_call(
        solve_kernel,
        out_shape=[shape(CHUNKS * 4 * VARS, LANES), shape(5 * CROSS, LANES)],
        in_specs=[HBM, HBM, VMEM, VMEM],
        out_specs=[VMEM, VMEM],
        scratch_shapes=[TABLE] * 2
        + [
            pltpu.VMEM((CELLS // 2, LANES), F32),
            pltpu.VMEM((CHUNKS * LANES, LANES), F32), composed, composed,
            pltpu.VMEM((VARS, CHUNKS, LANES), F32),
            pltpu.VMEM((GROUPS, VARS, CHUNKS, LANES), F32),
            pltpu.VMEM((2 * LANES, LANES), F32),
            pltpu.SemaphoreType.DMA((2,)),
        ],
        compiler_params=PARAMS,
        name="solve_cells",
    )(owner, count, arrived, faces.reshape(CROSS * KEPT, LANES))
    faces = lax.all_to_all(faces.reshape(5 * CROSS, 1, LANES), "cross", 0, 0, tiled=True)
    results = pl.pallas_call(
        join_kernel,
        out_shape=shape(STREAM * VARS, LANES),
        in_specs=[VMEM, VMEM],
        out_specs=VMEM,
        scratch_shapes=[pltpu.VMEM((2 * LANES, LANES), F32)],
        compiler_params=PARAMS,
        name="join_faces",
    )(results, faces.reshape(5 * CROSS, LANES))
    returned = lax.all_to_all(
        results.reshape(STREAM * VARS, 1, LANES), "stream", 0, 0, tiled=True
    )
    outs = pl.pallas_call(
        unpack_kernel,
        out_shape=[shape(VARS, PLANES, CELLS)] * 2,
        in_specs=[VMEM] * 3,
        out_specs=[VMEM] * 2,
        scratch_shapes=[pltpu.VMEM((32, CELLS), F32)],
        compiler_params=PARAMS,
        name="unpack_cells",
    )(matrix, diagonal, returned.reshape(STREAM * VARS, LANES))
    return tuple(x.transpose(1, 0, 2) for x in outs)


def solution(mesh):
    return jax.shard_map(
        local,
        mesh=mesh,
        in_specs=(
            P("stream", None, "cross"),
            P("stream", "cross"),
            P("stream", None, None, "cross"),
            P("stream", None, None, "cross"),
            P(),
            P(),
            P(),
            P(),
            P(),
        ),
        out_specs=(P("stream", None, "cross"), P("stream", None, "cross")),
        check_vma=False,
    )
```

```python
import functools

import jax
import jax.numpy as jnp
from jax import lax
from jax.experimental import pallas as pl
from jax.experimental.pallas import tpu as pltpu
from jax.sharding import PartitionSpec as P

VARS = 5
CELLS = 1024
LINKS = 4
WINDOW = CELLS // LINKS
STREAM = 32
CROSS = 16
PLANES = 2
CHUNKS = 8
GROUPS = 4
LANES = 128
FACE_WEIGHT = 0.25

LOWER = 0
UPPER = 25
SOURCE = 50
ROWS = 110
ORDER = list(range(0, CROSS, 2)) + list(range(CROSS - 1, 0, -2))
KEPT = 28
PIECES = 7

F32 = jnp.float32
BF16 = jnp.bfloat16
HBM = pl.BlockSpec(memory_space=pltpu.HBM)
SMEM = pl.BlockSpec(memory_space=pltpu.SMEM)
VMEM = pl.BlockSpec(memory_space=pltpu.VMEM)
PARAMS = pltpu.CompilerParams(vmem_limit_bytes=24 * 1024 * 1024)
TABLE = pltpu.SMEM((LINKS, CROSS), jnp.int32)


def thirds(x):
    high = x.astype(BF16)
    rest = x - high.astype(F32)
    middle = rest.astype(BF16)
    low = (rest - middle.astype(F32)).astype(BF16)
    return jnp.concatenate([high, middle, low], axis=0)


def times(x, matrix):
    n = x.shape[0]
    parts = jnp.dot(thirds(x), matrix, preferred_element_type=F32)
    return (parts[2 * n:] + parts[n:2 * n]) + parts[:n]


def copy_in(pairs, sems):
    copies = [pltpu.make_async_copy(src, dst, sems.at[i]) for i, (src, dst) in enumerate(pairs)]
    for copy in copies:
        copy.start()
    return copies


def slots_of(own, link, owner_ref, start_ref, count_ref, flip_ref):
    owner = owner_ref[link, own]
    count = count_ref[link, own]
    turned = jnp.logical_and(flip_ref[link, own] == 1, own > owner)
    bound = jnp.where(turned, count, 0)
    offset = start_ref[link, own] - link * WINDOW
    cell = lax.broadcasted_iota(jnp.int32, (1, WINDOW), 1)
    place = (cell - offset) & (WINDOW - 1)
    place = jnp.where(place < bound, count - 1 - place, place)
    rest = place & 127
    return ((rest >> 4) << 5) + ((place >> 7) << 4) + (rest & 15)


def onehot(row):
    rows = lax.broadcasted_iota(jnp.int32, (WINDOW, WINDOW), 0)
    return jnp.where(rows == row, 1.0, 0.0).astype(BF16)


def pack_kernel(
    owner_in, start_in, count_in, flip_in, live_in, rhs_in, diagonal_in, lower_in, upper_in,
    out_ref, matrix_ref,
    owner_ref, start_ref, count_ref, flip_ref, live_ref, rhs_ref, diagonal_ref, lower_ref, upper_ref,
    rows_ref, sems,
):
    copies = copy_in(
        [
            (owner_in, owner_ref), (start_in, start_ref), (count_in, count_ref),
            (flip_in, flip_ref), (live_in, live_ref), (rhs_in, rhs_ref),
            (diagonal_in, diagonal_ref), (lower_in, lower_ref), (upper_in, upper_ref),
        ],
        sems,
    )
    own = lax.axis_index("cross")
    rows_ref[pl.ds(ROWS, LANES - ROWS), :] = jnp.zeros((LANES - ROWS, CELLS), F32)
    for copy in copies[:5]:
        copy.wait()
    for link in range(LINKS):
        matrix_ref[link] = onehot(slots_of(own, link, owner_ref, start_ref, count_ref, flip_ref))
    for copy in copies[5:]:
        copy.wait()
    cell = lax.broadcasted_iota(jnp.int32, (PLANES, CELLS), 1)
    live = cell < live_ref[own]
    for a in range(VARS):
        for b in range(VARS):
            at = VARS * a + b
            rows_ref[pl.ds(2 * (LOWER + at), 2), :] = lower_ref[a, b]
            rows_ref[pl.ds(2 * (UPPER + at), 2), :] = upper_ref[a, b]
        source = jnp.where(live, rhs_ref[a], 0.0) / diagonal_ref[...]
        rows_ref[pl.ds(2 * (SOURCE + a), 2), :] = source
    for link in range(LINKS):
        parts = lax.dot_general(
            matrix_ref[link],
            thirds(rows_ref[:, link * WINDOW:(link + 1) * WINDOW]),
            (((1,), (1,)), ((), ())),
            preferred_element_type=F32,
        )
        out_ref[link * WINDOW:(link + 1) * WINDOW, :] = (
            parts[:, 2 * LANES:] + parts[:, LANES:2 * LANES]
        ) + parts[:, :LANES]


def total(rows, first=None):
    if first is None:
        return [(t[0] + t[1]) + (t[2] + t[3]) + t[4] for t in rows]
    return [((x + t[0]) + (t[1] + t[2])) + (t[3] + t[4]) for x, t in zip(first, rows)]


def entry(system_ref, at, p):
    row = 8 * (2 * at + p)
    return system_ref[row:row + 8, :]


def apply(system_ref, at, p, x, first=None):
    return total(
        [[entry(system_ref, at + VARS * a + b, p) * x[b] for b in range(VARS)] for a in range(VARS)],
        first,
    )


def compose(system_ref, at, later, earlier, out_ref):
    for c in range(VARS):
        column = [entry(system_ref, at + VARS * b + c, earlier) for b in range(VARS)]
        for a, x in enumerate(apply(system_ref, at, later, column)):
            out_ref[VARS * a + c] = x


def relay(matrix_ref, offset, offset_ref, state_ref, up):
    for a in range(VARS):
        offset_ref[a] = offset[a]
    state = [jnp.zeros((1, LANES), F32) for _ in range(VARS)]
    groups = range(GROUPS) if up else range(GROUPS - 1, -1, -1)
    chunks = range(CHUNKS) if up else range(CHUNKS - 1, -1, -1)
    for group in groups:
        if group != groups[0]:
            state = [pltpu.roll(x, 32 if up else 96, 1) for x in state]
        for k in chunks:
            row = slice(k, k + 1)
            for a in range(VARS):
                state_ref[group, a, row, :] = state[a]
            state = total(
                [
                    [matrix_ref[VARS * a + b, row, :] * state[b] for b in range(VARS)]
                    for a in range(VARS)
                ],
                [offset_ref[a, row, :] for a in range(VARS)],
            )
    lane = lax.broadcasted_iota(jnp.int32, (CHUNKS, LANES), 1) >> 5
    out = []
    for a in range(VARS):
        x = state_ref[GROUPS - 1, a]
        for group in range(GROUPS - 1):
            x = jnp.where(lane == group, state_ref[group, a], x)
        out.append(x)
    return out


def plus(x, y):
    return [a + b for a, b in zip(x, y)]


def rank_of(block):
    return jnp.where((block & 1) == 0, block >> 1, CROSS - 1 - (block >> 1))


def face_matrix(owner_ref, count_ref):
    position = lax.axis_index("stream")
    link = position >> 3
    slot = ((position & 7) << 4) + rank_of(lax.axis_index("cross"))
    lane = lax.broadcasted_iota(jnp.int32, (1, LANES), 1)
    source = jnp.full((1, LANES), -1, jnp.int32)
    for rank, block in enumerate(ORDER):
        taken = jnp.where(
            slot < count_ref[link, block], rank_of(owner_ref[link, block]), -LANES
        )
        source = jnp.where((lane & 31) == rank, (lane & 96) + taken, source)
    rows = lax.broadcasted_iota(jnp.int32, (LANES, LANES), 0)
    return jnp.where(rows == source, FACE_WEIGHT, 0.0).astype(BF16)


def faces_kernel(in_ref, out_ref):
    lane = lax.broadcasted_iota(jnp.int32, (CROSS, LANES), 1)
    for row in range(KEPT):
        piece = row % PIECES
        first = 32 * (KEPT + row // PIECES)
        spare = pltpu.roll(in_ref[first:first + CROSS, :], ROWS - 16 * piece, 1)
        own = in_ref[32 * row:32 * row + CROSS, :]
        out_ref[pl.ds(row, CROSS, stride=KEPT), :] = jnp.where(lane < ROWS, own, spare)


def gather_faces(face_ref, rows_ref):
    piece_of = lax.broadcasted_iota(jnp.int32, (CROSS, LANES), 1) >> 4
    for chunk in range(KEPT, STREAM):
        last = jnp.zeros((CROSS, LANES), F32)
        for piece in range(PIECES):
            row = PIECES * (chunk - KEPT) + piece
            found = face_ref[pl.ds(row, CROSS, stride=KEPT), :]
            rows_ref[CROSS * row:CROSS * (row + 1), :] = found
            moved = pltpu.roll(found, LANES - ROWS + 16 * piece, 1)
            last = jnp.where(piece_of == piece, moved, last)
        rows_ref[CROSS * chunk:CROSS * (chunk + 1), :] = last


def solve_kernel(
    owner_in, count_in, in_ref, face_ref, out_ref, send_ref,
    owner_ref, count_ref, rows_ref, system_ref, lower_ref, upper_ref, offset_ref, state_ref, values_ref, sems,
):
    copies = copy_in([(owner_in, owner_ref), (count_in, count_ref)], sems)
    values_ref[160:, :] = jnp.zeros((96, LANES), F32)
    gather_faces(face_ref, rows_ref)
    for k in range(CHUNKS):
        parts = []
        for group in range(GROUPS):
            chunk = CHUNKS * group + k
            parts += [
                rows_ref[CROSS * chunk:CROSS * (chunk + 1), :],
                in_ref[32 * chunk + 16:32 * chunk + 32, :],
            ]
        system_ref[pl.ds(k, LANES, stride=CHUNKS), :] = jnp.concatenate(parts, axis=0).T
    for copy in copies:
        copy.wait()
    matrix = face_matrix(owner_ref, count_ref)
    lower = functools.partial(apply, system_ref, LOWER)
    upper = functools.partial(apply, system_ref, UPPER)
    compose(system_ref, LOWER, 1, 0, lower_ref)
    compose(system_ref, UPPER, 0, 1, upper_ref)

    def upper_sweep(lowered):
        offset = upper(0, lowered[1], lowered[0])
        after = relay(upper_ref, offset, offset_ref, state_ref, False)
        coupled_1 = upper(1, after)
        delta_1 = plus(lowered[1], coupled_1)
        coupled_0 = upper(0, delta_1)
        return [coupled_0, coupled_1], [plus(lowered[0], coupled_0), delta_1]

    def faces_of(delta):
        parts = times(jnp.concatenate(delta[0] + delta[1], axis=0), matrix)
        rows = [parts[CHUNKS * i:CHUNKS * (i + 1)] for i in range(2 * VARS)]
        return [rows[:VARS], rows[VARS:]]

    source = [[entry(system_ref, SOURCE + a, p) for a in range(VARS)] for p in range(PLANES)]
    before = relay(lower_ref, lower(1, source[0], source[1]), offset_ref, state_ref, True)
    lowered_0 = lower(0, before, source[0])
    lowered_1 = lower(1, lowered_0, source[1])
    coupled, first = upper_sweep([lowered_0, lowered_1])

    faces = faces_of(first)
    joint_0 = plus(faces[0], coupled[0])
    joint_1 = plus(faces[1], coupled[1])
    before = relay(lower_ref, lower(1, joint_0, joint_1), offset_ref, state_ref, True)
    along = lower(0, before)
    lowered_1 = lower(1, plus(joint_0, along), faces[1])
    coupled, second = upper_sweep([plus(faces[0], along), lowered_1])

    faces = faces_of(second)
    row = lax.broadcasted_iota(jnp.int32, (CHUNKS, LANES), 0)
    lane = lax.broadcasted_iota(jnp.int32, (CHUNKS, LANES), 1)
    previous = []
    for x in coupled[1]:
        x = pltpu.roll(x, 1, 0)
        x = jnp.where(row == 0, jnp.where(lane < 32, 0.0, pltpu.roll(x, 32, 1)), x)
        previous.append(x)
    results = [
        plus(first[0], second[0]),
        plus(first[1], second[1]),
        lower(0, previous, faces[0]),
        lower(1, coupled[0], faces[1]),
    ]
    for g in range(4):
        for a in range(VARS):
            at = CHUNKS * (VARS * g + a)
            out_ref[at:at + CHUNKS, :] = results[g][a]
            values_ref[at:at + CHUNKS, :] = results[g][a]
    turned = values_ref[0:LANES, :].T
    others = values_ref[LANES:2 * LANES, :].T
    lane_group = lax.broadcasted_iota(jnp.int32, (CROSS, LANES), 1) >> 5
    fifth = others[0:CROSS]
    for group in range(GROUPS):
        rows = slice(32 * group, 32 * group + CROSS)
        send_ref[pl.ds(group, CROSS, stride=5), :] = turned[rows]
        if group:
            fifth = jnp.where(lane_group == group, pltpu.roll(others[rows], 32 * group, 1), fifth)
    send_ref[pl.ds(4, CROSS, stride=5), :] = fifth


def regroup(parts):
    lane = lax.broadcasted_iota(jnp.int32, parts[0].shape, 1)
    first_half = lane < 64
    even = (lane & 32) == 0
    half = [None] * 4
    for i in range(2):
        x, y = parts[i], parts[i + 2]
        half[i] = jnp.where(first_half, x, pltpu.roll(y, 64, 1))
        half[i + 2] = jnp.where(first_half, pltpu.roll(x, 64, 1), y)
    out = [None] * 4
    for i in (0, 2):
        x, y = half[i], half[i + 1]
        out[i] = jnp.where(even, x, pltpu.roll(y, 32, 1))
        out[i + 1] = jnp.where(even, pltpu.roll(x, 96, 1), y)
    return out


def join_kernel(in_ref, face_ref, out_ref, values_ref):
    lane = lax.broadcasted_iota(jnp.int32, (8, LANES), 1)
    returned = (lane & 16) == 0
    blank = jnp.zeros((16, LANES), F32)
    fifth = face_ref[pl.ds(4, CROSS, stride=5), :]
    parts = []
    others = []
    for group in range(GROUPS):
        parts += [face_ref[pl.ds(group, CROSS, stride=5), :], blank]
        others += [pltpu.roll(fifth, (LANES - 32 * group) % LANES, 1) if group else fifth, blank]
    values_ref[0:LANES, :] = jnp.concatenate(parts, axis=0).T
    values_ref[LANES:2 * LANES, :] = jnp.concatenate(others, axis=0).T
    for a in range(VARS):
        tiles = []
        for g in range(4):
            at = CHUNKS * (VARS * g + a)
            rows = slice(at, at + CHUNKS)
            tiles.append(jnp.where(returned, values_ref[rows, :], in_ref[rows, :]))
        for group, tile in enumerate(regroup(tiles)):
            out_ref[pl.ds(VARS * CHUNKS * group + a, CHUNKS, stride=VARS), :] = tile


def unpack_kernel(matrix_ref, diagonal_ref, in_ref, solution_ref, residual_ref, rows_ref):
    for column in range(8):
        tiles = regroup(
            [in_ref[VARS * (4 * column + e):VARS * (4 * column + e + 1), :] for e in range(4)]
        )
        for g, tile in enumerate(tiles):
            rows_ref[8 * g:8 * g + VARS, LANES * column:LANES * (column + 1)] = tile
    for link in range(LINKS):
        window = slice(link * WINDOW, (link + 1) * WINDOW)
        cells = times(rows_ref[:, window], matrix_ref[link])
        for p in range(PLANES):
            residual = cells[16 + 8 * p:16 + 8 * p + VARS] * diagonal_ref[p:p + 1, window]
            for a in range(VARS):
                solution_ref[a, p:p + 1, window] = cells[8 * p + a:8 * p + a + 1]
                residual_ref[a, p:p + 1, window] = residual[a:a + 1]


def shape(*dims):
    return jax.ShapeDtypeStruct(dims, F32)


def local(
    rhs,
    diagonal,
    lower_transfer,
    upper_transfer,
    face_owner,
    face_start,
    face_count,
    face_flip,
    block_cells,
):
    owner, start, count, flip = face_owner.T, face_start.T, face_count.T, face_flip.T
    transfer = pltpu.VMEM((VARS, VARS, PLANES, CELLS), F32)
    planes = pltpu.VMEM((PLANES, CELLS), F32)
    in_hbm = functools.partial(pltpu.with_memory_space_constraint, memory_space=pltpu.HBM)
    packed, matrix = pl.pallas_call(
        pack_kernel,
        out_shape=[shape(CELLS, LANES), jax.ShapeDtypeStruct((LINKS, WINDOW, WINDOW), BF16)],
        in_specs=[HBM] * 9,
        out_specs=[VMEM] * 2,
        scratch_shapes=[TABLE] * 4
        + [
            pltpu.SMEM((CROSS,), jnp.int32), pltpu.VMEM((VARS, PLANES, CELLS), F32), planes,
            transfer, transfer, pltpu.VMEM((LANES, CELLS), F32), pltpu.SemaphoreType.DMA((9,)),
        ],
        compiler_params=PARAMS,
        name="pack_cells",
    )(
        *[
            in_hbm(x)
            for x in (
                owner, start, count, flip,
                block_cells,
                rhs.transpose(1, 0, 2),
                diagonal,
                lower_transfer.transpose(1, 2, 0, 3),
                upper_transfer.transpose(1, 2, 0, 3),
            )
        ]
    )
    arrived = lax.all_to_all(packed.reshape(STREAM, 32, LANES), "stream", 0, 0, tiled=True)
    arrived = arrived.reshape(CELLS, LANES)
    faces = pl.pallas_call(
        faces_kernel,
        out_shape=shape(CROSS * KEPT, LANES),
        in_specs=[VMEM],
        out_specs=VMEM,
        compiler_params=PARAMS,
        name="take_faces",
    )(arrived)
    faces = lax.all_to_all(faces.reshape(CROSS * KEPT // 4, 4, LANES), "cross", 0, 0, axis_index_groups=[ORDER], tiled=True)

    composed = pltpu.VMEM((VARS * VARS, CHUNKS, LANES), F32)
    results, faces = pl.pallas_call(
        solve_kernel,
        out_shape=[shape(CHUNKS * 4 * VARS, LANES), shape(5 * CROSS, LANES)],
        in_specs=[HBM, HBM, VMEM, VMEM],
        out_specs=[VMEM, VMEM],
        scratch_shapes=[TABLE] * 2
        + [
            pltpu.VMEM((CELLS // 2, LANES), F32),
            pltpu.VMEM((CHUNKS * LANES, LANES), F32), composed, composed,
            pltpu.VMEM((VARS, CHUNKS, LANES), F32),
            pltpu.VMEM((GROUPS, VARS, CHUNKS, LANES), F32),
            pltpu.VMEM((2 * LANES, LANES), F32),
            pltpu.SemaphoreType.DMA((2,)),
        ],
        compiler_params=PARAMS,
        name="solve_cells",
    )(owner, count, arrived, faces.reshape(CROSS * KEPT, LANES))
    faces = lax.all_to_all(faces.reshape(5 * CROSS, 1, LANES), "cross", 0, 0, axis_index_groups=[ORDER], tiled=True)
    results = pl.pallas_call(
        join_kernel,
        out_shape=shape(STREAM * VARS, LANES),
        in_specs=[VMEM, VMEM],
        out_specs=VMEM,
        scratch_shapes=[pltpu.VMEM((2 * LANES, LANES), F32)],
        compiler_params=PARAMS,
        name="join_faces",
    )(results, faces.reshape(5 * CROSS, LANES))
    returned = lax.all_to_all(
        results.reshape(STREAM * VARS, 1, LANES), "stream", 0, 0, tiled=True
    )
    outs = pl.pallas_call(
        unpack_kernel,
        out_shape=[shape(VARS, PLANES, CELLS)] * 2,
        in_specs=[VMEM] * 3,
        out_specs=[VMEM] * 2,
        scratch_shapes=[pltpu.VMEM((32, CELLS), F32)],
        compiler_params=PARAMS,
        name="unpack_cells",
    )(matrix, diagonal, returned.reshape(STREAM * VARS, LANES))
    return tuple(x.transpose(1, 0, 2) for x in outs)


def solution(mesh):
    return jax.shard_map(
        local,
        mesh=mesh,
        in_specs=(
            P("stream", None, "cross"),
            P("stream", "cross"),
            P("stream", None, None, "cross"),
            P("stream", None, None, "cross"),
            P(),
            P(),
            P(),
            P(),
            P(),
        ),
        out_specs=(P("stream", None, "cross"), P("stream", None, "cross")),
        check_vma=False,
    )
```

```python
import functools

import jax
import jax.numpy as jnp
from jax import lax
from jax.experimental import pallas as pl
from jax.experimental.pallas import tpu as pltpu
from jax.sharding import PartitionSpec as P

VARS = 5
CELLS = 1024
LINKS = 4
WINDOW = CELLS // LINKS
STREAM = 32
CROSS = 16
PLANES = 2
CHUNKS = 8
GROUPS = 4
LANES = 128
FACE_WEIGHT = 0.25

LOWER = 0
UPPER = 25
SOURCE = 50
ROWS = 110
ORDER = [z for i in range(CROSS // 2) for z in (i, CROSS - 1 - i)]
ENDS = (0, 3, 1, 2)
CORNERS = sorted(
    range(STREAM),
    key=lambda s: (
        ENDS.index(s // 8) // 2 + ENDS.index(s // 2 % 4) // 2,
        ENDS.index(s // 8) ^ ENDS.index(s // 2 % 4),
        ENDS.index(s // 8),
        s % 2,
    ),
)
PLACE = [CORNERS.index(s) for s in range(STREAM)]
KEPT = 28
PIECES = 7

F32 = jnp.float32
BF16 = jnp.bfloat16
HBM = pl.BlockSpec(memory_space=pltpu.HBM)
SMEM = pl.BlockSpec(memory_space=pltpu.SMEM)
VMEM = pl.BlockSpec(memory_space=pltpu.VMEM)
PARAMS = pltpu.CompilerParams(vmem_limit_bytes=24 * 1024 * 1024)
TABLE = pltpu.SMEM((LINKS, CROSS), jnp.int32)


def thirds(x):
    high = x.astype(BF16)
    rest = x - high.astype(F32)
    middle = rest.astype(BF16)
    low = (rest - middle.astype(F32)).astype(BF16)
    return jnp.concatenate([high, middle, low], axis=0)


def times(x, matrix):
    n = x.shape[0]
    parts = jnp.dot(thirds(x), matrix, preferred_element_type=F32)
    return (parts[2 * n:] + parts[n:2 * n]) + parts[:n]


def copy_in(pairs, sems):
    copies = [pltpu.make_async_copy(src, dst, sems.at[i]) for i, (src, dst) in enumerate(pairs)]
    for copy in copies:
        copy.start()
    return copies


def slots_of(own, link, owner_ref, start_ref, count_ref, flip_ref):
    owner = owner_ref[link, own]
    count = count_ref[link, own]
    turned = jnp.logical_and(flip_ref[link, own] == 1, own > owner)
    bound = jnp.where(turned, count, 0)
    offset = start_ref[link, own] - link * WINDOW
    cell = lax.broadcasted_iota(jnp.int32, (1, WINDOW), 1)
    place = (cell - offset) & (WINDOW - 1)
    place = jnp.where(place < bound, count - 1 - place, place)
    rest = place & 127
    return ((rest >> 4) << 5) + ((place >> 7) << 4) + (rest & 15)


def onehot(row):
    rows = lax.broadcasted_iota(jnp.int32, (WINDOW, WINDOW), 0)
    return jnp.where(rows == row, 1.0, 0.0).astype(BF16)


def pack_kernel(
    owner_in, start_in, count_in, flip_in, live_in, rhs_in, diagonal_in, lower_in, upper_in,
    out_ref, matrix_ref,
    owner_ref, start_ref, count_ref, flip_ref, live_ref, rhs_ref, diagonal_ref, lower_ref, upper_ref,
    rows_ref, sems,
):
    copies = copy_in(
        [
            (owner_in, owner_ref), (start_in, start_ref), (count_in, count_ref),
            (flip_in, flip_ref), (live_in, live_ref), (rhs_in, rhs_ref),
            (diagonal_in, diagonal_ref), (lower_in, lower_ref), (upper_in, upper_ref),
        ],
        sems,
    )
    own = lax.axis_index("cross")
    rows_ref[pl.ds(ROWS, LANES - ROWS), :] = jnp.zeros((LANES - ROWS, CELLS), F32)
    for copy in copies[:5]:
        copy.wait()
    for link in range(LINKS):
        matrix_ref[link] = onehot(slots_of(own, link, owner_ref, start_ref, count_ref, flip_ref))
    for copy in copies[5:]:
        copy.wait()
    cell = lax.broadcasted_iota(jnp.int32, (PLANES, CELLS), 1)
    live = cell < live_ref[own]
    for a in range(VARS):
        for b in range(VARS):
            at = VARS * a + b
            rows_ref[pl.ds(2 * (LOWER + at), 2), :] = lower_ref[a, b]
            rows_ref[pl.ds(2 * (UPPER + at), 2), :] = upper_ref[a, b]
        source = jnp.where(live, rhs_ref[a], 0.0) / diagonal_ref[...]
        rows_ref[pl.ds(2 * (SOURCE + a), 2), :] = source
    for link in range(LINKS):
        parts = lax.dot_general(
            matrix_ref[link],
            thirds(rows_ref[:, link * WINDOW:(link + 1) * WINDOW]),
            (((1,), (1,)), ((), ())),
            preferred_element_type=F32,
        )
        rows = (parts[:, 2 * LANES:] + parts[:, LANES:2 * LANES]) + parts[:, :LANES]
        for e in range(8):
            first = 32 * PLACE[8 * link + e]
            out_ref[first:first + 32, :] = rows[32 * e:32 * e + 32]


def total(rows, first=None):
    if first is None:
        return [(t[0] + t[1]) + (t[2] + t[3]) + t[4] for t in rows]
    return [((x + t[0]) + (t[1] + t[2])) + (t[3] + t[4]) for x, t in zip(first, rows)]


def entry(system_ref, at, p):
    row = 8 * (2 * at + p)
    return system_ref[row:row + 8, :]


def apply(system_ref, at, p, x, first=None):
    return total(
        [[entry(system_ref, at + VARS * a + b, p) * x[b] for b in range(VARS)] for a in range(VARS)],
        first,
    )


def compose(system_ref, at, later, earlier, out_ref):
    for c in range(VARS):
        column = [entry(system_ref, at + VARS * b + c, earlier) for b in range(VARS)]
        for a, x in enumerate(apply(system_ref, at, later, column)):
            out_ref[VARS * a + c] = x


def relay(matrix_ref, offset, offset_ref, state_ref, up):
    for a in range(VARS):
        offset_ref[a] = offset[a]
    state = [jnp.zeros((1, LANES), F32) for _ in range(VARS)]
    groups = range(GROUPS) if up else range(GROUPS - 1, -1, -1)
    chunks = range(CHUNKS) if up else range(CHUNKS - 1, -1, -1)
    for group in groups:
        if group != groups[0]:
            state = [pltpu.roll(x, 32 if up else 96, 1) for x in state]
        for k in chunks:
            row = slice(k, k + 1)
            for a in range(VARS):
                state_ref[group, a, row, :] = state[a]
            state = total(
                [
                    [matrix_ref[VARS * a + b, row, :] * state[b] for b in range(VARS)]
                    for a in range(VARS)
                ],
                [offset_ref[a, row, :] for a in range(VARS)],
            )
    lane = lax.broadcasted_iota(jnp.int32, (CHUNKS, LANES), 1) >> 5
    out = []
    for a in range(VARS):
        x = state_ref[GROUPS - 1, a]
        for group in range(GROUPS - 1):
            x = jnp.where(lane == group, state_ref[group, a], x)
        out.append(x)
    return out


def plus(x, y):
    return [a + b for a, b in zip(x, y)]


def rank_of(block):
    return jnp.where(block < CROSS // 2, 2 * block, 2 * (CROSS - 1 - block) + 1)


def face_matrix(owner_ref, count_ref):
    position = lax.axis_index("stream")
    link = position >> 3
    slot = ((position & 7) << 4) + rank_of(lax.axis_index("cross"))
    lane = lax.broadcasted_iota(jnp.int32, (1, LANES), 1)
    source = jnp.full((1, LANES), -1, jnp.int32)
    for rank, block in enumerate(ORDER):
        taken = jnp.where(
            slot < count_ref[link, block], rank_of(owner_ref[link, block]), -LANES
        )
        source = jnp.where((lane & 31) == rank, (lane & 96) + taken, source)
    rows = lax.broadcasted_iota(jnp.int32, (LANES, LANES), 0)
    return jnp.where(rows == source, FACE_WEIGHT, 0.0).astype(BF16)


def faces_kernel(in_ref, out_ref):
    lane = lax.broadcasted_iota(jnp.int32, (CROSS, LANES), 1)
    for row in range(KEPT):
        piece = row % PIECES
        first = 32 * PLACE[KEPT + row // PIECES]
        spare = pltpu.roll(in_ref[first:first + CROSS, :], ROWS - 16 * piece, 1)
        own = in_ref[32 * PLACE[row]:32 * PLACE[row] + CROSS, :]
        out_ref[pl.ds(row, CROSS, stride=KEPT), :] = jnp.where(lane < ROWS, own, spare)


def gather_faces(face_ref, rows_ref):
    piece_of = lax.broadcasted_iota(jnp.int32, (CROSS, LANES), 1) >> 4
    for chunk in range(KEPT, STREAM):
        last = jnp.zeros((CROSS, LANES), F32)
        for piece in range(PIECES):
            row = PIECES * (chunk - KEPT) + piece
            found = face_ref[pl.ds(row, CROSS, stride=KEPT), :]
            rows_ref[CROSS * row:CROSS * (row + 1), :] = found
            moved = pltpu.roll(found, LANES - ROWS + 16 * piece, 1)
            last = jnp.where(piece_of == piece, moved, last)
        rows_ref[CROSS * chunk:CROSS * (chunk + 1), :] = last


def solve_kernel(
    owner_in, count_in, in_ref, face_ref, out_ref, send_ref,
    owner_ref, count_ref, rows_ref, system_ref, lower_ref, upper_ref, offset_ref, state_ref, values_ref, sems,
):
    copies = copy_in([(owner_in, owner_ref), (count_in, count_ref)], sems)
    values_ref[160:, :] = jnp.zeros((96, LANES), F32)
    gather_faces(face_ref, rows_ref)
    for k in range(CHUNKS):
        parts = []
        for group in range(GROUPS):
            chunk = CHUNKS * group + k
            parts += [
                rows_ref[CROSS * chunk:CROSS * (chunk + 1), :],
                in_ref[32 * PLACE[chunk] + 16:32 * PLACE[chunk] + 32, :],
            ]
        system_ref[pl.ds(k, LANES, stride=CHUNKS), :] = jnp.concatenate(parts, axis=0).T
    for copy in copies:
        copy.wait()
    matrix = face_matrix(owner_ref, count_ref)
    lower = functools.partial(apply, system_ref, LOWER)
    upper = functools.partial(apply, system_ref, UPPER)
    compose(system_ref, LOWER, 1, 0, lower_ref)
    compose(system_ref, UPPER, 0, 1, upper_ref)

    def upper_sweep(lowered):
        offset = upper(0, lowered[1], lowered[0])
        after = relay(upper_ref, offset, offset_ref, state_ref, False)
        coupled_1 = upper(1, after)
        delta_1 = plus(lowered[1], coupled_1)
        coupled_0 = upper(0, delta_1)
        return [coupled_0, coupled_1], [plus(lowered[0], coupled_0), delta_1]

    def faces_of(delta):
        parts = times(jnp.concatenate(delta[0] + delta[1], axis=0), matrix)
        rows = [parts[CHUNKS * i:CHUNKS * (i + 1)] for i in range(2 * VARS)]
        return [rows[:VARS], rows[VARS:]]

    source = [[entry(system_ref, SOURCE + a, p) for a in range(VARS)] for p in range(PLANES)]
    before = relay(lower_ref, lower(1, source[0], source[1]), offset_ref, state_ref, True)
    lowered_0 = lower(0, before, source[0])
    lowered_1 = lower(1, lowered_0, source[1])
    coupled, first = upper_sweep([lowered_0, lowered_1])

    faces = faces_of(first)
    joint_0 = plus(faces[0], coupled[0])
    joint_1 = plus(faces[1], coupled[1])
    before = relay(lower_ref, lower(1, joint_0, joint_1), offset_ref, state_ref, True)
    along = lower(0, before)
    lowered_1 = lower(1, plus(joint_0, along), faces[1])
    coupled, second = upper_sweep([plus(faces[0], along), lowered_1])

    faces = faces_of(second)
    row = lax.broadcasted_iota(jnp.int32, (CHUNKS, LANES), 0)
    lane = lax.broadcasted_iota(jnp.int32, (CHUNKS, LANES), 1)
    previous = []
    for x in coupled[1]:
        x = pltpu.roll(x, 1, 0)
        x = jnp.where(row == 0, jnp.where(lane < 32, 0.0, pltpu.roll(x, 32, 1)), x)
        previous.append(x)
    results = [
        plus(first[0], second[0]),
        plus(first[1], second[1]),
        lower(0, previous, faces[0]),
        lower(1, coupled[0], faces[1]),
    ]
    for g in range(4):
        for a in range(VARS):
            at = CHUNKS * (VARS * g + a)
            out_ref[at:at + CHUNKS, :] = results[g][a]
            values_ref[at:at + CHUNKS, :] = results[g][a]
    turned = values_ref[0:LANES, :].T
    others = values_ref[LANES:2 * LANES, :].T
    lane_group = lax.broadcasted_iota(jnp.int32, (CROSS, LANES), 1) >> 5
    fifth = others[0:CROSS]
    for group in range(GROUPS):
        rows = slice(32 * group, 32 * group + CROSS)
        send_ref[pl.ds(group, CROSS, stride=5), :] = turned[rows]
        if group:
            fifth = jnp.where(lane_group == group, pltpu.roll(others[rows], 32 * group, 1), fifth)
    send_ref[pl.ds(4, CROSS, stride=5), :] = fifth


def regroup(parts):
    lane = lax.broadcasted_iota(jnp.int32, parts[0].shape, 1)
    first_half = lane < 64
    even = (lane & 32) == 0
    half = [None] * 4
    for i in range(2):
        x, y = parts[i], parts[i + 2]
        half[i] = jnp.where(first_half, x, pltpu.roll(y, 64, 1))
        half[i + 2] = jnp.where(first_half, pltpu.roll(x, 64, 1), y)
    out = [None] * 4
    for i in (0, 2):
        x, y = half[i], half[i + 1]
        out[i] = jnp.where(even, x, pltpu.roll(y, 32, 1))
        out[i + 1] = jnp.where(even, pltpu.roll(x, 96, 1), y)
    return out


def join_kernel(in_ref, face_ref, out_ref, values_ref):
    lane = lax.broadcasted_iota(jnp.int32, (8, LANES), 1)
    returned = (lane & 16) == 0
    blank = jnp.zeros((16, LANES), F32)
    fifth = face_ref[pl.ds(4, CROSS, stride=5), :]
    parts = []
    others = []
    for group in range(GROUPS):
        parts += [face_ref[pl.ds(group, CROSS, stride=5), :], blank]
        others += [pltpu.roll(fifth, (LANES - 32 * group) % LANES, 1) if group else fifth, blank]
    values_ref[0:LANES, :] = jnp.concatenate(parts, axis=0).T
    values_ref[LANES:2 * LANES, :] = jnp.concatenate(others, axis=0).T
    for a in range(VARS):
        tiles = []
        for g in range(4):
            at = CHUNKS * (VARS * g + a)
            rows = slice(at, at + CHUNKS)
            tiles.append(jnp.where(returned, values_ref[rows, :], in_ref[rows, :]))
        for group, tile in enumerate(regroup(tiles)):
            out_ref[pl.ds(VARS * CHUNKS * group + a, CHUNKS, stride=VARS), :] = tile


def unpack_kernel(matrix_ref, diagonal_ref, in_ref, solution_ref, residual_ref, rows_ref):
    for column in range(8):
        tiles = regroup(
            [in_ref[VARS * (4 * column + e):VARS * (4 * column + e + 1), :] for e in range(4)]
        )
        for g, tile in enumerate(tiles):
            rows_ref[8 * g:8 * g + VARS, LANES * column:LANES * (column + 1)] = tile
    for link in range(LINKS):
        window = slice(link * WINDOW, (link + 1) * WINDOW)
        cells = times(rows_ref[:, window], matrix_ref[link])
        for p in range(PLANES):
            residual = cells[16 + 8 * p:16 + 8 * p + VARS] * diagonal_ref[p:p + 1, window]
            for a in range(VARS):
                solution_ref[a, p:p + 1, window] = cells[8 * p + a:8 * p + a + 1]
                residual_ref[a, p:p + 1, window] = residual[a:a + 1]


def shape(*dims):
    return jax.ShapeDtypeStruct(dims, F32)


def local(
    rhs,
    diagonal,
    lower_transfer,
    upper_transfer,
    face_owner,
    face_start,
    face_count,
    face_flip,
    block_cells,
):
    owner, start, count, flip = face_owner.T, face_start.T, face_count.T, face_flip.T
    transfer = pltpu.VMEM((VARS, VARS, PLANES, CELLS), F32)
    planes = pltpu.VMEM((PLANES, CELLS), F32)
    in_hbm = functools.partial(pltpu.with_memory_space_constraint, memory_space=pltpu.HBM)
    packed, matrix = pl.pallas_call(
        pack_kernel,
        out_shape=[shape(CELLS, LANES), jax.ShapeDtypeStruct((LINKS, WINDOW, WINDOW), BF16)],
        in_specs=[HBM] * 9,
        out_specs=[VMEM] * 2,
        scratch_shapes=[TABLE] * 4
        + [
            pltpu.SMEM((CROSS,), jnp.int32), pltpu.VMEM((VARS, PLANES, CELLS), F32), planes,
            transfer, transfer, pltpu.VMEM((LANES, CELLS), F32), pltpu.SemaphoreType.DMA((9,)),
        ],
        compiler_params=PARAMS,
        name="pack_cells",
    )(
        *[
            in_hbm(x)
            for x in (
                owner, start, count, flip,
                block_cells,
                rhs.transpose(1, 0, 2),
                diagonal,
                lower_transfer.transpose(1, 2, 0, 3),
                upper_transfer.transpose(1, 2, 0, 3),
            )
        ]
    )
    arrived = lax.all_to_all(
        packed.reshape(STREAM, 32, LANES), "stream", 0, 0, axis_index_groups=[CORNERS], tiled=True
    )
    arrived = arrived.reshape(CELLS, LANES)
    faces = pl.pallas_call(
        faces_kernel,
        out_shape=shape(CROSS * KEPT, LANES),
        in_specs=[VMEM],
        out_specs=VMEM,
        compiler_params=PARAMS,
        name="take_faces",
    )(arrived)
    faces = lax.all_to_all(faces.reshape(CROSS * KEPT // 4, 4, LANES), "cross", 0, 0, axis_index_groups=[ORDER], tiled=True)

    composed = pltpu.VMEM((VARS * VARS, CHUNKS, LANES), F32)
    results, faces = pl.pallas_call(
        solve_kernel,
        out_shape=[shape(CHUNKS * 4 * VARS, LANES), shape(5 * CROSS, LANES)],
        in_specs=[HBM, HBM, VMEM, VMEM],
        out_specs=[VMEM, VMEM],
        scratch_shapes=[TABLE] * 2
        + [
            pltpu.VMEM((CELLS // 2, LANES), F32),
            pltpu.VMEM((CHUNKS * LANES, LANES), F32), composed, composed,
            pltpu.VMEM((VARS, CHUNKS, LANES), F32),
            pltpu.VMEM((GROUPS, VARS, CHUNKS, LANES), F32),
            pltpu.VMEM((2 * LANES, LANES), F32),
            pltpu.SemaphoreType.DMA((2,)),
        ],
        compiler_params=PARAMS,
        name="solve_cells",
    )(owner, count, arrived, faces.reshape(CROSS * KEPT, LANES))
    faces = lax.all_to_all(faces.reshape(5 * CROSS, 1, LANES), "cross", 0, 0, axis_index_groups=[ORDER], tiled=True)
    results = pl.pallas_call(
        join_kernel,
        out_shape=shape(STREAM * VARS, LANES),
        in_specs=[VMEM, VMEM],
        out_specs=VMEM,
        scratch_shapes=[pltpu.VMEM((2 * LANES, LANES), F32)],
        compiler_params=PARAMS,
        name="join_faces",
    )(results, faces.reshape(5 * CROSS, LANES))
    returned = lax.all_to_all(
        results.reshape(STREAM * VARS, 1, LANES), "stream", 0, 0, tiled=True
    )
    outs = pl.pallas_call(
        unpack_kernel,
        out_shape=[shape(VARS, PLANES, CELLS)] * 2,
        in_specs=[VMEM] * 3,
        out_specs=[VMEM] * 2,
        scratch_shapes=[pltpu.VMEM((32, CELLS), F32)],
        compiler_params=PARAMS,
        name="unpack_cells",
    )(matrix, diagonal, returned.reshape(STREAM * VARS, LANES))
    return tuple(x.transpose(1, 0, 2) for x in outs)


def solution(mesh):
    return jax.shard_map(
        local,
        mesh=mesh,
        in_specs=(
            P("stream", None, "cross"),
            P("stream", "cross"),
            P("stream", None, None, "cross"),
            P("stream", None, None, "cross"),
            P(),
            P(),
            P(),
            P(),
            P(),
        ),
        out_specs=(P("stream", None, "cross"), P("stream", None, "cross")),
        check_vma=False,
    )
```

```python
import functools

import jax
import jax.numpy as jnp
from jax import lax
from jax.experimental import pallas as pl
from jax.experimental.pallas import tpu as pltpu
from jax.sharding import PartitionSpec as P

VARS = 5
CELLS = 1024
LINKS = 4
WINDOW = CELLS // LINKS
STREAM = 32
CROSS = 16
PLANES = 2
CHUNKS = 8
GROUPS = 4
LANES = 128
FACE_WEIGHT = 0.25

LOWER = 0
UPPER = 25
SOURCE = 50
ROWS = 110
ORDER = list(range(0, CROSS, 2)) + list(range(CROSS - 1, 0, -2))
KEPT = 28
PIECES = 7

F32 = jnp.float32
BF16 = jnp.bfloat16
HBM = pl.BlockSpec(memory_space=pltpu.HBM)
SMEM = pl.BlockSpec(memory_space=pltpu.SMEM)
VMEM = pl.BlockSpec(memory_space=pltpu.VMEM)
PARAMS = pltpu.CompilerParams(vmem_limit_bytes=24 * 1024 * 1024)
TABLE = pltpu.SMEM((LINKS, CROSS), jnp.int32)


def thirds(x):
    high = x.astype(BF16)
    rest = x - high.astype(F32)
    middle = rest.astype(BF16)
    low = (rest - middle.astype(F32)).astype(BF16)
    return jnp.concatenate([high, middle, low], axis=0)


def times(x, matrix):
    n = x.shape[0]
    parts = jnp.dot(thirds(x), matrix, preferred_element_type=F32)
    return (parts[2 * n:] + parts[n:2 * n]) + parts[:n]


def copy_in(pairs, sems):
    copies = [pltpu.make_async_copy(src, dst, sems.at[i]) for i, (src, dst) in enumerate(pairs)]
    for copy in copies:
        copy.start()
    return copies


def slots_of(own, link, owner_ref, start_ref, count_ref, flip_ref):
    owner = owner_ref[link, own]
    count = count_ref[link, own]
    turned = jnp.logical_and(flip_ref[link, own] == 1, own > owner)
    bound = jnp.where(turned, count, 0)
    offset = start_ref[link, own] - link * WINDOW
    cell = lax.broadcasted_iota(jnp.int32, (1, WINDOW), 1)
    place = (cell - offset) & (WINDOW - 1)
    place = jnp.where(place < bound, count - 1 - place, place)
    rest = place & 127
    return ((rest >> 4) << 5) + ((place >> 7) << 4) + (rest & 15)


def onehot(row):
    rows = lax.broadcasted_iota(jnp.int32, (WINDOW, WINDOW), 0)
    return jnp.where(rows == row, 1.0, 0.0).astype(BF16)


def pack_kernel(
    owner_in, start_in, count_in, flip_in, live_in, rhs_in, diagonal_in, lower_in, upper_in,
    out_ref, matrix_ref,
    owner_ref, start_ref, count_ref, flip_ref, live_ref, rhs_ref, diagonal_ref, lower_ref, upper_ref,
    rows_ref, sems,
):
    copies = copy_in(
        [
            (owner_in, owner_ref), (start_in, start_ref), (count_in, count_ref),
            (flip_in, flip_ref), (live_in, live_ref), (rhs_in, rhs_ref),
            (diagonal_in, diagonal_ref), (lower_in, lower_ref), (upper_in, upper_ref),
        ],
        sems,
    )
    own = lax.axis_index("cross")
    rows_ref[pl.ds(ROWS, LANES - ROWS), :] = jnp.zeros((LANES - ROWS, CELLS), F32)
    for copy in copies[:5]:
        copy.wait()
    for link in range(LINKS):
        matrix_ref[link] = onehot(slots_of(own, link, owner_ref, start_ref, count_ref, flip_ref))
    for copy in copies[5:]:
        copy.wait()
    cell = lax.broadcasted_iota(jnp.int32, (PLANES, CELLS), 1)
    live = cell < live_ref[own]
    for a in range(VARS):
        for b in range(VARS):
            at = VARS * a + b
            rows_ref[pl.ds(2 * (LOWER + at), 2), :] = lower_ref[a, b]
            rows_ref[pl.ds(2 * (UPPER + at), 2), :] = upper_ref[a, b]
        source = jnp.where(live, rhs_ref[a], 0.0) / diagonal_ref[...]
        rows_ref[pl.ds(2 * (SOURCE + a), 2), :] = source
    for link in range(LINKS):
        parts = lax.dot_general(
            matrix_ref[link],
            thirds(rows_ref[:, link * WINDOW:(link + 1) * WINDOW]),
            (((1,), (1,)), ((), ())),
            preferred_element_type=F32,
        )
        out_ref[link * WINDOW:(link + 1) * WINDOW, :] = (
            parts[:, 2 * LANES:] + parts[:, LANES:2 * LANES]
        ) + parts[:, :LANES]


def total(rows, first=None):
    if first is None:
        return [(t[0] + t[1]) + (t[2] + t[3]) + t[4] for t in rows]
    return [((x + t[0]) + (t[1] + t[2])) + (t[3] + t[4]) for x, t in zip(first, rows)]


def entry(system_ref, at, p):
    row = 8 * (2 * at + p)
    return system_ref[row:row + 8, :]


def apply(system_ref, at, p, x, first=None):
    return total(
        [[entry(system_ref, at + VARS * a + b, p) * x[b] for b in range(VARS)] for a in range(VARS)],
        first,
    )


def compose(system_ref, at, later, earlier, out_ref):
    for c in range(VARS):
        column = [entry(system_ref, at + VARS * b + c, earlier) for b in range(VARS)]
        for a, x in enumerate(apply(system_ref, at, later, column)):
            out_ref[VARS * a + c] = x


def relay(matrix_ref, offset, offset_ref, state_ref, up):
    for a in range(VARS):
        offset_ref[a] = offset[a]
    state = [jnp.zeros((1, LANES), F32) for _ in range(VARS)]
    groups = range(GROUPS) if up else range(GROUPS - 1, -1, -1)
    chunks = range(CHUNKS) if up else range(CHUNKS - 1, -1, -1)
    for group in groups:
        if group != groups[0]:
            state = [pltpu.roll(x, 32 if up else 96, 1) for x in state]
        for k in chunks:
            row = slice(k, k + 1)
            for a in range(VARS):
                state_ref[group, a, row, :] = state[a]
            state = total(
                [
                    [matrix_ref[VARS * a + b, row, :] * state[b] for b in range(VARS)]
                    for a in range(VARS)
                ],
                [offset_ref[a, row, :] for a in range(VARS)],
            )
    lane = lax.broadcasted_iota(jnp.int32, (CHUNKS, LANES), 1) >> 5
    out = []
    for a in range(VARS):
        x = state_ref[GROUPS - 1, a]
        for group in range(GROUPS - 1):
            x = jnp.where(lane == group, state_ref[group, a], x)
        out.append(x)
    return out


def plus(x, y):
    return [a + b for a, b in zip(x, y)]


def rank_of(block):
    return jnp.where((block & 1) == 0, block >> 1, CROSS - 1 - (block >> 1))


def face_matrix(owner_ref, count_ref):
    position = lax.axis_index("stream")
    link = position >> 3
    slot = ((position & 7) << 4) + rank_of(lax.axis_index("cross"))
    lane = lax.broadcasted_iota(jnp.int32, (1, LANES), 1)
    source = jnp.full((1, LANES), -1, jnp.int32)
    for rank, block in enumerate(ORDER):
        taken = jnp.where(
            slot < count_ref[link, block], rank_of(owner_ref[link, block]), -LANES
        )
        source = jnp.where((lane & 31) == rank, (lane & 96) + taken, source)
    rows = lax.broadcasted_iota(jnp.int32, (LANES, LANES), 0)
    return jnp.where(rows == source, FACE_WEIGHT, 0.0).astype(BF16)


def faces_kernel(in_ref, out_ref):
    lane = lax.broadcasted_iota(jnp.int32, (CROSS, LANES), 1)
    for row in range(KEPT):
        piece = row % PIECES
        first = 32 * (KEPT + row // PIECES)
        spare = pltpu.roll(in_ref[first:first + CROSS, :], ROWS - 16 * piece, 1)
        own = in_ref[32 * row:32 * row + CROSS, :]
        out_ref[pl.ds(row, CROSS, stride=KEPT), :] = jnp.where(lane < ROWS, own, spare)


def gather_faces(face_ref, rows_ref):
    piece_of = lax.broadcasted_iota(jnp.int32, (CROSS, LANES), 1) >> 4
    for chunk in range(KEPT, STREAM):
        last = jnp.zeros((CROSS, LANES), F32)
        for piece in range(PIECES):
            row = PIECES * (chunk - KEPT) + piece
            found = face_ref[pl.ds(row, CROSS, stride=KEPT), :]
            rows_ref[CROSS * row:CROSS * (row + 1), :] = found
            moved = pltpu.roll(found, LANES - ROWS + 16 * piece, 1)
            last = jnp.where(piece_of == piece, moved, last)
        rows_ref[CROSS * chunk:CROSS * (chunk + 1), :] = last


def solve_kernel(
    owner_in, count_in, in_ref, face_ref, out_ref, send_ref,
    owner_ref, count_ref, rows_ref, system_ref, lower_ref, upper_ref, offset_ref, state_ref, values_ref, sems,
):
    copies = copy_in([(owner_in, owner_ref), (count_in, count_ref)], sems)
    values_ref[160:, :] = jnp.zeros((96, LANES), F32)
    gather_faces(face_ref, rows_ref)
    for k in range(CHUNKS):
        parts = []
        for group in range(GROUPS):
            chunk = CHUNKS * group + k
            parts += [
                rows_ref[CROSS * chunk:CROSS * (chunk + 1), :],
                in_ref[32 * chunk + 16:32 * chunk + 32, :],
            ]
        system_ref[pl.ds(k, LANES, stride=CHUNKS), :] = jnp.concatenate(parts, axis=0).T
    for copy in copies:
        copy.wait()
    matrix = face_matrix(owner_ref, count_ref)
    lower = functools.partial(apply, system_ref, LOWER)
    upper = functools.partial(apply, system_ref, UPPER)
    compose(system_ref, LOWER, 1, 0, lower_ref)
    compose(system_ref, UPPER, 0, 1, upper_ref)

    def upper_sweep(lowered):
        offset = upper(0, lowered[1], lowered[0])
        after = relay(upper_ref, offset, offset_ref, state_ref, False)
        coupled_1 = upper(1, after)
        delta_1 = plus(lowered[1], coupled_1)
        coupled_0 = upper(0, delta_1)
        return [coupled_0, coupled_1], [plus(lowered[0], coupled_0), delta_1]

    def faces_of(delta):
        parts = times(jnp.concatenate(delta[0] + delta[1], axis=0), matrix)
        rows = [parts[CHUNKS * i:CHUNKS * (i + 1)] for i in range(2 * VARS)]
        return [rows[:VARS], rows[VARS:]]

    source = [[entry(system_ref, SOURCE + a, p) for a in range(VARS)] for p in range(PLANES)]
    before = relay(lower_ref, lower(1, source[0], source[1]), offset_ref, state_ref, True)
    lowered_0 = lower(0, before, source[0])
    lowered_1 = lower(1, lowered_0, source[1])
    coupled, first = upper_sweep([lowered_0, lowered_1])

    faces = faces_of(first)
    joint_0 = plus(faces[0], coupled[0])
    joint_1 = plus(faces[1], coupled[1])
    before = relay(lower_ref, lower(1, joint_0, joint_1), offset_ref, state_ref, True)
    along = lower(0, before)
    lowered_1 = lower(1, plus(joint_0, along), faces[1])
    coupled, second = upper_sweep([plus(faces[0], along), lowered_1])

    faces = faces_of(second)
    row = lax.broadcasted_iota(jnp.int32, (CHUNKS, LANES), 0)
    lane = lax.broadcasted_iota(jnp.int32, (CHUNKS, LANES), 1)
    previous = []
    for x in coupled[1]:
        x = pltpu.roll(x, 1, 0)
        x = jnp.where(row == 0, jnp.where(lane < 32, 0.0, pltpu.roll(x, 32, 1)), x)
        previous.append(x)
    results = [
        plus(first[0], second[0]),
        plus(first[1], second[1]),
        lower(0, previous, faces[0]),
        lower(1, coupled[0], faces[1]),
    ]
    for g in range(4):
        for a in range(VARS):
            at = CHUNKS * (VARS * g + a)
            out_ref[at:at + CHUNKS, :] = results[g][a]
            values_ref[at:at + CHUNKS, :] = results[g][a]
    turned = values_ref[0:LANES, :].T
    others = values_ref[LANES:2 * LANES, :].T
    lane_group = lax.broadcasted_iota(jnp.int32, (CROSS, LANES), 1) >> 5
    fifth = others[0:CROSS]
    for group in range(GROUPS):
        rows = slice(32 * group, 32 * group + CROSS)
        for rank, block in enumerate(ORDER):
            first = 32 * group + rank
            send_ref[5 * block + group:5 * block + group + 1, :] = turned[first:first + 1]
        if group:
            fifth = jnp.where(lane_group == group, pltpu.roll(others[rows], 32 * group, 1), fifth)
    for rank, block in enumerate(ORDER):
        send_ref[5 * block + 4:5 * block + 5, :] = fifth[rank:rank + 1]


def regroup(parts):
    lane = lax.broadcasted_iota(jnp.int32, parts[0].shape, 1)
    first_half = lane < 64
    even = (lane & 32) == 0
    half = [None] * 4
    for i in range(2):
        x, y = parts[i], parts[i + 2]
        half[i] = jnp.where(first_half, x, pltpu.roll(y, 64, 1))
        half[i + 2] = jnp.where(first_half, pltpu.roll(x, 64, 1), y)
    out = [None] * 4
    for i in (0, 2):
        x, y = half[i], half[i + 1]
        out[i] = jnp.where(even, x, pltpu.roll(y, 32, 1))
        out[i + 1] = jnp.where(even, pltpu.roll(x, 96, 1), y)
    return out


def join_kernel(in_ref, face_ref, out_ref, values_ref, ranked_ref):
    lane = lax.broadcasted_iota(jnp.int32, (8, LANES), 1)
    returned = (lane & 16) == 0
    blank = jnp.zeros((16, LANES), F32)
    for row in range(5):
        for rank, block in enumerate(ORDER):
            first = CROSS * row + rank
            ranked_ref[first:first + 1, :] = face_ref[5 * block + row:5 * block + row + 1, :]
    fifth = ranked_ref[4 * CROSS:, :]
    parts = []
    others = []
    for group in range(GROUPS):
        parts += [ranked_ref[CROSS * group:CROSS * (group + 1), :], blank]
        others += [pltpu.roll(fifth, (LANES - 32 * group) % LANES, 1) if group else fifth, blank]
    values_ref[0:LANES, :] = jnp.concatenate(parts, axis=0).T
    values_ref[LANES:2 * LANES, :] = jnp.concatenate(others, axis=0).T
    for a in range(VARS):
        tiles = []
        for g in range(4):
            at = CHUNKS * (VARS * g + a)
            rows = slice(at, at + CHUNKS)
            tiles.append(jnp.where(returned, values_ref[rows, :], in_ref[rows, :]))
        for group, tile in enumerate(regroup(tiles)):
            out_ref[pl.ds(VARS * CHUNKS * group + a, CHUNKS, stride=VARS), :] = tile


def unpack_kernel(matrix_ref, diagonal_ref, in_ref, solution_ref, residual_ref, rows_ref):
    for column in range(8):
        tiles = regroup(
            [in_ref[VARS * (4 * column + e):VARS * (4 * column + e + 1), :] for e in range(4)]
        )
        for g, tile in enumerate(tiles):
            rows_ref[8 * g:8 * g + VARS, LANES * column:LANES * (column + 1)] = tile
    for link in range(LINKS):
        window = slice(link * WINDOW, (link + 1) * WINDOW)
        cells = times(rows_ref[:, window], matrix_ref[link])
        for p in range(PLANES):
            residual = cells[16 + 8 * p:16 + 8 * p + VARS] * diagonal_ref[p:p + 1, window]
            for a in range(VARS):
                solution_ref[a, p:p + 1, window] = cells[8 * p + a:8 * p + a + 1]
                residual_ref[a, p:p + 1, window] = residual[a:a + 1]


def shape(*dims):
    return jax.ShapeDtypeStruct(dims, F32)


def local(
    rhs,
    diagonal,
    lower_transfer,
    upper_transfer,
    face_owner,
    face_start,
    face_count,
    face_flip,
    block_cells,
):
    owner, start, count, flip = face_owner.T, face_start.T, face_count.T, face_flip.T
    transfer = pltpu.VMEM((VARS, VARS, PLANES, CELLS), F32)
    planes = pltpu.VMEM((PLANES, CELLS), F32)
    in_hbm = functools.partial(pltpu.with_memory_space_constraint, memory_space=pltpu.HBM)
    packed, matrix = pl.pallas_call(
        pack_kernel,
        out_shape=[shape(CELLS, LANES), jax.ShapeDtypeStruct((LINKS, WINDOW, WINDOW), BF16)],
        in_specs=[HBM] * 9,
        out_specs=[VMEM] * 2,
        scratch_shapes=[TABLE] * 4
        + [
            pltpu.SMEM((CROSS,), jnp.int32), pltpu.VMEM((VARS, PLANES, CELLS), F32), planes,
            transfer, transfer, pltpu.VMEM((LANES, CELLS), F32), pltpu.SemaphoreType.DMA((9,)),
        ],
        compiler_params=PARAMS,
        name="pack_cells",
    )(
        *[
            in_hbm(x)
            for x in (
                owner, start, count, flip,
                block_cells,
                rhs.transpose(1, 0, 2),
                diagonal,
                lower_transfer.transpose(1, 2, 0, 3),
                upper_transfer.transpose(1, 2, 0, 3),
            )
        ]
    )
    arrived = lax.all_to_all(packed.reshape(STREAM, 32, LANES), "stream", 0, 0, tiled=True)
    arrived = arrived.reshape(CELLS, LANES)
    faces = pl.pallas_call(
        faces_kernel,
        out_shape=shape(CROSS * KEPT, LANES),
        in_specs=[VMEM],
        out_specs=VMEM,
        compiler_params=PARAMS,
        name="take_faces",
    )(arrived)
    faces = lax.all_to_all(faces.reshape(CROSS * KEPT // 4, 4, LANES), "cross", 0, 0, axis_index_groups=[ORDER], tiled=True)

    composed = pltpu.VMEM((VARS * VARS, CHUNKS, LANES), F32)
    results, faces = pl.pallas_call(
        solve_kernel,
        out_shape=[shape(CHUNKS * 4 * VARS, LANES), shape(5 * CROSS, LANES)],
        in_specs=[HBM, HBM, VMEM, VMEM],
        out_specs=[VMEM, VMEM],
        scratch_shapes=[TABLE] * 2
        + [
            pltpu.VMEM((CELLS // 2, LANES), F32),
            pltpu.VMEM((CHUNKS * LANES, LANES), F32), composed, composed,
            pltpu.VMEM((VARS, CHUNKS, LANES), F32),
            pltpu.VMEM((GROUPS, VARS, CHUNKS, LANES), F32),
            pltpu.VMEM((2 * LANES, LANES), F32),
            pltpu.SemaphoreType.DMA((2,)),
        ],
        compiler_params=PARAMS,
        name="solve_cells",
    )(owner, count, arrived, faces.reshape(CROSS * KEPT, LANES))
    faces = lax.all_to_all(faces.reshape(5 * CROSS, 1, LANES), "cross", 0, 0, tiled=True)
    results = pl.pallas_call(
        join_kernel,
        out_shape=shape(STREAM * VARS, LANES),
        in_specs=[VMEM, VMEM],
        out_specs=VMEM,
        scratch_shapes=[
            pltpu.VMEM((2 * LANES, LANES), F32), pltpu.VMEM((5 * CROSS, LANES), F32)
        ],
        compiler_params=PARAMS,
        name="join_faces",
    )(results, faces.reshape(5 * CROSS, LANES))
    returned = lax.all_to_all(
        results.reshape(STREAM * VARS, 1, LANES), "stream", 0, 0, tiled=True
    )
    outs = pl.pallas_call(
        unpack_kernel,
        out_shape=[shape(VARS, PLANES, CELLS)] * 2,
        in_specs=[VMEM] * 3,
        out_specs=[VMEM] * 2,
        scratch_shapes=[pltpu.VMEM((32, CELLS), F32)],
        compiler_params=PARAMS,
        name="unpack_cells",
    )(matrix, diagonal, returned.reshape(STREAM * VARS, LANES))
    return tuple(x.transpose(1, 0, 2) for x in outs)


def solution(mesh):
    return jax.shard_map(
        local,
        mesh=mesh,
        in_specs=(
            P("stream", None, "cross"),
            P("stream", "cross"),
            P("stream", None, None, "cross"),
            P("stream", None, None, "cross"),
            P(),
            P(),
            P(),
            P(),
            P(),
        ),
        out_specs=(P("stream", None, "cross"), P("stream", None, "cross")),
        check_vma=False,
    )
```

```python
import functools

import jax
import jax.numpy as jnp
from jax import lax
from jax.experimental import pallas as pl
from jax.experimental.pallas import tpu as pltpu
from jax.sharding import PartitionSpec as P

VARS = 5
CELLS = 1024
LINKS = 4
WINDOW = CELLS // LINKS
STREAM = 32
CROSS = 16
PLANES = 2
CHUNKS = 8
GROUPS = 4
LANES = 128
FACE_WEIGHT = 0.25

LOWER = 0
UPPER = 25
SOURCE = 50
ROWS = 110
KEPT = 28
PIECES = 7

F32 = jnp.float32
BF16 = jnp.bfloat16
HBM = pl.BlockSpec(memory_space=pltpu.HBM)
SMEM = pl.BlockSpec(memory_space=pltpu.SMEM)
VMEM = pl.BlockSpec(memory_space=pltpu.VMEM)
PARAMS = pltpu.CompilerParams(vmem_limit_bytes=24 * 1024 * 1024)
TABLE = pltpu.SMEM((LINKS, CROSS), jnp.int32)


def thirds(x):
    high = x.astype(BF16)
    rest = x - high.astype(F32)
    middle = rest.astype(BF16)
    low = (rest - middle.astype(F32)).astype(BF16)
    return jnp.concatenate([high, middle, low], axis=0)


def times(x, matrix):
    n = x.shape[0]
    parts = jnp.dot(thirds(x), matrix, preferred_element_type=F32)
    return (parts[2 * n:] + parts[n:2 * n]) + parts[:n]


def copy_in(pairs, sems):
    copies = [pltpu.make_async_copy(src, dst, sems.at[i]) for i, (src, dst) in enumerate(pairs)]
    for copy in copies:
        copy.start()
    return copies


def slots_of(own, link, owner_ref, start_ref, count_ref, flip_ref):
    owner = owner_ref[link, own]
    count = count_ref[link, own]
    turned = jnp.logical_and(flip_ref[link, own] == 1, own > owner)
    bound = jnp.where(turned, count, 0)
    offset = start_ref[link, own] - link * WINDOW
    cell = lax.broadcasted_iota(jnp.int32, (1, WINDOW), 1)
    place = (cell - offset) & (WINDOW - 1)
    place = jnp.where(place < bound, count - 1 - place, place)
    rest = place & 127
    return ((rest >> 4) << 5) + ((place >> 7) << 4) + (rest & 15)


def onehot(row):
    rows = lax.broadcasted_iota(jnp.int32, (WINDOW, WINDOW), 0)
    return jnp.where(rows == row, 1.0, 0.0).astype(BF16)


def pack_kernel(
    owner_in, start_in, count_in, flip_in, live_in, rhs_in, diagonal_in, lower_in, upper_in,
    out_ref, matrix_ref,
    owner_ref, start_ref, count_ref, flip_ref, live_ref, rhs_ref, diagonal_ref, lower_ref, upper_ref,
    rows_ref, sems,
):
    copies = copy_in(
        [
            (owner_in, owner_ref), (start_in, start_ref), (count_in, count_ref),
            (flip_in, flip_ref), (lower_in, lower_ref), (upper_in, upper_ref),
            (live_in, live_ref), (rhs_in, rhs_ref), (diagonal_in, diagonal_ref),
        ],
        sems,
    )
    own = lax.axis_index("cross")
    rows_ref[pl.ds(ROWS, LANES - ROWS), :] = jnp.zeros((LANES - ROWS, CELLS), F32)
    for copy in copies[:4]:
        copy.wait()
    for link in range(LINKS):
        matrix_ref[link] = onehot(slots_of(own, link, owner_ref, start_ref, count_ref, flip_ref))
    for copy, first, ref in ((copies[4], LOWER, lower_ref), (copies[5], UPPER, upper_ref)):
        copy.wait()
        for a in range(VARS):
            for b in range(VARS):
                rows_ref[pl.ds(2 * (first + VARS * a + b), 2), :] = ref[a, b]
    for copy in copies[6:]:
        copy.wait()
    cell = lax.broadcasted_iota(jnp.int32, (PLANES, CELLS), 1)
    live = cell < live_ref[own]
    for a in range(VARS):
        source = jnp.where(live, rhs_ref[a], 0.0) / diagonal_ref[...]
        rows_ref[pl.ds(2 * (SOURCE + a), 2), :] = source
    for link in range(LINKS):
        parts = lax.dot_general(
            matrix_ref[link],
            thirds(rows_ref[:, link * WINDOW:(link + 1) * WINDOW]),
            (((1,), (1,)), ((), ())),
            preferred_element_type=F32,
        )
        out_ref[link * WINDOW:(link + 1) * WINDOW, :] = (
            parts[:, 2 * LANES:] + parts[:, LANES:2 * LANES]
        ) + parts[:, :LANES]


def total(rows, first=None):
    if first is None:
        return [(t[0] + t[1]) + (t[2] + t[3]) + t[4] for t in rows]
    return [((x + t[0]) + (t[1] + t[2])) + (t[3] + t[4]) for x, t in zip(first, rows)]


def entry(system_ref, at, p):
    row = 8 * (2 * at + p)
    return system_ref[row:row + 8, :]


def apply(system_ref, at, p, x, first=None):
    return total(
        [[entry(system_ref, at + VARS * a + b, p) * x[b] for b in range(VARS)] for a in range(VARS)],
        first,
    )


def compose(system_ref, at, later, earlier, out_ref):
    for c in range(VARS):
        column = [entry(system_ref, at + VARS * b + c, earlier) for b in range(VARS)]
        for a, x in enumerate(apply(system_ref, at, later, column)):
            out_ref[VARS * a + c] = x


def relay(matrix_ref, offset, offset_ref, state_ref, up):
    for a in range(VARS):
        offset_ref[a] = offset[a]
    state = [jnp.zeros((1, LANES), F32) for _ in range(VARS)]
    groups = range(GROUPS) if up else range(GROUPS - 1, -1, -1)
    chunks = range(CHUNKS) if up else range(CHUNKS - 1, -1, -1)
    for group in groups:
        if group != groups[0]:
            state = [pltpu.roll(x, 32 if up else 96, 1) for x in state]
        for k in chunks:
            row = slice(k, k + 1)
            for a in range(VARS):
                state_ref[group, a, row, :] = state[a]
            state = total(
                [
                    [matrix_ref[VARS * a + b, row, :] * state[b] for b in range(VARS)]
                    for a in range(VARS)
                ],
                [offset_ref[a, row, :] for a in range(VARS)],
            )
    lane = lax.broadcasted_iota(jnp.int32, (CHUNKS, LANES), 1) >> 5
    out = []
    for a in range(VARS):
        x = state_ref[GROUPS - 1, a]
        for group in range(GROUPS - 1):
            x = jnp.where(lane == group, state_ref[group, a], x)
        out.append(x)
    return out


def plus(x, y):
    return [a + b for a, b in zip(x, y)]


def face_matrix(owner_ref, count_ref):
    position = lax.axis_index("stream")
    link = position >> 3
    slot = ((position & 7) << 4) + lax.axis_index("cross")
    lane = lax.broadcasted_iota(jnp.int32, (1, LANES), 1)
    source = jnp.full((1, LANES), -1, jnp.int32)
    for block in range(CROSS):
        taken = jnp.where(slot < count_ref[link, block], owner_ref[link, block], -LANES)
        source = jnp.where((lane & 31) == block, (lane & 96) + taken, source)
    rows = lax.broadcasted_iota(jnp.int32, (LANES, LANES), 0)
    return jnp.where(rows == source, FACE_WEIGHT, 0.0).astype(BF16)


def faces_kernel(in_ref, out_ref):
    lane = lax.broadcasted_iota(jnp.int32, (CROSS, LANES), 1)
    for row in range(KEPT):
        piece = row % PIECES
        first = 32 * (KEPT + row // PIECES)
        spare = pltpu.roll(in_ref[first:first + CROSS, :], ROWS - 16 * piece, 1)
        own = in_ref[32 * row:32 * row + CROSS, :]
        out_ref[pl.ds(row, CROSS, stride=KEPT), :] = jnp.where(lane < ROWS, own, spare)


def face_rows(face_ref, chunk):
    if chunk < KEPT:
        return face_ref[pl.ds(chunk, CROSS, stride=KEPT), :]
    piece_of = lax.broadcasted_iota(jnp.int32, (CROSS, LANES), 1) >> 4
    out = jnp.zeros((CROSS, LANES), F32)
    for piece in range(PIECES):
        row = PIECES * (chunk - KEPT) + piece
        moved = pltpu.roll(
            face_ref[pl.ds(row, CROSS, stride=KEPT), :], LANES - ROWS + 16 * piece, 1
        )
        out = jnp.where(piece_of == piece, moved, out)
    return out


def solve_kernel(
    owner_in, count_in, in_ref, face_ref, out_ref, send_ref,
    owner_ref, count_ref, system_ref, lower_ref, upper_ref, offset_ref, state_ref, values_ref, sems,
):
    copies = copy_in([(owner_in, owner_ref), (count_in, count_ref)], sems)
    values_ref[160:, :] = jnp.zeros((96, LANES), F32)
    for k in range(CHUNKS):
        parts = []
        for group in range(GROUPS):
            chunk = CHUNKS * group + k
            parts += [face_rows(face_ref, chunk), in_ref[32 * chunk + 16:32 * chunk + 32, :]]
        system_ref[pl.ds(k, LANES, stride=CHUNKS), :] = jnp.concatenate(parts, axis=0).T
    for copy in copies:
        copy.wait()
    matrix = face_matrix(owner_ref, count_ref)
    lower = functools.partial(apply, system_ref, LOWER)
    upper = functools.partial(apply, system_ref, UPPER)
    compose(system_ref, LOWER, 1, 0, lower_ref)
    compose(system_ref, UPPER, 0, 1, upper_ref)

    def upper_sweep(lowered):
        offset = upper(0, lowered[1], lowered[0])
        after = relay(upper_ref, offset, offset_ref, state_ref, False)
        coupled_1 = upper(1, after)
        delta_1 = plus(lowered[1], coupled_1)
        coupled_0 = upper(0, delta_1)
        return [coupled_0, coupled_1], [plus(lowered[0], coupled_0), delta_1]

    def faces_of(delta):
        parts = times(jnp.concatenate(delta[0] + delta[1], axis=0), matrix)
        rows = [parts[CHUNKS * i:CHUNKS * (i + 1)] for i in range(2 * VARS)]
        return [rows[:VARS], rows[VARS:]]

    source = [[entry(system_ref, SOURCE + a, p) for a in range(VARS)] for p in range(PLANES)]
    before = relay(lower_ref, lower(1, source[0], source[1]), offset_ref, state_ref, True)
    lowered_0 = lower(0, before, source[0])
    lowered_1 = lower(1, lowered_0, source[1])
    coupled, first = upper_sweep([lowered_0, lowered_1])

    faces = faces_of(first)
    joint_0 = plus(faces[0], coupled[0])
    joint_1 = plus(faces[1], coupled[1])
    before = relay(lower_ref, lower(1, joint_0, joint_1), offset_ref, state_ref, True)
    along = lower(0, before)
    lowered_1 = lower(1, plus(joint_0, along), faces[1])
    coupled, second = upper_sweep([plus(faces[0], along), lowered_1])

    faces = faces_of(second)
    row = lax.broadcasted_iota(jnp.int32, (CHUNKS, LANES), 0)
    lane = lax.broadcasted_iota(jnp.int32, (CHUNKS, LANES), 1)
    previous = []
    for x in coupled[1]:
        x = pltpu.roll(x, 1, 0)
        x = jnp.where(row == 0, jnp.where(lane < 32, 0.0, pltpu.roll(x, 32, 1)), x)
        previous.append(x)
    results = [
        plus(first[0], second[0]),
        plus(first[1], second[1]),
        lower(0, previous, faces[0]),
        lower(1, coupled[0], faces[1]),
    ]
    for g in range(4):
        for a in range(VARS):
            out_ref[pl.ds(8 * g + a, CHUNKS, stride=32), :] = results[g][a]
            values_ref[pl.ds(5 * g + a, CHUNKS, stride=20), :] = results[g][a]
    turned = values_ref[0:LANES, :].T
    others = values_ref[LANES:2 * LANES, :].T
    lane_group = lax.broadcasted_iota(jnp.int32, (CROSS, LANES), 1) >> 5
    fifth = others[0:CROSS]
    for group in range(GROUPS):
        rows = slice(32 * group, 32 * group + CROSS)
        send_ref[pl.ds(group, CROSS, stride=5), :] = turned[rows]
        if group:
            fifth = jnp.where(lane_group == group, pltpu.roll(others[rows], 32 * group, 1), fifth)
    send_ref[pl.ds(4, CROSS, stride=5), :] = fifth


def regroup(parts):
    lane = lax.broadcasted_iota(jnp.int32, parts[0].shape, 1)
    first_half = lane < 64
    even = (lane & 32) == 0
    half = [None] * 4
    for i in range(2):
        x, y = parts[i], parts[i + 2]
        half[i] = jnp.where(first_half, x, pltpu.roll(y, 64, 1))
        half[i + 2] = jnp.where(first_half, pltpu.roll(x, 64, 1), y)
    out = [None] * 4
    for i in (0, 2):
        x, y = half[i], half[i + 1]
        out[i] = jnp.where(even, x, pltpu.roll(y, 32, 1))
        out[i + 1] = jnp.where(even, pltpu.roll(x, 96, 1), y)
    return out


def join_kernel(in_ref, face_ref, out_ref, values_ref):
    lane = lax.broadcasted_iota(jnp.int32, (8, LANES), 1)
    returned = (lane & 16) == 0
    blank = jnp.zeros((16, LANES), F32)
    fifth = face_ref[pl.ds(4, CROSS, stride=5), :]
    parts = []
    others = []
    for group in range(GROUPS):
        parts += [face_ref[pl.ds(group, CROSS, stride=5), :], blank]
        others += [pltpu.roll(fifth, (LANES - 32 * group) % LANES, 1) if group else fifth, blank]
    values_ref[0:LANES, :] = jnp.concatenate(parts, axis=0).T
    values_ref[LANES:2 * LANES, :] = jnp.concatenate(others, axis=0).T
    for k in range(CHUNKS):
        tiles = []
        for g in range(4):
            at = 5 * (4 * k + g)
            tiles.append(jnp.where(returned, values_ref[at:at + 8, :], in_ref[32 * k + 8 * g:32 * k + 8 * g + 8, :]))
        for group, tile in enumerate(regroup(tiles)):
            out_ref[CHUNKS * group + k] = tile


def unpack_kernel(matrix_ref, diagonal_ref, in_ref, solution_ref, residual_ref, rows_ref):
    for column in range(8):
        tiles = regroup([in_ref[4 * column + e] for e in range(4)])
        for g, tile in enumerate(tiles):
            rows_ref[8 * g:8 * g + 8, LANES * column:LANES * (column + 1)] = tile
    for link in range(LINKS):
        window = slice(link * WINDOW, (link + 1) * WINDOW)
        cells = times(rows_ref[:, window], matrix_ref[link])
        for p in range(PLANES):
            residual = cells[16 + 8 * p:16 + 8 * p + VARS] * diagonal_ref[p:p + 1, window]
            for a in range(VARS):
                solution_ref[a, p:p + 1, window] = cells[8 * p + a:8 * p + a + 1]
                residual_ref[a, p:p + 1, window] = residual[a:a + 1]


def shape(*dims):
    return jax.ShapeDtypeStruct(dims, F32)


def local(
    rhs,
    diagonal,
    lower_transfer,
    upper_transfer,
    face_owner,
    face_start,
    face_count,
    face_flip,
    block_cells,
):
    owner, start, count, flip = face_owner.T, face_start.T, face_count.T, face_flip.T
    transfer = pltpu.VMEM((VARS, VARS, PLANES, CELLS), F32)
    planes = pltpu.VMEM((PLANES, CELLS), F32)
    in_hbm = functools.partial(pltpu.with_memory_space_constraint, memory_space=pltpu.HBM)
    packed, matrix = pl.pallas_call(
        pack_kernel,
        out_shape=[shape(CELLS, LANES), jax.ShapeDtypeStruct((LINKS, WINDOW, WINDOW), BF16)],
        in_specs=[HBM] * 9,
        out_specs=[VMEM] * 2,
        scratch_shapes=[TABLE] * 4
        + [
            pltpu.SMEM((CROSS,), jnp.int32), pltpu.VMEM((VARS, PLANES, CELLS), F32), planes,
            transfer, transfer, pltpu.VMEM((LANES, CELLS), F32), pltpu.SemaphoreType.DMA((9,)),
        ],
        compiler_params=PARAMS,
        name="pack_cells",
    )(
        *[
            in_hbm(x)
            for x in (
                owner, start, count, flip,
                block_cells,
                rhs.transpose(1, 0, 2),
                diagonal,
                lower_transfer.transpose(1, 2, 0, 3),
                upper_transfer.transpose(1, 2, 0, 3),
            )
        ]
    )
    arrived = lax.all_to_all(packed.reshape(STREAM, 32, LANES), "stream", 0, 0, tiled=True)
    arrived = arrived.reshape(CELLS, LANES)
    faces = pl.pallas_call(
        faces_kernel,
        out_shape=shape(CROSS * KEPT, LANES),
        in_specs=[VMEM],
        out_specs=VMEM,
        compiler_params=PARAMS,
        name="take_faces",
    )(arrived)
    faces = lax.all_to_all(faces.reshape(CROSS * KEPT // 4, 4, LANES), "cross", 0, 0, tiled=True)

    composed = pltpu.VMEM((VARS * VARS, CHUNKS, LANES), F32)
    results, faces = pl.pallas_call(
        solve_kernel,
        out_shape=[shape(CHUNKS * 32, LANES), shape(5 * CROSS, LANES)],
        in_specs=[HBM, HBM, VMEM, VMEM],
        out_specs=[VMEM, VMEM],
        scratch_shapes=[TABLE] * 2
        + [
            pltpu.VMEM((CHUNKS * LANES, LANES), F32), composed, composed,
            pltpu.VMEM((VARS, CHUNKS, LANES), F32),
            pltpu.VMEM((GROUPS, VARS, CHUNKS, LANES), F32),
            pltpu.VMEM((2 * LANES, LANES), F32),
            pltpu.SemaphoreType.DMA((2,)),
        ],
        compiler_params=PARAMS,
        name="solve_cells",
    )(owner, count, arrived, faces.reshape(CROSS * KEPT, LANES))
    faces = lax.all_to_all(faces.reshape(5 * CROSS, 1, LANES), "cross", 0, 0, tiled=True)
    results = pl.pallas_call(
        join_kernel,
        out_shape=shape(STREAM, 8, LANES),
        in_specs=[VMEM, VMEM],
        out_specs=VMEM,
        scratch_shapes=[pltpu.VMEM((2 * LANES, LANES), F32)],
        compiler_params=PARAMS,
        name="join_faces",
    )(results, faces.reshape(5 * CROSS, LANES))
    returned = lax.all_to_all(results, "stream", 0, 0, tiled=True)
    outs = pl.pallas_call(
        unpack_kernel,
        out_shape=[shape(VARS, PLANES, CELLS)] * 2,
        in_specs=[VMEM] * 3,
        out_specs=[VMEM] * 2,
        scratch_shapes=[pltpu.VMEM((32, CELLS), F32)],
        compiler_params=PARAMS,
        name="unpack_cells",
    )(matrix, diagonal, returned)
    return tuple(x.transpose(1, 0, 2) for x in outs)


def solution(mesh):
    return jax.shard_map(
        local,
        mesh=mesh,
        in_specs=(
            P("stream", None, "cross"),
            P("stream", "cross"),
            P("stream", None, None, "cross"),
            P("stream", None, None, "cross"),
            P(),
            P(),
            P(),
            P(),
            P(),
        ),
        out_specs=(P("stream", None, "cross"), P("stream", None, "cross")),
        check_vma=False,
    )
```

```python
import functools

import jax
import jax.numpy as jnp
from jax import lax
from jax.experimental import pallas as pl
from jax.experimental.pallas import tpu as pltpu
from jax.sharding import PartitionSpec as P

VARS = 5
CELLS = 1024
LINKS = 4
WINDOW = CELLS // LINKS
STREAM = 32
CROSS = 16
PLANES = 2
CHUNKS = 8
GROUPS = 4
LANES = 128
FACE_WEIGHT = 0.25

LOWER = 0
UPPER = 25
SOURCE = 50
ROWS = 110
KEPT = 28
PIECES = 7

F32 = jnp.float32
BF16 = jnp.bfloat16
HBM = pl.BlockSpec(memory_space=pltpu.HBM)
SMEM = pl.BlockSpec(memory_space=pltpu.SMEM)
VMEM = pl.BlockSpec(memory_space=pltpu.VMEM)
PARAMS = pltpu.CompilerParams(vmem_limit_bytes=24 * 1024 * 1024)
TABLE = pltpu.SMEM((LINKS, CROSS), jnp.int32)


def thirds(x):
    high = x.astype(BF16)
    rest = x - high.astype(F32)
    middle = rest.astype(BF16)
    low = (rest - middle.astype(F32)).astype(BF16)
    return jnp.concatenate([high, middle, low], axis=0)


def times(x, matrix):
    n = x.shape[0]
    parts = jnp.dot(thirds(x), matrix, preferred_element_type=F32)
    return (parts[2 * n:] + parts[n:2 * n]) + parts[:n]


def copy_in(pairs, sems):
    copies = [pltpu.make_async_copy(src, dst, sems.at[i]) for i, (src, dst) in enumerate(pairs)]
    for copy in copies:
        copy.start()
    return copies


def slots_of(own, link, owner_ref, start_ref, count_ref, flip_ref):
    owner = owner_ref[link, own]
    count = count_ref[link, own]
    turned = jnp.logical_and(flip_ref[link, own] == 1, own > owner)
    bound = jnp.where(turned, count, 0)
    offset = start_ref[link, own] - link * WINDOW
    cell = lax.broadcasted_iota(jnp.int32, (1, WINDOW), 1)
    place = (cell - offset) & (WINDOW - 1)
    place = jnp.where(place < bound, count - 1 - place, place)
    rest = place & 127
    return ((rest >> 4) << 5) + ((place >> 7) << 4) + (rest & 15)


def onehot(row):
    rows = lax.broadcasted_iota(jnp.int32, (WINDOW, WINDOW), 0)
    return jnp.where(rows == row, 1.0, 0.0).astype(BF16)


def pack_kernel(
    owner_in, start_in, count_in, flip_in, live_in, rhs_in, diagonal_in, lower_in, upper_in,
    out_ref, matrix_ref,
    owner_ref, start_ref, count_ref, flip_ref, live_ref, rhs_ref, diagonal_ref, lower_ref, upper_ref,
    rows_ref, sems,
):
    copies = copy_in(
        [
            (owner_in, owner_ref), (start_in, start_ref), (count_in, count_ref),
            (flip_in, flip_ref), (live_in, live_ref), (rhs_in, rhs_ref),
            (diagonal_in, diagonal_ref), (lower_in, lower_ref), (upper_in, upper_ref),
        ],
        sems,
    )
    own = lax.axis_index("cross")
    rows_ref[pl.ds(ROWS, LANES - ROWS), :] = jnp.zeros((LANES - ROWS, CELLS), F32)
    for copy in copies[:5]:
        copy.wait()
    for link in range(LINKS):
        matrix_ref[link] = onehot(slots_of(own, link, owner_ref, start_ref, count_ref, flip_ref))
    for copy in copies[5:]:
        copy.wait()
    cell = lax.broadcasted_iota(jnp.int32, (PLANES, CELLS), 1)
    live = cell < live_ref[own]
    for a in range(VARS):
        for b in range(VARS):
            at = VARS * a + b
            rows_ref[pl.ds(2 * (LOWER + at), 2), :] = lower_ref[a, b]
            rows_ref[pl.ds(2 * (UPPER + at), 2), :] = upper_ref[a, b]
        source = jnp.where(live, rhs_ref[a], 0.0) / diagonal_ref[...]
        rows_ref[pl.ds(2 * (SOURCE + a), 2), :] = source
    for link in range(LINKS):
        parts = lax.dot_general(
            matrix_ref[link],
            thirds(rows_ref[:, link * WINDOW:(link + 1) * WINDOW]),
            (((1,), (1,)), ((), ())),
            preferred_element_type=F32,
        )
        out_ref[link * WINDOW:(link + 1) * WINDOW, :] = (
            parts[:, 2 * LANES:] + parts[:, LANES:2 * LANES]
        ) + parts[:, :LANES]


def total(rows, first=None):
    if first is None:
        return [(t[0] + t[1]) + (t[2] + t[3]) + t[4] for t in rows]
    return [((x + t[0]) + (t[1] + t[2])) + (t[3] + t[4]) for x, t in zip(first, rows)]


def entry(system_ref, at, p):
    row = 8 * (2 * at + p)
    return system_ref[row:row + 8, :]


def apply(system_ref, at, p, x, first=None):
    return total(
        [[entry(system_ref, at + VARS * a + b, p) * x[b] for b in range(VARS)] for a in range(VARS)],
        first,
    )


def compose(system_ref, at, later, earlier, out_ref):
    for c in range(VARS):
        column = [entry(system_ref, at + VARS * b + c, earlier) for b in range(VARS)]
        for a, x in enumerate(apply(system_ref, at, later, column)):
            out_ref[VARS * a + c] = x


def relay(matrix_ref, pair_ref, offset, offset_ref, state_ref, up):
    back = 1 if up else CHUNKS - 1
    matrix = [[matrix_ref[VARS * a + b] for b in range(VARS)] for a in range(VARS)]

    def passed(x, first=None):
        return total([[matrix[a][b] * x[b] for b in range(VARS)] for a in range(VARS)], first)

    for a, x in enumerate(passed([pltpu.roll(x, back, 0) for x in offset], offset)):
        offset_ref[a] = x
    state = [jnp.zeros((1, LANES), F32) for _ in range(VARS)]
    groups = range(GROUPS) if up else range(GROUPS - 1, -1, -1)
    chunks = range(0, CHUNKS, 2) if up else range(CHUNKS - 1, -1, -2)
    for group in groups:
        if group != groups[0]:
            state = [pltpu.roll(x, 32 if up else 96, 1) for x in state]
        for k in chunks:
            row = slice(k, k + 1)
            for a in range(VARS):
                state_ref[group, a, row, :] = state[a]
            row = slice(k + 1, k + 2) if up else slice(k - 1, k)
            state = total(
                [
                    [pair_ref[VARS * a + b, row, :] * state[b] for b in range(VARS)]
                    for a in range(VARS)
                ],
                [offset_ref[a, row, :] for a in range(VARS)],
            )
    lane = lax.broadcasted_iota(jnp.int32, (CHUNKS, LANES), 1) >> 5
    out = []
    for a in range(VARS):
        x = state_ref[GROUPS - 1, a]
        for group in range(GROUPS - 1):
            x = jnp.where(lane == group, state_ref[group, a], x)
        out.append(x)
    row = lax.broadcasted_iota(jnp.int32, (CHUNKS, LANES), 0) & 1
    inner = [pltpu.roll(x, back, 0) for x in passed(out, offset)]
    return [jnp.where(row == (0 if up else 1), x, y) for x, y in zip(out, inner)]


def pair(matrix_ref, pair_ref, up):
    for c in range(VARS):
        column = [
            pltpu.roll(matrix_ref[VARS * b + c], 1 if up else CHUNKS - 1, 0) for b in range(VARS)
        ]
        for a in range(VARS):
            t = [matrix_ref[VARS * a + b] * column[b] for b in range(VARS)]
            pair_ref[VARS * a + c] = total([t])[0]


def plus(x, y):
    return [a + b for a, b in zip(x, y)]


def face_matrix(owner_ref, count_ref):
    position = lax.axis_index("stream")
    link = position >> 3
    slot = ((position & 7) << 4) + lax.axis_index("cross")
    lane = lax.broadcasted_iota(jnp.int32, (1, LANES), 1)
    source = jnp.full((1, LANES), -1, jnp.int32)
    for block in range(CROSS):
        taken = jnp.where(slot < count_ref[link, block], owner_ref[link, block], -LANES)
        source = jnp.where((lane & 31) == block, (lane & 96) + taken, source)
    rows = lax.broadcasted_iota(jnp.int32, (LANES, LANES), 0)
    return jnp.where(rows == source, FACE_WEIGHT, 0.0).astype(BF16)


def faces_kernel(in_ref, out_ref):
    lane = lax.broadcasted_iota(jnp.int32, (CROSS, LANES), 1)
    for row in range(KEPT):
        piece = row % PIECES
        first = 32 * (KEPT + row // PIECES)
        spare = pltpu.roll(in_ref[first:first + CROSS, :], ROWS - 16 * piece, 1)
        own = in_ref[32 * row:32 * row + CROSS, :]
        out_ref[pl.ds(row, CROSS, stride=KEPT), :] = jnp.where(lane < ROWS, own, spare)


def face_rows(face_ref, chunk):
    if chunk < KEPT:
        return face_ref[pl.ds(chunk, CROSS, stride=KEPT), :]
    piece_of = lax.broadcasted_iota(jnp.int32, (CROSS, LANES), 1) >> 4
    out = jnp.zeros((CROSS, LANES), F32)
    for piece in range(PIECES):
        row = PIECES * (chunk - KEPT) + piece
        moved = pltpu.roll(
            face_ref[pl.ds(row, CROSS, stride=KEPT), :], LANES - ROWS + 16 * piece, 1
        )
        out = jnp.where(piece_of == piece, moved, out)
    return out


def solve_kernel(
    owner_in, count_in, in_ref, face_ref, out_ref, send_ref,
    owner_ref, count_ref, system_ref, lower_ref, upper_ref, lower_pair, upper_pair, offset_ref, state_ref, values_ref, sems,
):
    copies = copy_in([(owner_in, owner_ref), (count_in, count_ref)], sems)
    values_ref[160:, :] = jnp.zeros((96, LANES), F32)
    for k in range(CHUNKS):
        parts = []
        for group in range(GROUPS):
            chunk = CHUNKS * group + k
            parts += [face_rows(face_ref, chunk), in_ref[32 * chunk + 16:32 * chunk + 32, :]]
        system_ref[pl.ds(k, LANES, stride=CHUNKS), :] = jnp.concatenate(parts, axis=0).T
    for copy in copies:
        copy.wait()
    matrix = face_matrix(owner_ref, count_ref)
    lower = functools.partial(apply, system_ref, LOWER)
    upper = functools.partial(apply, system_ref, UPPER)
    compose(system_ref, LOWER, 1, 0, lower_ref)
    compose(system_ref, UPPER, 0, 1, upper_ref)
    pair(lower_ref, lower_pair, True)
    pair(upper_ref, upper_pair, False)

    def upper_sweep(lowered):
        offset = upper(0, lowered[1], lowered[0])
        after = relay(upper_ref, upper_pair, offset, offset_ref, state_ref, False)
        coupled_1 = upper(1, after)
        delta_1 = plus(lowered[1], coupled_1)
        coupled_0 = upper(0, delta_1)
        return [coupled_0, coupled_1], [plus(lowered[0], coupled_0), delta_1]

    def faces_of(delta):
        parts = times(jnp.concatenate(delta[0] + delta[1], axis=0), matrix)
        rows = [parts[CHUNKS * i:CHUNKS * (i + 1)] for i in range(2 * VARS)]
        return [rows[:VARS], rows[VARS:]]

    source = [[entry(system_ref, SOURCE + a, p) for a in range(VARS)] for p in range(PLANES)]
    before = relay(lower_ref, lower_pair, lower(1, source[0], source[1]), offset_ref, state_ref, True)
    lowered_0 = lower(0, before, source[0])
    lowered_1 = lower(1, lowered_0, source[1])
    coupled, first = upper_sweep([lowered_0, lowered_1])

    faces = faces_of(first)
    joint_0 = plus(faces[0], coupled[0])
    joint_1 = plus(faces[1], coupled[1])
    before = relay(lower_ref, lower_pair, lower(1, joint_0, joint_1), offset_ref, state_ref, True)
    along = lower(0, before)
    lowered_1 = lower(1, plus(joint_0, along), faces[1])
    coupled, second = upper_sweep([plus(faces[0], along), lowered_1])

    faces = faces_of(second)
    row = lax.broadcasted_iota(jnp.int32, (CHUNKS, LANES), 0)
    lane = lax.broadcasted_iota(jnp.int32, (CHUNKS, LANES), 1)
    previous = []
    for x in coupled[1]:
        x = pltpu.roll(x, 1, 0)
        x = jnp.where(row == 0, jnp.where(lane < 32, 0.0, pltpu.roll(x, 32, 1)), x)
        previous.append(x)
    results = [
        plus(first[0], second[0]),
        plus(first[1], second[1]),
        lower(0, previous, faces[0]),
        lower(1, coupled[0], faces[1]),
    ]
    for g in range(4):
        for a in range(VARS):
            out_ref[pl.ds(8 * g + a, CHUNKS, stride=32), :] = results[g][a]
            values_ref[pl.ds(5 * g + a, CHUNKS, stride=20), :] = results[g][a]
    turned = values_ref[0:LANES, :].T
    others = values_ref[LANES:2 * LANES, :].T
    lane_group = lax.broadcasted_iota(jnp.int32, (CROSS, LANES), 1) >> 5
    fifth = others[0:CROSS]
    for group in range(GROUPS):
        rows = slice(32 * group, 32 * group + CROSS)
        send_ref[pl.ds(group, CROSS, stride=5), :] = turned[rows]
        if group:
            fifth = jnp.where(lane_group == group, pltpu.roll(others[rows], 32 * group, 1), fifth)
    send_ref[pl.ds(4, CROSS, stride=5), :] = fifth


def regroup(parts):
    lane = lax.broadcasted_iota(jnp.int32, parts[0].shape, 1)
    first_half = lane < 64
    even = (lane & 32) == 0
    half = [None] * 4
    for i in range(2):
        x, y = parts[i], parts[i + 2]
        half[i] = jnp.where(first_half, x, pltpu.roll(y, 64, 1))
        half[i + 2] = jnp.where(first_half, pltpu.roll(x, 64, 1), y)
    out = [None] * 4
    for i in (0, 2):
        x, y = half[i], half[i + 1]
        out[i] = jnp.where(even, x, pltpu.roll(y, 32, 1))
        out[i + 1] = jnp.where(even, pltpu.roll(x, 96, 1), y)
    return out


def join_kernel(in_ref, face_ref, out_ref, values_ref):
    lane = lax.broadcasted_iota(jnp.int32, (8, LANES), 1)
    returned = (lane & 16) == 0
    blank = jnp.zeros((16, LANES), F32)
    fifth = face_ref[pl.ds(4, CROSS, stride=5), :]
    parts = []
    others = []
    for group in range(GROUPS):
        parts += [face_ref[pl.ds(group, CROSS, stride=5), :], blank]
        others += [pltpu.roll(fifth, (LANES - 32 * group) % LANES, 1) if group else fifth, blank]
    values_ref[0:LANES, :] = jnp.concatenate(parts, axis=0).T
    values_ref[LANES:2 * LANES, :] = jnp.concatenate(others, axis=0).T
    for k in range(CHUNKS):
        tiles = []
        for g in range(4):
            at = 5 * (4 * k + g)
            tiles.append(jnp.where(returned, values_ref[at:at + 8, :], in_ref[32 * k + 8 * g:32 * k + 8 * g + 8, :]))
        for group, tile in enumerate(regroup(tiles)):
            out_ref[CHUNKS * group + k] = tile


def unpack_kernel(matrix_ref, diagonal_ref, in_ref, solution_ref, residual_ref, rows_ref):
    for column in range(8):
        tiles = regroup([in_ref[4 * column + e] for e in range(4)])
        for g, tile in enumerate(tiles):
            rows_ref[8 * g:8 * g + 8, LANES * column:LANES * (column + 1)] = tile
    for link in range(LINKS):
        window = slice(link * WINDOW, (link + 1) * WINDOW)
        cells = times(rows_ref[:, window], matrix_ref[link])
        for p in range(PLANES):
            residual = cells[16 + 8 * p:16 + 8 * p + VARS] * diagonal_ref[p:p + 1, window]
            for a in range(VARS):
                solution_ref[a, p:p + 1, window] = cells[8 * p + a:8 * p + a + 1]
                residual_ref[a, p:p + 1, window] = residual[a:a + 1]


def shape(*dims):
    return jax.ShapeDtypeStruct(dims, F32)


def local(
    rhs,
    diagonal,
    lower_transfer,
    upper_transfer,
    face_owner,
    face_start,
    face_count,
    face_flip,
    block_cells,
):
    owner, start, count, flip = face_owner.T, face_start.T, face_count.T, face_flip.T
    transfer = pltpu.VMEM((VARS, VARS, PLANES, CELLS), F32)
    planes = pltpu.VMEM((PLANES, CELLS), F32)
    in_hbm = functools.partial(pltpu.with_memory_space_constraint, memory_space=pltpu.HBM)
    packed, matrix = pl.pallas_call(
        pack_kernel,
        out_shape=[shape(CELLS, LANES), jax.ShapeDtypeStruct((LINKS, WINDOW, WINDOW), BF16)],
        in_specs=[HBM] * 9,
        out_specs=[VMEM] * 2,
        scratch_shapes=[TABLE] * 4
        + [
            pltpu.SMEM((CROSS,), jnp.int32), pltpu.VMEM((VARS, PLANES, CELLS), F32), planes,
            transfer, transfer, pltpu.VMEM((LANES, CELLS), F32), pltpu.SemaphoreType.DMA((9,)),
        ],
        compiler_params=PARAMS,
        name="pack_cells",
    )(
        *[
            in_hbm(x)
            for x in (
                owner, start, count, flip,
                block_cells,
                rhs.transpose(1, 0, 2),
                diagonal,
                lower_transfer.transpose(1, 2, 0, 3),
                upper_transfer.transpose(1, 2, 0, 3),
            )
        ]
    )
    arrived = lax.all_to_all(packed.reshape(STREAM, 32, LANES), "stream", 0, 0, tiled=True)
    arrived = arrived.reshape(CELLS, LANES)
    faces = pl.pallas_call(
        faces_kernel,
        out_shape=shape(CROSS * KEPT, LANES),
        in_specs=[VMEM],
        out_specs=VMEM,
        compiler_params=PARAMS,
        name="take_faces",
    )(arrived)
    faces = lax.all_to_all(faces.reshape(CROSS * KEPT // 4, 4, LANES), "cross", 0, 0, tiled=True)

    composed = pltpu.VMEM((VARS * VARS, CHUNKS, LANES), F32)
    results, faces = pl.pallas_call(
        solve_kernel,
        out_shape=[shape(CHUNKS * 32, LANES), shape(5 * CROSS, LANES)],
        in_specs=[HBM, HBM, VMEM, VMEM],
        out_specs=[VMEM, VMEM],
        scratch_shapes=[TABLE] * 2
        + [
            pltpu.VMEM((CHUNKS * LANES, LANES), F32), composed, composed, composed, composed,
            pltpu.VMEM((VARS, CHUNKS, LANES), F32),
            pltpu.VMEM((GROUPS, VARS, CHUNKS, LANES), F32),
            pltpu.VMEM((2 * LANES, LANES), F32),
            pltpu.SemaphoreType.DMA((2,)),
        ],
        compiler_params=PARAMS,
        name="solve_cells",
    )(owner, count, arrived, faces.reshape(CROSS * KEPT, LANES))
    faces = lax.all_to_all(faces.reshape(5 * CROSS, 1, LANES), "cross", 0, 0, tiled=True)
    results = pl.pallas_call(
        join_kernel,
        out_shape=shape(STREAM, 8, LANES),
        in_specs=[VMEM, VMEM],
        out_specs=VMEM,
        scratch_shapes=[pltpu.VMEM((2 * LANES, LANES), F32)],
        compiler_params=PARAMS,
        name="join_faces",
    )(results, faces.reshape(5 * CROSS, LANES))
    returned = lax.all_to_all(results, "stream", 0, 0, tiled=True)
    outs = pl.pallas_call(
        unpack_kernel,
        out_shape=[shape(VARS, PLANES, CELLS)] * 2,
        in_specs=[VMEM] * 3,
        out_specs=[VMEM] * 2,
        scratch_shapes=[pltpu.VMEM((32, CELLS), F32)],
        compiler_params=PARAMS,
        name="unpack_cells",
    )(matrix, diagonal, returned)
    return tuple(x.transpose(1, 0, 2) for x in outs)


def solution(mesh):
    return jax.shard_map(
        local,
        mesh=mesh,
        in_specs=(
            P("stream", None, "cross"),
            P("stream", "cross"),
            P("stream", None, None, "cross"),
            P("stream", None, None, "cross"),
            P(),
            P(),
            P(),
            P(),
            P(),
        ),
        out_specs=(P("stream", None, "cross"), P("stream", None, "cross")),
        check_vma=False,
    )
```
